32 devices in a mesh: mx: 8 (over y, x, core), my: 4 (over z).
Axes of the slice: x: 2, y: 2, z: 4, core: 2. Of those that a mesh axis runs over, the one named last changes fastest.
Arguments:
- density: float32 [128, 64, 128], P('mx', 'my'), may hold values from 0.5 to 2
- momentum: float32 [3, 128, 64, 128], P(None, 'mx', 'my'), may hold values from -1.8 to 1.8
- energy: float32 [128, 64, 128], P('mx', 'my'), may hold values from -6 to 6
- entropy: float32 [128, 64, 128], P('mx', 'my'), may hold values from 0.5 to 16, as said below
- tracers: float32 [9, 128, 64, 128], P(None, 'mx', 'my'), may hold values from -6 to 6
- leaf_flags: int32 [16, 8, 16], P('mx', 'my'), may hold values 0 or 1
Outputs:
- section: float32 [15, 128, 64, 128], P(None, 'mx', 'my')
- gravity_accel: float32 [3, 128, 64, 128], P(None, 'mx', 'my')
The draws below stay inside these ranges and needn't reach their ends.
Inputs may be any that keep to these rules, and one draw needn't show every extreme that they name: `entropy`: positive.
All inputs are finite; a program needn't handle non-finite values. No bound on the sum of `leaf_flags` on one device may be relied on, other than what follows from the above.
Results may differ from the reference program's by a relative error of at most 0.0003.
Values sent between devices are 32-bit elements; how exact they have to be, the bound alone decides.
A program may use at most 128 MiB of HBM per device.

```python
import math
import jax
import jax.numpy as jnp
import numpy as np
from jax import lax

SUB = 8
NF = 15
LEVELS = 3
GZ = 16
SX = 16
SY = 8
NX = 128
NY = 64
NZ = 128


def draw_entropy(key, part):
    base_value = jnp.exp(jax.random.uniform(key, (NX, NY, NZ), jnp.float32, math.log(0.5), math.log(2.0)))
    across_x = jnp.arange(NX, dtype=jnp.float32)[:, None, None] / NX
    across_y = jnp.arange(NY, dtype=jnp.float32)[None, :, None] / NY
    return base_value * jnp.exp2(2.0 * across_x + across_y)


def set_ends(drawn, key, low, top_value):
    index_at = [jax.random.randint(jax.random.fold_in(key, axis), (), 0, length) for axis, length in enumerate(drawn.shape)]
    widest = drawn.shape.index(max(drawn.shape))
    next_to = index_at[:widest] + [(index_at[widest] + 1) % drawn.shape[widest]] + index_at[widest + 1:]
    return drawn.at[tuple(index_at)].set(low).at[tuple(next_to)].set(top_value)


def block_scale(rng, dims, cuts, least, top_value):
    def one(position, shards_of):
        steps = jax.random.uniform(jax.random.fold_in(jax.random.fold_in(rng, 6), position), (shards_of,), jnp.float32, least / len(cuts), top_value / len(cuts))
        return jnp.repeat(jnp.exp(steps), dims[position] // shards_of).reshape((-1,) + (1,) * (len(dims) - position - 1))

    factor_of = one(*cuts[0])
    for cut in cuts[1:]:
        factor_of = factor_of * one(*cut)
    return factor_of


def bell_draw(key, shape, deviation, limit, pieces=(), kind=jnp.bfloat16):
    array = jax.random.normal(key, shape, jnp.float32) * deviation
    if len(pieces) > 0:
        array = block_scale(key, shape, pieces, -0.22, 0.18) * array
    return jnp.clip(array, min=-limit, max=limit).astype(kind)


def setup_inputs(seed: int = 0) -> dict:
    keys = jax.random.split(jax.random.key(seed), 7)
    density = jnp.clip(jnp.exp(math.log(2.0) - 1.3862944 * jax.random.uniform(keys[0], (NX, NY, NZ), jnp.float32) ** block_scale(keys[0], (NX, NY, NZ), ((0, 8), (1, 4)), -0.2, 0.2)), 0.5, 2.0)
    momentum = bell_draw(keys[1], (3, NX, NY, NZ), 0.3, 1.8, ((1, 8), (2, 4)), jnp.float32)
    energy = bell_draw(keys[2], (NX, NY, NZ), 1.0, 6.0, ((0, 8), (1, 4)), jnp.float32)
    entropy = draw_entropy(jax.random.fold_in(keys[6], 71), 0)
    tracers = bell_draw(keys[4], (NF - 6, NX, NY, NZ), 1.0, 6.0, ((1, 8), (2, 4)), jnp.float32)
    leaf_flags = set_ends((jax.random.randint(keys[5], (SX, SY, GZ), 0, 4) < 3).astype(jnp.int32), jax.random.fold_in(keys[5], 1), 0, 1)
    return dict(density=density, momentum=momentum, energy=energy, entropy=entropy, tracers=tracers, leaf_flags=leaf_flags)


gamma_gas = 5.0 / 3.0
courant = 0.3
gravity = 0.02
highest = lax.Precision.HIGHEST
multi_index = [(power_x, power_y, degree_sum - power_x - power_y) for degree_sum in range(4) for power_x in range(degree_sum, -1, -1) for power_y in range(degree_sum - power_x, -1, -1)]

def factorial_of(exponent):
    return math.factorial(exponent[0]) * math.factorial(exponent[1]) * math.factorial(exponent[2])

def inverse_derivative(exponent, vectors):
    axes_list = [0] * exponent[0] + [1] * exponent[1] + [2] * exponent[2]
    radius = np.sqrt(np.sum(vectors * vectors, axis=1))
    radius_safe = np.where(radius > 0.0, radius, 1.0)
    degree = len(axes_list)
    if degree == 0:
        result = 1.0 / radius_safe
    elif degree == 1:
        result = -vectors[:, axes_list[0]] / radius_safe ** 3
    elif degree == 2:
        index_one, index_two = axes_list
        result = 3.0 * vectors[:, index_one] * vectors[:, index_two] / radius_safe ** 5 - float(index_one == index_two) / radius_safe ** 3
    else:
        index_one, index_two, index_three = axes_list
        crossed = float(index_one == index_two) * vectors[:, index_three] + float(index_one == index_three) * vectors[:, index_two] + float(index_two == index_three) * vectors[:, index_one]
        result = -15.0 * vectors[:, index_one] * vectors[:, index_two] * vectors[:, index_three] / radius_safe ** 7 + 3.0 * crossed / radius_safe ** 5
    return np.where(radius > 0.0, result, 0.0)

def offset_grid(reach_x, reach_y, reach_z):
    return [(shift_x, shift_y, shift_z) for shift_x in range(-reach_x, reach_x + 1) for shift_y in range(-reach_y, reach_y + 1) for shift_z in range(-reach_z, reach_z + 1)]

def translation_kernel(spacing, offsets):
    vectors = np.asarray(offsets) * (-1.0 * spacing)
    entries = np.zeros((len(offsets), len(multi_index), len(multi_index)))
    for row_index, target_power in enumerate(multi_index):
        for column_index, source_power in enumerate(multi_index):
            if sum(target_power) + sum(source_power) <= 3:
                joined = (target_power[0] + source_power[0], target_power[1] + source_power[1], target_power[2] + source_power[2])
                entries[:, row_index, column_index] = -gravity * (-1.0) ** sum(source_power) / factorial_of(source_power) * inverse_derivative(joined, vectors)
    return jnp.asarray(entries, dtype=jnp.float32)

def upward_matrices(spacing):
    entries = np.zeros((2, 2, 2, len(multi_index), len(multi_index)))
    for octant in range(8):
        octant_bits = (octant >> 2 & 1, octant >> 1 & 1, octant & 1)
        displacement = [(octant_bits[dimension] - 0.5) * spacing for dimension in range(3)]
        for row_index, target_power in enumerate(multi_index):
            for column_index, source_power in enumerate(multi_index):
                if all((source_power[dimension] <= target_power[dimension] for dimension in range(3))):
                    entry_value = 1.0
                    for dimension in range(3):
                        entry_value *= math.comb(target_power[dimension], source_power[dimension]) * displacement[dimension] ** (target_power[dimension] - source_power[dimension])
                    entries[octant_bits[0], octant_bits[1], octant_bits[2], row_index, column_index] = entry_value
    return jnp.asarray(entries, dtype=jnp.float32)

def downward_matrices(spacing):
    entries = np.zeros((2, 2, 2, len(multi_index), len(multi_index)))
    for octant in range(8):
        octant_bits = (octant >> 2 & 1, octant >> 1 & 1, octant & 1)
        displacement = [(octant_bits[dimension] - 0.5) * spacing for dimension in range(3)]
        for row_index, target_power in enumerate(multi_index):
            for column_index, source_power in enumerate(multi_index):
                if all((source_power[dimension] >= target_power[dimension] for dimension in range(3))):
                    entry_value = 1.0
                    for dimension in range(3):
                        lifted = source_power[dimension] - target_power[dimension]
                        entry_value *= displacement[dimension] ** lifted / math.factorial(lifted)
                    entries[octant_bits[0], octant_bits[1], octant_bits[2], row_index, column_index] = entry_value
    return jnp.asarray(entries, dtype=jnp.float32)

def moment_table(cells_edge):
    centres = (np.arange(cells_edge) + 0.5) / cells_edge - 0.5
    volume = 1.0 / cells_edge ** 3
    entries = np.zeros((cells_edge, cells_edge, cells_edge, len(multi_index)))
    for column_index, exponent in enumerate(multi_index):
        entries[:, :, :, column_index] = volume * centres[:, None, None] ** exponent[0] * centres[None, :, None] ** exponent[1] * centres[None, None, :] ** exponent[2]
    return jnp.asarray(entries, dtype=jnp.float32)

def field_table(cells_edge):
    centres = (np.arange(cells_edge) + 0.5) / cells_edge - 0.5
    entries = np.zeros((cells_edge, cells_edge, cells_edge, 3, len(multi_index)))
    for column_index, exponent in enumerate(multi_index):
        for dimension in range(3):
            if exponent[dimension] > 0:
                lowered = list(exponent)
                lowered[dimension] -= 1
                entries[:, :, :, dimension, column_index] = -exponent[dimension] / factorial_of(exponent) * centres[:, None, None] ** lowered[0] * centres[None, :, None] ** lowered[1] * centres[None, None, :] ** lowered[2]
    return jnp.asarray(entries, dtype=jnp.float32)

def allowed(coords, offset, rule_name):
    touching = (jnp.abs(offset[0]) <= 1) & (jnp.abs(offset[1]) <= 1) & (jnp.abs(offset[2]) <= 1)
    accepted = (coords[0] >= 0) & (coords[1] >= 0) & (coords[2] >= 0)
    if rule_name == 'coarsest':
        return accepted & jnp.logical_not(touching)
    for dimension in range(3):
        parent_step = jnp.floor_divide(coords[dimension] + offset[dimension], 2) - jnp.floor_divide(coords[dimension], 2)
        accepted = accepted & (jnp.abs(parent_step) <= 1)
    if rule_name == 'finest':
        nonzero = (offset[0] != 0) | (offset[1] != 0) | (offset[2] != 0)
        return accepted & nonzero
    return accepted & jnp.logical_not(touching)

def coordinates(start_x, start_y, start_z, block_shape):
    along_x = start_x + jnp.arange(block_shape[0], dtype=jnp.int32)[:, None, None]
    along_y = start_y + jnp.arange(block_shape[1], dtype=jnp.int32)[None, :, None]
    along_z = start_z + jnp.arange(block_shape[2], dtype=jnp.int32)[None, None, :]
    return (along_x, along_y, along_z)

def local_from_far(extended, margins, kernels, offsets, coords, block_shape, rule_name):
    offset_table = jnp.asarray(offsets, dtype=jnp.int32)
    moments_count = extended.shape[0]
    zero_index = jnp.zeros((), jnp.int32)

    def visit(running, item):
        kernel_matrix, offset = item
        starts = (zero_index, margins[0] + offset[0], margins[1] + offset[1], margins[2] + offset[2])
        source = lax.dynamic_slice(extended, starts, (moments_count,) + tuple(block_shape))
        weight = allowed(coords, offset, rule_name).astype(jnp.float32)
        term = jnp.einsum('ga,axyz->gxyz', kernel_matrix, source, precision=highest)
        return (running + term * weight, None)
    initial = jnp.zeros((moments_count,) + tuple(block_shape), jnp.float32)
    running, _ = lax.scan(visit, initial, (kernels, offset_table))
    return running

def upward(child, matrices):
    moments_count, size_x, size_y, size_z = child.shape
    grouped = child.reshape(moments_count, size_x // 2, 2, size_y // 2, 2, size_z // 2, 2)
    return jnp.einsum('uvwga,axuyvzw->gxyz', matrices, grouped, precision=highest)

def downward(parent, matrices):
    moments_count, size_x, size_y, size_z = parent.shape
    spread = jnp.einsum('uvwgb,bxyz->gxuyvzw', matrices, parent, precision=highest)
    return spread.reshape(moments_count, 2 * size_x, 2 * size_y, 2 * size_z)

def gravity_field(density, leaf_flags):
    size_x, size_y, size_z = leaf_flags.shape
    cells_edge = density.shape[0] // size_x
    grouped = density.reshape(size_x, cells_edge, size_y, cells_edge, size_z, cells_edge)
    moments = jnp.einsum('xaybzc,abcg->gxyz', grouped, moment_table(cells_edge), precision=highest)
    moments = moments * leaf_flags.astype(jnp.float32)[None]
    levels_list = [moments]
    for level_index in range(1, LEVELS + 1):
        levels_list.append(upward(levels_list[-1], upward_matrices(2.0 ** (level_index - 1))))
    coarsest = levels_list[LEVELS]
    coarse_shape = coarsest.shape[1:]
    reach_top = (coarse_shape[0] - 1, coarse_shape[1] - 1, coarse_shape[2] - 1)
    top_offsets = offset_grid(reach_top[0], reach_top[1], reach_top[2])
    padded = jnp.pad(coarsest, ((0, 0), (reach_top[0], reach_top[0]), (reach_top[1], reach_top[1]), (reach_top[2], reach_top[2])))
    expansion = local_from_far(padded, reach_top, translation_kernel(2.0 ** LEVELS, top_offsets), top_offsets, coordinates(0, 0, 0, coarse_shape), coarse_shape, 'coarsest')
    near_offsets = offset_grid(3, 3, 3)
    for level_index in range(LEVELS - 1, -1, -1):
        current = levels_list[level_index]
        block_shape = current.shape[1:]
        padded = jnp.pad(current, ((0, 0), (3, 3), (3, 3), (3, 3)))
        rule_name = 'finest' if level_index == 0 else 'middle'
        carried = downward(expansion, downward_matrices(2.0 ** level_index))
        expansion = carried + local_from_far(padded, (3, 3, 3), translation_kernel(2.0 ** level_index, near_offsets), near_offsets, coordinates(0, 0, 0, block_shape), block_shape, rule_name)
    accel_cells = jnp.einsum('abcig,gxyz->ixaybzc', field_table(cells_edge), expansion, precision=highest)
    return accel_cells.reshape(3, density.shape[0], density.shape[1], density.shape[2])

def flux_of(states, direction):
    mass_density = states[0]
    velocity = states[1 + direction] / mass_density
    pressure = (gamma_gas - 1.0) * states[5] ** gamma_gas
    sound_speed = jnp.sqrt(gamma_gas * pressure / mass_density)
    flux_vector = states * velocity[None]
    flux_vector = flux_vector.at[1 + direction].add(pressure)
    flux_vector = flux_vector.at[4].add(pressure * velocity)
    return (flux_vector, jnp.abs(velocity) + sound_speed)

def face_flux(extended, direction):
    axis_dim = direction + 1
    faces = extended.shape[axis_dim] - 5
    outer_left, inner_left, left_cell, right_cell, inner_right, outer_right = [lax.slice_in_dim(extended, begin_index, begin_index + faces, axis=axis_dim) for begin_index in range(6)]
    interface = (37.0 * (left_cell + right_cell) - 8.0 * (inner_left + inner_right) + (outer_left + outer_right)) / 60.0
    left_state = jnp.clip(interface, jnp.minimum(jnp.minimum(inner_left, left_cell), right_cell), jnp.maximum(jnp.maximum(inner_left, left_cell), right_cell))
    right_state = jnp.clip(interface, jnp.minimum(jnp.minimum(left_cell, right_cell), inner_right), jnp.maximum(jnp.maximum(left_cell, right_cell), inner_right))
    flux_left, speed_left = flux_of(left_state, direction)
    flux_right, speed_right = flux_of(right_state, direction)
    speed_face = jnp.maximum(speed_left, speed_right)
    return 0.5 * (flux_left + flux_right) - 0.5 * speed_face[None] * (right_state - left_state)

def cell_speed(conserved):
    velocity = conserved[1:4] / conserved[0][None]
    pressure = (gamma_gas - 1.0) * conserved[5] ** gamma_gas
    sound_speed = jnp.sqrt(gamma_gas * pressure / conserved[0])
    return lax.optimization_barrier(jnp.max(jnp.abs(velocity), axis=0)) + sound_speed

def reference(density, momentum, energy, entropy, tracers, leaf_flags):
    conserved = jnp.concatenate([density[None], momentum, energy[None], entropy[None], tracers], axis=0)
    gravity_accel = gravity_field(density, leaf_flags)
    fastest = jnp.max(cell_speed(conserved))
    step_size = courant / (SUB * fastest)
    tendency = jnp.zeros_like(conserved)
    for direction in range(3):
        widths = [(0, 0), (0, 0), (0, 0), (0, 0)]
        widths[direction + 1] = (3, 3)
        extended = jnp.pad(conserved, widths, mode='edge')
        tendency = tendency - jnp.diff(face_flux(extended, direction), axis=direction + 1) * SUB
    tendency = tendency.at[1:4].add(density[None] * gravity_accel)
    tendency = tendency.at[4].add(lax.optimization_barrier(jnp.sum(momentum * gravity_accel, axis=0)))
    return (conserved + step_size * tendency, gravity_accel)
```

```python
import functools
import math

import jax
import jax.numpy as jnp
import numpy as np
from jax import lax
from jax.experimental import pallas as pl
from jax.experimental.pallas import tpu as pltpu
from jax.sharding import PartitionSpec as P

MESH = pl.DeviceIdType.MESH
SUB = 8
LEVELS = 3


gamma_gas = 5.0 / 3.0
courant = 0.3
gravity = 0.02
highest = lax.Precision.HIGHEST
multi_index = [
    (power_x, power_y, degree_sum - power_x - power_y)
    for degree_sum in range(4)
    for power_x in range(degree_sum, -1, -1)
    for power_y in range(degree_sum - power_x, -1, -1)
]


def factorial_of(exponent):
    return math.factorial(exponent[0]) * math.factorial(exponent[1]) * math.factorial(exponent[2])


def inverse_derivative(exponent, vectors):
    axes_list = [0] * exponent[0] + [1] * exponent[1] + [2] * exponent[2]
    radius = np.sqrt(np.sum(vectors * vectors, axis=1))
    radius_safe = np.where(radius > 0.0, radius, 1.0)
    degree = len(axes_list)
    if degree == 0:
        result = 1.0 / radius_safe
    elif degree == 1:
        result = -vectors[:, axes_list[0]] / radius_safe**3
    elif degree == 2:
        index_one, index_two = axes_list
        result = (
            3.0 * vectors[:, index_one] * vectors[:, index_two] / radius_safe**5
            - float(index_one == index_two) / radius_safe**3
        )
    else:
        index_one, index_two, index_three = axes_list
        crossed = (
            float(index_one == index_two) * vectors[:, index_three]
            + float(index_one == index_three) * vectors[:, index_two]
            + float(index_two == index_three) * vectors[:, index_one]
        )
        result = (
            -15.0
            * vectors[:, index_one]
            * vectors[:, index_two]
            * vectors[:, index_three]
            / radius_safe**7
            + 3.0 * crossed / radius_safe**5
        )
    return np.where(radius > 0.0, result, 0.0)


def offset_grid(reach_x, reach_y, reach_z):
    return [
        (shift_x, shift_y, shift_z)
        for shift_x in range(-reach_x, reach_x + 1)
        for shift_y in range(-reach_y, reach_y + 1)
        for shift_z in range(-reach_z, reach_z + 1)
    ]


def translation_kernel(spacing, offsets):
    vectors = np.asarray(offsets) * (-1.0 * spacing)
    entries = np.zeros((len(offsets), len(multi_index), len(multi_index)))
    for row_index, target_power in enumerate(multi_index):
        for column_index, source_power in enumerate(multi_index):
            if sum(target_power) + sum(source_power) <= 3:
                joined = (
                    target_power[0] + source_power[0],
                    target_power[1] + source_power[1],
                    target_power[2] + source_power[2],
                )
                entries[:, row_index, column_index] = (
                    -gravity
                    * (-1.0) ** sum(source_power)
                    / factorial_of(source_power)
                    * inverse_derivative(joined, vectors)
                )
    return entries.astype(np.float32)


def upward_matrices(spacing):
    entries = np.zeros((2, 2, 2, len(multi_index), len(multi_index)))
    for octant in range(8):
        octant_bits = (octant >> 2 & 1, octant >> 1 & 1, octant & 1)
        displacement = [(octant_bits[dimension] - 0.5) * spacing for dimension in range(3)]
        for row_index, target_power in enumerate(multi_index):
            for column_index, source_power in enumerate(multi_index):
                if all(
                    (source_power[dimension] <= target_power[dimension] for dimension in range(3))
                ):
                    entry_value = 1.0
                    for dimension in range(3):
                        entry_value *= math.comb(
                            target_power[dimension], source_power[dimension]
                        ) * displacement[dimension] ** (
                            target_power[dimension] - source_power[dimension]
                        )
                    entries[
                        octant_bits[0], octant_bits[1], octant_bits[2], row_index, column_index
                    ] = entry_value
    return entries.astype(np.float32)


def downward_matrices(spacing):
    entries = np.zeros((2, 2, 2, len(multi_index), len(multi_index)))
    for octant in range(8):
        octant_bits = (octant >> 2 & 1, octant >> 1 & 1, octant & 1)
        displacement = [(octant_bits[dimension] - 0.5) * spacing for dimension in range(3)]
        for row_index, target_power in enumerate(multi_index):
            for column_index, source_power in enumerate(multi_index):
                if all(
                    (source_power[dimension] >= target_power[dimension] for dimension in range(3))
                ):
                    entry_value = 1.0
                    for dimension in range(3):
                        lifted = source_power[dimension] - target_power[dimension]
                        entry_value *= displacement[dimension] ** lifted / math.factorial(lifted)
                    entries[
                        octant_bits[0], octant_bits[1], octant_bits[2], row_index, column_index
                    ] = entry_value
    return entries.astype(np.float32)


slot = 128
wide = 256
count_m = len(multi_index)
degrees = np.array([sum(exponent) for exponent in multi_index])
inner_columns = [
    (dx * 3 + dy) * 4 + bx * 2 + by
    for dx in range(3)
    for dy in range(3)
    for bx in range(2)
    for by in range(2)
    if 1 <= 2 * dx + bx <= 4 and 1 <= 2 * dy + by <= 4
]


def split_pair(table):
    table = jnp.asarray(table, jnp.float32)
    high = table.astype(jnp.bfloat16)
    return high, (table - high.astype(jnp.float32)).astype(jnp.bfloat16)


def window_tables():
    columns = [
        (2 * dx - 2 + bx, 2 * dy - 2 + by)
        for dx in range(3)
        for dy in range(3)
        for bx in range(2)
        for by in range(2)
    ]
    children = [(i >> 2 & 1, i >> 1 & 1, i & 1) for i in range(8)]
    sources = [(cx, cy, sz - 2) for cx, cy in columns for sz in range(6)]
    offsets = np.array([[[s[k] - t[k] for k in range(3)] for t in children] for s in sources])
    kernels = np.asarray(translation_kernel(1.0, offsets.reshape(-1, 3)), np.float64)
    kernels = kernels.reshape(36, 6, 8, count_m, count_m)
    touching = (np.abs(offsets).max(axis=2) <= 1).reshape(36, 6, 8, 1, 1)

    def laid(part):
        out = np.zeros((36, slot, 8, 32))
        out[:, : 6 * count_m, :, :count_m] = part.transpose(0, 1, 4, 2, 3).reshape(
            36, 6 * count_m, 8, count_m
        )
        return out.reshape(36, slot, wide)

    middle = laid(np.where(touching, 0.0, kernels))
    close = laid(np.where(touching, kernels, 0.0))[np.array(inner_columns)]
    return middle.reshape(-1, wide), close.reshape(-1, wide)


def moment_tables(cells_z):
    centres = (np.arange(SUB) + 0.5) / SUB - 0.5
    spread = np.zeros((2, 4, 2, SUB, 4, slot))
    along_z = np.zeros((cells_z, 4, slot))
    pick_up = np.zeros((4, slot, slot))
    lift = np.asarray(upward_matrices(1.0), np.float64)
    lift_two = np.asarray(upward_matrices(2.0), np.float64)
    second = np.zeros((4, slot, 2 * slot))
    for sd in range(6):
        for index, power in enumerate(multi_index):
            lane = sd * count_m + index
            for bx in range(2):
                for by in range(2):
                    spread[bx, power[0], by, :, bx * 2 + by, lane] = (
                        centres ** power[1] / SUB**3
                    )
            along_z[:, :, lane] = (np.tile(centres, cells_z // SUB) ** power[2])[:, None]
            for bx in range(2):
                for by in range(2):
                    for dz in range(2):
                        for lower in range(count_m):
                            pick_up[bx * 2 + by, (2 + dz) * count_m + lower, lane] = (
                                lift[bx, by, dz, index, lower] * 0.5 ** sum(power)
                            )
                            second[bx * 2 + by, lower, dz * slot + lane] = (
                                lift_two[bx, by, dz, index, lower]
                                * 2.0 ** degrees[lower]
                                * 0.25 ** sum(power)
                            )
    parents = cells_z // SUB // 2
    rows = np.arange(8)
    cell_rows = np.zeros((6, 8, cells_z))
    one_rows = np.zeros((6, 8, 8))
    two_rows = np.zeros((2, 6, 8, 8))
    for s in range(3):
        for dz in range(2):
            sd = s * 2 + dz
            for row in rows:
                cell_rows[sd, row] = np.arange(cells_z) // SUB == 2 * (row + s - 1) + dz
                if row < parents // 2:
                    one_rows[sd, row] = rows == 2 * (row + s - 1) + dz
                if 4 <= row < 4 + parents // 4:
                    second_z = 2 * (row - 4 + s - 1) + dz
                    if 0 <= second_z < parents // 2:
                        for dz_one in range(2):
                            two_rows[dz_one, sd, row] = rows == 2 * second_z + dz_one
    return (
        spread.reshape(128, 4 * slot),
        along_z.reshape(cells_z, 4 * slot),
        cell_rows.reshape(48, cells_z),
        pick_up.reshape(4 * slot, slot),
        one_rows.reshape(48, 8),
        second,
        two_rows.reshape(96, 8),
        (np.arange(cells_z)[None, :] // SUB == np.arange(cells_z // SUB)[:, None]).astype(float),
    )


def down_tables(cells_z):
    def stacked(spacing):
        down = np.asarray(downward_matrices(spacing), np.float64)
        out = np.zeros((2, 2, 2, 32, 2, 32))
        for bz in range(2):
            for child in range(2):
                out[:, :, bz, :count_m, child, :count_m] = down[:, :, child].transpose(0, 1, 3, 2)
        return out

    scale = np.zeros((16, 8, 32))
    scale[:8, :, :count_m] = 1.0
    scale[8:12, :, :count_m] = 0.5 ** (degrees + 1)
    scale[12:14, :, :count_m] = 0.25 ** (degrees + 1)
    near = stacked(1.0)
    near = near.transpose(2, 3, 0, 1, 4, 5).reshape(64, wide)
    rows = np.arange(8)
    take_one = (np.arange(16)[None, :] == 8 + rows[:, None]) & (rows[:, None] < 4)
    take_two = (np.arange(16)[None, :] == 12 + rows[:, None] // 2) & (rows[:, None] < 4)
    take_zero = np.arange(8)[None, :] == rows[:, None] // 2
    centres = (np.arange(SUB) + 0.5) / SUB - 0.5
    to_z = np.arange(cells_z)[None, :] // (2 * SUB) == rows[:, None]
    heights = np.tile(centres, cells_z // SUB)
    bz_of = np.arange(cells_z) // SUB % 2
    weights = np.zeros((2, 2, 2, 2, 32, cells_z))
    fields = np.zeros((3, 2, 3, 2, SUB, 2, 2, 2, 32))
    for index, power in enumerate(multi_index):
        for bz in range(2):
            weights[0, :, :, bz, index] = (bz_of == bz) * heights ** power[2]
            if power[2] > 0:
                weights[1, :, :, bz, index] = (bz_of == bz) * heights ** (power[2] - 1)
        for k in range(3):
            if power[k] > 0:
                lowered = list(power)
                lowered[k] -= 1
                for bx in range(2):
                    for by in range(2):
                        fields[k, bx, lowered[0], by, :, bx, by, :, index] = (
                            -power[k] / factorial_of(power) * centres ** lowered[1]
                        )[:, None]
    return (
        scale.reshape(16, wide),
        stacked(2.0).reshape(4, 64, 64),
        near,
        take_one.astype(float),
        take_two.astype(float),
        take_zero.astype(float),
        to_z.astype(float),
        weights.reshape(2, wide, cells_z),
        fields.reshape(3, 96, wide),
    )


def top_tables(nx, ny):
    lift = np.asarray(upward_matrices(4.0), np.float64)
    raise_up = np.zeros((4, slot, slot))
    lower_down = np.zeros((4, slot, 64))
    down = np.asarray(downward_matrices(4.0), np.float64)
    for bx in range(2):
        for by in range(2):
            for dz in range(2):
                raise_up[bx * 2 + by, (2 + dz) * count_m : (3 + dz) * count_m, :count_m] = (
                    lift[bx, by, dz] * 4.0 ** degrees[None, :]
                ).T
                lower_down[bx * 2 + by, :count_m, dz * 32 : dz * 32 + count_m] = down[bx, by, dz].T
    offsets = np.array(offset_grid(nx - 1, ny - 1, 1))
    kernels = np.asarray(translation_kernel(8.0, offsets), np.float64)
    counting = np.abs(offsets).max(axis=1) > 1
    far = np.zeros((len(offsets), slot, slot))
    far[:, :count_m, :count_m] = (kernels * counting[:, None, None]).transpose(0, 2, 1)
    return bool(counting.any()), raise_up, lower_down, far


def exact(left, right):
    return jnp.dot(left, right, precision=highest, preferred_element_type=jnp.float32)


def contract_rows(left, right):
    return lax.dot_general(
        left, right, (((0,), (0,)), ((), ())), precision=highest,
        preferred_element_type=jnp.float32,
    )


def sound(entropy, inverse):
    pressure = (gamma_gas - 1.0) * jnp.exp(gamma_gas * jnp.log(entropy))
    return pressure, jnp.sqrt(gamma_gas * pressure * inverse)


def states_of(stencil):
    a, b, c, d, e, f = stencil
    interface = (37.0 / 60.0) * (c + d) - (8.0 / 60.0) * (b + e) + (1.0 / 60.0) * (a + f)
    low, high = jnp.minimum(c, d), jnp.maximum(c, d)
    left = jnp.minimum(jnp.maximum(interface, jnp.minimum(b, low)), jnp.maximum(b, high))
    right = jnp.minimum(jnp.maximum(interface, jnp.minimum(e, low)), jnp.maximum(e, high))
    return left, right


def emit_fluxes(stencil_of, direction, count_fields, emit):
    mass = states_of(stencil_of(0))
    push = states_of(stencil_of(1 + direction))
    heat = states_of(stencil_of(5))
    inverse = [1.0 / value for value in mass]
    speed = [push[i] * inverse[i] for i in range(2)]
    gas = [sound(heat[i], inverse[i]) for i in range(2)]
    fastest = jnp.maximum(jnp.abs(speed[0]) + gas[0][1], jnp.abs(speed[1]) + gas[1][1])
    weight_left = 0.5 * (speed[0] + fastest)
    weight_right = 0.5 * (speed[1] - fastest)
    for field in range(count_fields):
        known = {0: mass, 1 + direction: push, 5: heat}
        left, right = known[field] if field in known else states_of(stencil_of(field))
        flux = left * weight_left + right * weight_right
        if field == 1 + direction:
            flux = flux + 0.5 * (gas[0][0] + gas[1][0])
        if field == 4:
            flux = flux + 0.5 * (gas[0][0] * speed[0] + gas[1][0] * speed[1])
        emit(field, flux)


def section_kernel(
    sizes, top,
    density, momentum, energy, entropy, tracers, flags,
    middle_hi, middle_lo, close_hi, close_lo,
    spread, along_z, cell_rows, pick_up, one_rows, second, two_rows, flag_z,
    scale, down_two, down_one, take_one, take_two, take_zero, to_z, weights, fields,
    raise_up, lower_down, far,
    section, accel,
    ext_x, ext_y, moved, previous, packed, packed_flux, tiles, near, window, rows_p,
    mid_hi, mid_lo, cls_hi, cls_lo,
    load_sem, table_sem, halo_send, halo_recv, first_send, first_recv,
    second_send, second_recv, side_send, side_recv,
):
    count_x, count_y, nf, cx, cy, cz = sizes
    mx, my = lax.axis_index("mx"), lax.axis_index("my")
    loads = [
        pltpu.make_async_copy(source, ext_x.at[pl.ds(begin, size), pl.ds(3, cx)], load_sem.at[i])
        for i, (source, begin, size) in enumerate(
            [(density, 0, 1), (momentum, 1, 3), (energy, 4, 1), (entropy, 5, 1), (tracers, 6, nf - 6)]
        )
    ]
    tables = [
        pltpu.make_async_copy(source, target, table_sem.at[i])
        for i, (source, target) in enumerate(
            [(middle_hi, mid_hi), (middle_lo, mid_lo), (close_hi, cls_hi), (close_lo, cls_lo)]
        )
    ]
    for copy in loads:
        copy.start()
    for copy in tables:
        copy.start()

    def at_x(step):
        return (lax.rem(mx + step + count_x, count_x), my)

    def at_y(step):
        return (mx, lax.rem(my + step + count_y, count_y))

    barrier = pltpu.get_barrier_semaphore()
    for step in range(1, count_x):
        pl.semaphore_signal(barrier, inc=1, device_id=at_x(step), device_id_type=MESH)
    for step in range(1, count_y):
        pl.semaphore_signal(barrier, inc=1, device_id=at_y(step), device_id_type=MESH)
    pl.semaphore_wait(barrier, count_x + count_y - 2)
    for copy in loads:
        copy.wait()

    def remote(source, target, send, recv, device):
        return pltpu.make_async_remote_copy(
            src_ref=source, dst_ref=target, send_sem=send, recv_sem=recv,
            device_id=device, device_id_type=MESH,
        )

    def halo_pair(buffer, length, base, place):
        lower = remote(
            buffer.at[:, pl.ds(3, 3)], buffer.at[:, pl.ds(length + 3, 3)],
            halo_send.at[base], halo_recv.at[base], place(-1),
        )
        upper = remote(
            buffer.at[:, pl.ds(length, 3)], buffer.at[:, pl.ds(0, 3)],
            halo_send.at[base + 1], halo_recv.at[base + 1], place(1),
        )
        return lower, upper

    def start_halo(pair, position, count):
        @pl.when(position > 0)
        def _():
            pair[0].start()

        @pl.when(position < count - 1)
        def _():
            pair[1].start()

    def finish_halo(pair, buffer, length, position, count):
        @pl.when(position > 0)
        def _():
            pair[0].wait_send()
            pair[1].wait_recv()

        @pl.when(position < count - 1)
        def _():
            pair[1].wait_send()
            pair[0].wait_recv()

        @pl.when(position == 0)
        def _():
            for row in range(3):
                buffer[:, row] = buffer[:, 3]

        @pl.when(position == count - 1)
        def _():
            for row in range(3):
                buffer[:, length + 3 + row] = buffer[:, length + 2]

    pair_x = halo_pair(ext_x, cx, 0, at_x)
    pair_y = halo_pair(ext_y, cy, 2, at_y)

    def turn(field, carry):
        for row in range(cy):
            ext_y[field, 3 + row] = ext_x[field, pl.ds(3, cx), row, :]
        return carry

    lax.fori_loop(0, nf, turn, 0)
    start_halo(pair_y, my, count_y)
    start_halo(pair_x, mx, count_x)

    def cell_speed(row, best):
        inverse = 1.0 / ext_x[0, 3 + row]
        largest = jnp.maximum(
            jnp.maximum(jnp.abs(ext_x[1, 3 + row]), jnp.abs(ext_x[2, 3 + row])),
            jnp.abs(ext_x[3, 3 + row]),
        )
        _, speed = sound(ext_x[5, 3 + row], inverse)
        return jnp.maximum(best, largest * inverse + speed)

    best = lax.fori_loop(0, cx, cell_speed, jnp.zeros((cy, cz), jnp.float32))
    best = jnp.max(best)

    for bx in range(2):
        flagged = jnp.concatenate(
            [
                exact(
                    jnp.broadcast_to(
                        flags[bx, by : by + 1, :].astype(jnp.float32), (SUB, flags.shape[2])
                    ),
                    flag_z[...],
                )
                for by in range(2)
            ],
            axis=0,
        )
        rows = [ext_x[0, 3 + bx * SUB + i] for i in range(SUB)]
        for power in range(4):
            total = jnp.zeros((cy, cz), jnp.float32)
            for i in range(SUB):
                total = total + rows[i] * (((i + 0.5) / SUB - 0.5) ** power)
            rows_p[pl.ds((bx * 4 + power) * 2 * SUB, 2 * SUB), :] = total * flagged
    weighted = contract_rows(rows_p[...], spread[...]) * along_z[...]
    shifted = exact(cell_rows[...], weighted)

    def choose(stack, lanes):
        lane = lax.rem(lax.broadcasted_iota(jnp.int32, (8, lanes), 1), slot)
        total = jnp.zeros((8, lanes), jnp.float32)
        for sd in range(6):
            inside = (lane >= sd * count_m) & (lane < (sd + 1) * count_m)
            total = total + jnp.where(inside, stack[sd * 8 : sd * 8 + 8], 0.0)
        return total

    block = choose(shifted, 4 * slot)
    near[1, 1] = block
    first = exact(block, pick_up[...])
    tile = choose(exact(one_rows[...], first), slot)
    px, py = lax.rem(mx, 2), lax.rem(my, 2)
    lifted = exact(first, second[px * 2 + py])
    for dz in range(2):
        part = exact(two_rows[dz * 48 : dz * 48 + 48], lifted[:, dz * slot : (dz + 1) * slot])
        tile = tile + choose(part, slot)
    row_index = lax.broadcasted_iota(jnp.int32, (8, slot), 0)
    tiles[mx, my] = jnp.where(row_index == 7, best, tile)

    for step in range(1, count_y):
        remote(
            tiles.at[mx, my], tiles.at[mx, my],
            first_send.at[step], first_recv.at[step], at_y(step),
        ).start()
    side_y = (
        remote(near.at[1, 1], near.at[1, 2], side_send.at[0], side_recv.at[0], at_y(-1)),
        remote(near.at[1, 1], near.at[1, 0], side_send.at[1], side_recv.at[1], at_y(1)),
    )
    start_halo(side_y, my, count_y)

    lane_z = lax.broadcasted_iota(jnp.int32, (cy, cz), 1)

    def pack(row, carry):
        mine = (lane_z >= row * 8) & (lane_z < row * 8 + 8)
        for field in range(nf):
            turned = pltpu.roll(ext_x[field, 3 + row], row * 8 + 3, 1)
            packed[field] = jnp.where(mine, turned, packed[field])
        return carry

    packed[...] = jnp.ones(packed.shape, jnp.float32)
    lax.fori_loop(0, cx, pack, 0)

    def end_stencil(field):
        value = packed[field]
        one = pltpu.roll(value, cz - 1, 1)
        two = pltpu.roll(value, cz - 2, 1)
        return value, one, two, two, two, two

    def end_emit(field, flux):
        packed_flux[field] = flux

    emit_fluxes(end_stencil, 2, nf, end_emit)

    def sweep_z(row, carry):
        def stencil(field):
            value = ext_x[field, 3 + row]
            first_lane = value[:, 0:1]
            last_lane = value[:, cz - 1 : cz]
            out = []
            for step in range(-3, 3):
                if step == 0:
                    out.append(value)
                elif step < 0:
                    out.append(jnp.where(lane_z < -step, first_lane, pltpu.roll(value, -step, 1)))
                else:
                    out.append(
                        jnp.where(lane_z >= cz - step, last_lane, pltpu.roll(value, cz - step, 1))
                    )
            return out

        def emit(field, flux):
            ending = pltpu.roll(packed_flux[field], cz - 1 - row * 8, 1)
            above = jnp.where(lane_z == cz - 1, ending, pltpu.roll(flux, cz - 1, 1))
            section[field, row] = above - flux

        emit_fluxes(stencil, 2, nf, emit)
        return carry

    lax.fori_loop(0, cx, sweep_z, 0)

    for step in range(1, count_y):
        arrived = tiles.at[mx, lax.rem(my - step + count_y, count_y)]
        copy = remote(arrived, arrived, first_send.at[step], first_recv.at[step], at_y(step))
        copy.wait_send()
        copy.wait_recv()

    def finish_side(pair, position, count, low, high):
        @pl.when(position > 0)
        def _():
            pair[0].wait_send()
            pair[1].wait_recv()

        @pl.when(position < count - 1)
        def _():
            pair[1].wait_send()
            pair[0].wait_recv()

        @pl.when(position == 0)
        def _():
            low[...] = jnp.zeros(low.shape, jnp.float32)

        @pl.when(position == count - 1)
        def _():
            high[...] = jnp.zeros(high.shape, jnp.float32)

    finish_side(side_y, my, count_y, near.at[1, 0], near.at[1, 2])
    for step in range(1, count_x):
        remote(
            tiles.at[mx], tiles.at[mx], second_send.at[step], second_recv.at[step], at_x(step)
        ).start()
    side_x = (
        remote(near.at[1], near.at[2], side_send.at[2], side_recv.at[2], at_x(-1)),
        remote(near.at[1], near.at[0], side_send.at[3], side_recv.at[3], at_x(1)),
    )
    start_halo(side_x, mx, count_x)

    def sweep(buffer, length, direction, store):
        def stencil_at(face):
            return lambda field: [buffer[field, face + i] for i in range(6)]

        def start_emit(field, flux):
            previous[field] = flux

        emit_fluxes(stencil_at(0), direction, nf, start_emit)

        def body(cell, carry):
            def emit(field, flux):
                store(field, cell, flux - previous[field])
                previous[field] = flux

            emit_fluxes(stencil_at(cell + 1), direction, nf, emit)
            return carry

        lax.fori_loop(0, length, body, 0)

    finish_halo(pair_y, ext_y, cy, my, count_y)

    def store_y(field, cell, value):
        moved[field, cell] = value

    sweep(ext_y, cy, 1, store_y)

    for step in range(1, count_x):
        arrived = tiles.at[lax.rem(mx - step + count_x, count_x)]
        copy = remote(arrived, arrived, second_send.at[step], second_recv.at[step], at_x(step))
        copy.wait_send()
        copy.wait_recv()
    finish_side(side_x, mx, count_x, near.at[0], near.at[2])

    fastest = jnp.max(jnp.max(tiles[...], axis=(0, 1))[7:8, :])
    step_size = courant / (SUB * jnp.full((1, cz), fastest, jnp.float32))

    one_x, one_y = mx // 2, my // 2
    two_x, two_y = mx // 4, my // 4

    def united(ux, uy):
        return (
            tiles[2 * ux, 2 * uy] + tiles[2 * ux, 2 * uy + 1]
            + tiles[2 * ux + 1, 2 * uy] + tiles[2 * ux + 1, 2 * uy + 1]
        )

    def held(value, count):
        return jnp.clip(value, 0, count - 1), (value >= 0) & (value < count)

    for dx in range(3):
        for dy in range(3):
            base = (dx * 3 + dy) * 4 * slot
            window[0:8, base : base + 4 * slot] = near[dx, dy]
            for bx in range(2):
                for by in range(2):
                    at = base + (bx * 2 + by) * slot
                    gx, in_x = held(2 * (one_x + dx - 1) + bx, count_x)
                    gy, in_y = held(2 * (one_y + dy - 1) + by, count_y)
                    ux, in_ux = held(2 * (two_x + dx - 1) + bx, count_x // 2)
                    uy, in_uy = held(2 * (two_y + dy - 1) + by, count_y // 2)
                    own = jnp.where(in_x & in_y, tiles[gx, gy], 0.0)
                    joint = jnp.where(in_ux & in_uy, united(ux, uy), 0.0)
                    window[8:16, at : at + slot] = jnp.where(
                        row_index < 4, own, jnp.where(row_index < 6, joint, 0.0)
                    )

    for copy in tables:
        copy.wait()

    def tripled(left, high, low):
        left_high = left.astype(jnp.bfloat16)
        left_low = (left - left_high.astype(jnp.float32)).astype(jnp.bfloat16)
        both = jnp.concatenate([left_high, left_low], axis=0)
        wide_part = jnp.dot(both, high, preferred_element_type=jnp.float32)
        size = left.shape[0]
        return (
            wide_part[:size] + wide_part[size:]
            + jnp.dot(left_high, low, preferred_element_type=jnp.float32)
        )

    sums = tripled(window[...], mid_hi[...], mid_lo[...]) * scale[...]
    inner = jnp.concatenate(
        [window[:, column * slot : (column + 1) * slot] for column in inner_columns], axis=1
    )
    touching = tripled(inner, cls_hi[...], cls_lo[...])

    def select(values, which):
        total = jnp.zeros((values.shape[0], 64), jnp.float32)
        for child in range(4):
            total = total + jnp.where(which == child, values[:, child * 64 : child * 64 + 64], 0.0)
        return total

    lane_64 = lax.broadcasted_iota(jnp.int32, (8, 64), 1)
    same_half = (lane_64 >= 32) == (lax.rem(lax.broadcasted_iota(jnp.int32, (8, 64), 0), 2) == 1)
    which_two = lax.rem(one_x, 2) * 2 + lax.rem(one_y, 2)
    second_sum = select(sums, which_two)
    if top:
        nx3, ny3 = count_x // 4, count_y // 4
        grown = jnp.zeros((8, slot), jnp.float32)
        for sx in range(nx3):
            for sy in range(ny3):
                source = jnp.zeros((8, slot), jnp.float32)
                for bx in range(2):
                    for by in range(2):
                        source = source + exact(
                            united(2 * sx + bx, 2 * sy + by), raise_up[bx * 2 + by]
                        )
                source = jnp.where((row_index == 4) | (row_index == 5), source, 0.0)
                place = ((sx - two_x + nx3 - 1) * (2 * ny3 - 1) + (sy - two_y + ny3 - 1)) * 3
                for dz in range(3):
                    moved_rows = source if dz == 1 else pltpu.roll(source, 1 if dz == 0 else 7, 0)
                    grown = grown + exact(moved_rows, far[place + dz])
        grown = jnp.where((row_index == 4) | (row_index == 5), grown, 0.0)
        carried = exact(grown, lower_down[which_two])
        second_sum = second_sum + jnp.concatenate([jnp.zeros((8, 64), jnp.float32), carried], axis=0)
    from_two = jnp.where(same_half, exact(take_two[...], second_sum), 0.0)
    first_sum = exact(take_one[...], select(sums, px * 2 + py)) + exact(
        from_two, down_two[px * 2 + py]
    )
    from_one = jnp.where(same_half, exact(take_zero[...], first_sum), 0.0)
    expansion = sums[0:8] + touching[0:8] + exact(from_one, down_one[...])
    on_z = contract_rows(expansion, to_z[...])
    for k in range(3):
        parts = exact(fields[k], on_z * weights[1 if k == 2 else 0])
        for row in range(cx):
            bx, height = row // SUB, (row % SUB + 0.5) / SUB - 0.5
            base = bx * 6 * SUB
            accel[k, row] = (
                parts[base : base + 2 * SUB]
                + height * parts[base + 2 * SUB : base + 4 * SUB]
                + (height * height) * parts[base + 4 * SUB : base + 6 * SUB]
            )

    finish_halo(pair_x, ext_x, cx, mx, count_x)

    def store_x(field, cell, value):
        total = (value + section[field, cell] + moved[field, :, cell, :]) * (-float(SUB))
        if 1 <= field <= 3:
            total = total + ext_x[0, 3 + cell] * accel[field - 1, cell]
        if field == 4:
            for k in range(3):
                total = total + ext_x[1 + k, 3 + cell] * accel[k, cell]
        section[field, cell] = ext_x[field, 3 + cell] + step_size * total

    sweep(ext_x, cx, 0, store_x)


def shards(density, momentum, energy, entropy, tracers, leaf_flags):
    count_x, count_y = lax.axis_size("mx"), lax.axis_size("my")
    cx, cy, cz = density.shape
    nf = 6 + tracers.shape[0]
    middle, close = window_tables()
    top, raise_up, lower_down, far = top_tables(count_x // 4, count_y // 4)
    constants = [
        *split_pair(middle),
        *split_pair(close),
        *[jnp.asarray(t, jnp.float32) for t in moment_tables(cz)],
        *[jnp.asarray(t, jnp.float32) for t in down_tables(cz)],
        *[jnp.asarray(t, jnp.float32) for t in (raise_up, lower_down, far)],
    ]
    anywhere = pl.BlockSpec(memory_space=pl.ANY)
    local = pl.BlockSpec(memory_space=pltpu.VMEM)
    dma = pltpu.SemaphoreType.DMA
    f32 = jnp.float32
    return pl.pallas_call(
        functools.partial(section_kernel, (count_x, count_y, nf, cx, cy, cz), top),
        out_shape=(
            jax.ShapeDtypeStruct((nf, cx, cy, cz), f32),
            jax.ShapeDtypeStruct((3, cx, cy, cz), f32),
        ),
        in_specs=[anywhere] * 5 + [local] + [anywhere] * 4 + [local] * (len(constants) - 4),
        out_specs=(local, local),
        scratch_shapes=[
            pltpu.VMEM((nf, cx + 6, cy, cz), f32),
            pltpu.VMEM((nf, cy + 6, cx, cz), f32),
            pltpu.VMEM((nf, cy, cx, cz), f32),
            pltpu.VMEM((nf, cy, cz), f32),
            pltpu.VMEM((nf, cy, cz), f32),
            pltpu.VMEM((nf, cy, cz), f32),
            pltpu.VMEM((count_x, count_y, 8, slot), f32),
            pltpu.VMEM((3, 3, 8, 4 * slot), f32),
            pltpu.VMEM((16, 36 * slot), f32),
            pltpu.VMEM((128, cz), f32),
            pltpu.VMEM(middle.shape, jnp.bfloat16),
            pltpu.VMEM(middle.shape, jnp.bfloat16),
            pltpu.VMEM(close.shape, jnp.bfloat16),
            pltpu.VMEM(close.shape, jnp.bfloat16),
            dma((5,)), dma((4,)), dma((4,)), dma((4,)),
            dma((count_y,)), dma((count_y,)), dma((count_x,)), dma((count_x,)),
            dma((4,)), dma((4,)),
        ],
        compiler_params=pltpu.CompilerParams(
            collective_id=0, has_side_effects=True, vmem_limit_bytes=56 * 1024 * 1024
        ),
    )(density[None], momentum, energy[None], entropy[None], tracers, leaf_flags, *constants)


def solution(mesh):
    placed = (
        P("mx", "my", None),
        P(None, "mx", "my", None),
        P("mx", "my", None),
        P("mx", "my", None),
        P(None, "mx", "my", None),
        P("mx", "my", None),
    )
    return jax.shard_map(
        shards,
        mesh=mesh,
        in_specs=placed,
        out_specs=(P(None, "mx", "my", None), P(None, "mx", "my", None)),
        check_vma=False,
    )
```

```python
import functools
import math

import jax
import jax.numpy as jnp
import numpy as np
from jax import lax
from jax.experimental import pallas as pl
from jax.experimental.pallas import tpu as pltpu
from jax.sharding import PartitionSpec as P

MESH = pl.DeviceIdType.MESH
SUB = 8
LEVELS = 3


gamma_gas = 5.0 / 3.0
courant = 0.3
gravity = 0.02
highest = lax.Precision.HIGHEST
multi_index = [
    (power_x, power_y, degree_sum - power_x - power_y)
    for degree_sum in range(4)
    for power_x in range(degree_sum, -1, -1)
    for power_y in range(degree_sum - power_x, -1, -1)
]


def factorial_of(exponent):
    return math.factorial(exponent[0]) * math.factorial(exponent[1]) * math.factorial(exponent[2])


def inverse_derivative(exponent, vectors):
    axes_list = [0] * exponent[0] + [1] * exponent[1] + [2] * exponent[2]
    radius = np.sqrt(np.sum(vectors * vectors, axis=1))
    radius_safe = np.where(radius > 0.0, radius, 1.0)
    degree = len(axes_list)
    if degree == 0:
        result = 1.0 / radius_safe
    elif degree == 1:
        result = -vectors[:, axes_list[0]] / radius_safe**3
    elif degree == 2:
        index_one, index_two = axes_list
        result = (
            3.0 * vectors[:, index_one] * vectors[:, index_two] / radius_safe**5
            - float(index_one == index_two) / radius_safe**3
        )
    else:
        index_one, index_two, index_three = axes_list
        crossed = (
            float(index_one == index_two) * vectors[:, index_three]
            + float(index_one == index_three) * vectors[:, index_two]
            + float(index_two == index_three) * vectors[:, index_one]
        )
        result = (
            -15.0
            * vectors[:, index_one]
            * vectors[:, index_two]
            * vectors[:, index_three]
            / radius_safe**7
            + 3.0 * crossed / radius_safe**5
        )
    return np.where(radius > 0.0, result, 0.0)


def offset_grid(reach_x, reach_y, reach_z):
    return [
        (shift_x, shift_y, shift_z)
        for shift_x in range(-reach_x, reach_x + 1)
        for shift_y in range(-reach_y, reach_y + 1)
        for shift_z in range(-reach_z, reach_z + 1)
    ]


def translation_kernel(spacing, offsets):
    vectors = np.asarray(offsets) * (-1.0 * spacing)
    entries = np.zeros((len(offsets), len(multi_index), len(multi_index)))
    for row_index, target_power in enumerate(multi_index):
        for column_index, source_power in enumerate(multi_index):
            if sum(target_power) + sum(source_power) <= 3:
                joined = (
                    target_power[0] + source_power[0],
                    target_power[1] + source_power[1],
                    target_power[2] + source_power[2],
                )
                entries[:, row_index, column_index] = (
                    -gravity
                    * (-1.0) ** sum(source_power)
                    / factorial_of(source_power)
                    * inverse_derivative(joined, vectors)
                )
    return entries.astype(np.float32)


def upward_matrices(spacing):
    entries = np.zeros((2, 2, 2, len(multi_index), len(multi_index)))
    for octant in range(8):
        octant_bits = (octant >> 2 & 1, octant >> 1 & 1, octant & 1)
        displacement = [(octant_bits[dimension] - 0.5) * spacing for dimension in range(3)]
        for row_index, target_power in enumerate(multi_index):
            for column_index, source_power in enumerate(multi_index):
                if all(
                    (source_power[dimension] <= target_power[dimension] for dimension in range(3))
                ):
                    entry_value = 1.0
                    for dimension in range(3):
                        entry_value *= math.comb(
                            target_power[dimension], source_power[dimension]
                        ) * displacement[dimension] ** (
                            target_power[dimension] - source_power[dimension]
                        )
                    entries[
                        octant_bits[0], octant_bits[1], octant_bits[2], row_index, column_index
                    ] = entry_value
    return entries.astype(np.float32)


def downward_matrices(spacing):
    entries = np.zeros((2, 2, 2, len(multi_index), len(multi_index)))
    for octant in range(8):
        octant_bits = (octant >> 2 & 1, octant >> 1 & 1, octant & 1)
        displacement = [(octant_bits[dimension] - 0.5) * spacing for dimension in range(3)]
        for row_index, target_power in enumerate(multi_index):
            for column_index, source_power in enumerate(multi_index):
                if all(
                    (source_power[dimension] >= target_power[dimension] for dimension in range(3))
                ):
                    entry_value = 1.0
                    for dimension in range(3):
                        lifted = source_power[dimension] - target_power[dimension]
                        entry_value *= displacement[dimension] ** lifted / math.factorial(lifted)
                    entries[
                        octant_bits[0], octant_bits[1], octant_bits[2], row_index, column_index
                    ] = entry_value
    return entries.astype(np.float32)


slot = 128
wide = 256
count_m = len(multi_index)
degrees = np.array([sum(exponent) for exponent in multi_index])
inner_columns = [
    (dx * 3 + dy) * 4 + bx * 2 + by
    for dx in range(3)
    for dy in range(3)
    for bx in range(2)
    for by in range(2)
    if 1 <= 2 * dx + bx <= 4 and 1 <= 2 * dy + by <= 4
]


def split_pair(table):
    table = jnp.asarray(table, jnp.float32)
    high = table.astype(jnp.bfloat16)
    return high, (table - high.astype(jnp.float32)).astype(jnp.bfloat16)


def window_tables():
    columns = [
        (2 * dx - 2 + bx, 2 * dy - 2 + by)
        for dx in range(3)
        for dy in range(3)
        for bx in range(2)
        for by in range(2)
    ]
    children = [(i >> 2 & 1, i >> 1 & 1, i & 1) for i in range(8)]
    sources = [(cx, cy, sz - 2) for cx, cy in columns for sz in range(6)]
    offsets = np.array([[[s[k] - t[k] for k in range(3)] for t in children] for s in sources])
    kernels = np.asarray(translation_kernel(1.0, offsets.reshape(-1, 3)), np.float64)
    kernels = kernels.reshape(36, 6, 8, count_m, count_m)
    touching = (np.abs(offsets).max(axis=2) <= 1).reshape(36, 6, 8, 1, 1)

    def laid(part):
        out = np.zeros((36, slot, 8, 32))
        out[:, : 6 * count_m, :, :count_m] = part.transpose(0, 1, 4, 2, 3).reshape(
            36, 6 * count_m, 8, count_m
        )
        return out.reshape(36, slot, wide)

    middle = laid(np.where(touching, 0.0, kernels))
    close = laid(np.where(touching, kernels, 0.0))[np.array(inner_columns)]
    return middle.reshape(-1, wide), close.reshape(-1, wide)


def moment_tables(cells_z):
    centres = (np.arange(SUB) + 0.5) / SUB - 0.5
    spread = np.zeros((2, 4, 2, SUB, 4, slot))
    along_z = np.zeros((cells_z, 4, slot))
    pick_up = np.zeros((4, slot, slot))
    lift = np.asarray(upward_matrices(1.0), np.float64)
    lift_two = np.asarray(upward_matrices(2.0), np.float64)
    second = np.zeros((4, slot, 2 * slot))
    for sd in range(6):
        for index, power in enumerate(multi_index):
            lane = sd * count_m + index
            for bx in range(2):
                for by in range(2):
                    spread[bx, power[0], by, :, bx * 2 + by, lane] = (
                        centres ** power[1] / SUB**3
                    )
            along_z[:, :, lane] = (np.tile(centres, cells_z // SUB) ** power[2])[:, None]
            for bx in range(2):
                for by in range(2):
                    for dz in range(2):
                        for lower in range(count_m):
                            pick_up[bx * 2 + by, (2 + dz) * count_m + lower, lane] = (
                                lift[bx, by, dz, index, lower] * 0.5 ** sum(power)
                            )
                            second[bx * 2 + by, lower, dz * slot + lane] = (
                                lift_two[bx, by, dz, index, lower]
                                * 2.0 ** degrees[lower]
                                * 0.25 ** sum(power)
                            )
    parents = cells_z // SUB // 2
    rows = np.arange(8)
    cell_rows = np.zeros((6, 8, cells_z))
    one_rows = np.zeros((6, 8, 8))
    two_rows = np.zeros((2, 6, 8, 8))
    for s in range(3):
        for dz in range(2):
            sd = s * 2 + dz
            for row in rows:
                cell_rows[sd, row] = np.arange(cells_z) // SUB == 2 * (row + s - 1) + dz
                if row < parents // 2:
                    one_rows[sd, row] = rows == 2 * (row + s - 1) + dz
                if 4 <= row < 4 + parents // 4:
                    second_z = 2 * (row - 4 + s - 1) + dz
                    if 0 <= second_z < parents // 2:
                        for dz_one in range(2):
                            two_rows[dz_one, sd, row] = rows == 2 * second_z + dz_one
    return (
        spread.reshape(128, 4 * slot),
        along_z.reshape(cells_z, 4 * slot),
        cell_rows.reshape(48, cells_z),
        pick_up.reshape(4 * slot, slot),
        one_rows.reshape(48, 8),
        second,
        two_rows.reshape(96, 8),
        (np.arange(cells_z)[None, :] // SUB == np.arange(cells_z // SUB)[:, None]).astype(float),
    )


def down_tables(cells_z):
    def stacked(spacing):
        down = np.asarray(downward_matrices(spacing), np.float64)
        out = np.zeros((2, 2, 2, 32, 2, 32))
        for bz in range(2):
            for child in range(2):
                out[:, :, bz, :count_m, child, :count_m] = down[:, :, child].transpose(0, 1, 3, 2)
        return out

    scale = np.zeros((16, 8, 32))
    scale[:8, :, :count_m] = 1.0
    scale[8:12, :, :count_m] = 0.5 ** (degrees + 1)
    scale[12:14, :, :count_m] = 0.25 ** (degrees + 1)
    near = stacked(1.0)
    near = near.transpose(2, 3, 0, 1, 4, 5).reshape(64, wide)
    rows = np.arange(8)
    take_one = (np.arange(16)[None, :] == 8 + rows[:, None]) & (rows[:, None] < 4)
    take_two = (np.arange(16)[None, :] == 12 + rows[:, None] // 2) & (rows[:, None] < 4)
    take_zero = np.arange(8)[None, :] == rows[:, None] // 2
    centres = (np.arange(SUB) + 0.5) / SUB - 0.5
    to_z = np.arange(cells_z)[None, :] // (2 * SUB) == rows[:, None]
    heights = np.tile(centres, cells_z // SUB)
    bz_of = np.arange(cells_z) // SUB % 2
    weights = np.zeros((2, 2, 2, 2, 32, cells_z))
    fields = np.zeros((3, 2, 3, 2, SUB, 2, 2, 2, 32))
    for index, power in enumerate(multi_index):
        for bz in range(2):
            weights[0, :, :, bz, index] = (bz_of == bz) * heights ** power[2]
            if power[2] > 0:
                weights[1, :, :, bz, index] = (bz_of == bz) * heights ** (power[2] - 1)
        for k in range(3):
            if power[k] > 0:
                lowered = list(power)
                lowered[k] -= 1
                for bx in range(2):
                    for by in range(2):
                        fields[k, bx, lowered[0], by, :, bx, by, :, index] = (
                            -power[k] / factorial_of(power) * centres ** lowered[1]
                        )[:, None]
    return (
        scale.reshape(16, wide),
        stacked(2.0).reshape(4, 64, 64),
        near,
        take_one.astype(float),
        take_two.astype(float),
        take_zero.astype(float),
        to_z.astype(float),
        weights.reshape(2, wide, cells_z),
        fields.reshape(3, 96, wide),
    )


def top_tables(nx, ny):
    lift = np.asarray(upward_matrices(4.0), np.float64)
    raise_up = np.zeros((4, slot, slot))
    lower_down = np.zeros((4, slot, 64))
    down = np.asarray(downward_matrices(4.0), np.float64)
    for bx in range(2):
        for by in range(2):
            for dz in range(2):
                raise_up[bx * 2 + by, (2 + dz) * count_m : (3 + dz) * count_m, :count_m] = (
                    lift[bx, by, dz] * 4.0 ** degrees[None, :]
                ).T
                lower_down[bx * 2 + by, :count_m, dz * 32 : dz * 32 + count_m] = down[bx, by, dz].T
    offsets = np.array(offset_grid(nx - 1, ny - 1, 1))
    kernels = np.asarray(translation_kernel(8.0, offsets), np.float64)
    counting = np.abs(offsets).max(axis=1) > 1
    far = np.zeros((len(offsets), slot, slot))
    far[:, :count_m, :count_m] = (kernels * counting[:, None, None]).transpose(0, 2, 1)
    return bool(counting.any()), raise_up, lower_down, far


def exact(left, right):
    return jnp.dot(left, right, precision=highest, preferred_element_type=jnp.float32)


def contract_rows(left, right):
    return lax.dot_general(
        left, right, (((0,), (0,)), ((), ())), precision=highest,
        preferred_element_type=jnp.float32,
    )


def sound(entropy, inverse):
    pressure = (gamma_gas - 1.0) * jnp.exp(gamma_gas * jnp.log(entropy))
    return pressure, jnp.sqrt(gamma_gas * pressure * inverse)


def states_of(stencil):
    a, b, c, d, e, f = stencil
    interface = (37.0 / 60.0) * (c + d) - (8.0 / 60.0) * (b + e) + (1.0 / 60.0) * (a + f)
    low, high = jnp.minimum(c, d), jnp.maximum(c, d)
    left = jnp.minimum(jnp.maximum(interface, jnp.minimum(b, low)), jnp.maximum(b, high))
    right = jnp.minimum(jnp.maximum(interface, jnp.minimum(e, low)), jnp.maximum(e, high))
    return left, right


def prepare(stencil_of, direction):
    mass = states_of(stencil_of(0))
    push = states_of(stencil_of(1 + direction))
    heat = states_of(stencil_of(5))
    inverse = [1.0 / value for value in mass]
    speed = [push[i] * inverse[i] for i in range(2)]
    gas = [sound(heat[i], inverse[i]) for i in range(2)]
    fastest = jnp.maximum(jnp.abs(speed[0]) + gas[0][1], jnp.abs(speed[1]) + gas[1][1])
    weights = 0.5 * (speed[0] + fastest), 0.5 * (speed[1] - fastest)
    flux = [left * weights[0] + right * weights[1] for left, right in (mass, push, heat)]
    flux[1] = flux[1] + 0.5 * (gas[0][0] + gas[1][0])
    work = 0.5 * (gas[0][0] * speed[0] + gas[1][0] * speed[1])
    return (*flux, *weights, work)


def apply(prepared, stencil_of, direction, count_fields, emit):
    known = dict(zip((0, 1 + direction, 5), prepared[:3]))
    for field in range(count_fields):
        if field in known:
            emit(field, known[field])
            continue
        left, right = states_of(stencil_of(field))
        flux = left * prepared[3] + right * prepared[4]
        emit(field, flux + prepared[5] if field == 4 else flux)


def section_kernel(
    sizes, top,
    density, momentum, energy, entropy, tracers, flags,
    middle_hi, middle_lo, close_hi, close_lo,
    spread, along_z, cell_rows, pick_up, one_rows, second, two_rows, flag_z,
    scale, down_two, down_one, take_one, take_two, take_zero, to_z, weights, fields,
    raise_up, lower_down, far,
    section, accel,
    ext_x, ext_y, moved, previous, packed, packed_flux, tiles, near, window, rows_p,
    mid_hi, mid_lo, cls_hi, cls_lo,
    load_sem, table_sem, halo_send, halo_recv, first_send, first_recv,
    second_send, second_recv, side_send, side_recv,
):
    count_x, count_y, nf, cx, cy, cz = sizes
    mx, my = lax.axis_index("mx"), lax.axis_index("my")
    loads = [
        pltpu.make_async_copy(source, ext_x.at[pl.ds(begin, size), pl.ds(3, cx)], load_sem.at[i])
        for i, (source, begin, size) in enumerate(
            [(density, 0, 1), (momentum, 1, 3), (energy, 4, 1), (entropy, 5, 1), (tracers, 6, nf - 6)]
        )
    ]
    tables = [
        pltpu.make_async_copy(source, target, table_sem.at[i])
        for i, (source, target) in enumerate(
            [(middle_hi, mid_hi), (middle_lo, mid_lo), (close_hi, cls_hi), (close_lo, cls_lo)]
        )
    ]
    for copy in loads:
        copy.start()
    for copy in tables:
        copy.start()

    def at_x(step):
        return (lax.rem(mx + step + count_x, count_x), my)

    def at_y(step):
        return (mx, lax.rem(my + step + count_y, count_y))

    barrier = pltpu.get_barrier_semaphore()
    for step in range(1, count_x):
        pl.semaphore_signal(barrier, inc=1, device_id=at_x(step), device_id_type=MESH)
    for step in range(1, count_y):
        pl.semaphore_signal(barrier, inc=1, device_id=at_y(step), device_id_type=MESH)
    for copy in loads:
        copy.wait()

    def remote(source, target, send, recv, device):
        return pltpu.make_async_remote_copy(
            src_ref=source, dst_ref=target, send_sem=send, recv_sem=recv,
            device_id=device, device_id_type=MESH,
        )

    def halo_pair(buffer, length, base, place):
        lower = remote(
            buffer.at[:, pl.ds(3, 3)], buffer.at[:, pl.ds(length + 3, 3)],
            halo_send.at[base], halo_recv.at[base], place(-1),
        )
        upper = remote(
            buffer.at[:, pl.ds(length, 3)], buffer.at[:, pl.ds(0, 3)],
            halo_send.at[base + 1], halo_recv.at[base + 1], place(1),
        )
        return lower, upper

    def start_halo(pair, position, count):
        @pl.when(position > 0)
        def _():
            pair[0].start()

        @pl.when(position < count - 1)
        def _():
            pair[1].start()

    def finish_halo(pair, buffer, length, position, count):
        @pl.when(position > 0)
        def _():
            pair[0].wait_send()
            pair[1].wait_recv()

        @pl.when(position < count - 1)
        def _():
            pair[1].wait_send()
            pair[0].wait_recv()

        @pl.when(position == 0)
        def _():
            for row in range(3):
                buffer[:, row] = buffer[:, 3]

        @pl.when(position == count - 1)
        def _():
            for row in range(3):
                buffer[:, length + 3 + row] = buffer[:, length + 2]

    pair_x = halo_pair(ext_x, cx, 0, at_x)
    pair_y = halo_pair(ext_y, cy, 2, at_y)

    def turn(field, carry):
        for row in range(cy):
            ext_y[field, 3 + row] = ext_x[field, pl.ds(3, cx), row, :]
        return carry

    lax.fori_loop(0, nf, turn, 0)
    pl.semaphore_wait(barrier, count_x + count_y - 2)
    start_halo(pair_y, my, count_y)
    start_halo(pair_x, mx, count_x)

    planes = 4

    def cell_speed(step, best):
        rows = pl.ds(3 + step * planes, planes)
        inverse = 1.0 / ext_x[0, rows]
        largest = jnp.maximum(
            jnp.maximum(jnp.abs(ext_x[1, rows]), jnp.abs(ext_x[2, rows])), jnp.abs(ext_x[3, rows])
        )
        _, speed = sound(ext_x[5, rows], inverse)
        return jnp.maximum(best, jnp.max(largest * inverse + speed, axis=0))

    best = lax.fori_loop(0, cx // planes, cell_speed, jnp.zeros((cy, cz), jnp.float32))
    best = jnp.max(best)

    for bx in range(2):
        flagged = jnp.concatenate(
            [
                exact(
                    jnp.broadcast_to(
                        flags[bx, by : by + 1, :].astype(jnp.float32), (SUB, flags.shape[2])
                    ),
                    flag_z[...],
                )
                for by in range(2)
            ],
            axis=0,
        )
        rows = [ext_x[0, 3 + bx * SUB + i] for i in range(SUB)]
        for power in range(4):
            total = jnp.zeros((cy, cz), jnp.float32)
            for i in range(SUB):
                total = total + rows[i] * (((i + 0.5) / SUB - 0.5) ** power)
            rows_p[pl.ds((bx * 4 + power) * 2 * SUB, 2 * SUB), :] = total * flagged
    weighted = contract_rows(rows_p[...], spread[...]) * along_z[...]
    shifted = exact(cell_rows[...], weighted)

    def choose(stack, lanes):
        lane = lax.rem(lax.broadcasted_iota(jnp.int32, (8, lanes), 1), slot)
        total = jnp.zeros((8, lanes), jnp.float32)
        for sd in range(6):
            inside = (lane >= sd * count_m) & (lane < (sd + 1) * count_m)
            total = total + jnp.where(inside, stack[sd * 8 : sd * 8 + 8], 0.0)
        return total

    block = choose(shifted, 4 * slot)
    near[1, 1] = block
    first = exact(block, pick_up[...])
    tile = choose(exact(one_rows[...], first), slot)
    px, py = lax.rem(mx, 2), lax.rem(my, 2)
    lifted = exact(first, second[px * 2 + py])
    for dz in range(2):
        part = exact(two_rows[dz * 48 : dz * 48 + 48], lifted[:, dz * slot : (dz + 1) * slot])
        tile = tile + choose(part, slot)
    row_index = lax.broadcasted_iota(jnp.int32, (8, slot), 0)
    tiles[mx, my] = jnp.where(row_index == 7, best, tile)

    for step in range(1, count_y):
        remote(
            tiles.at[mx, my], tiles.at[mx, my],
            first_send.at[step], first_recv.at[step], at_y(step),
        ).start()
    side_y = (
        remote(near.at[1, 1], near.at[1, 2], side_send.at[0], side_recv.at[0], at_y(-1)),
        remote(near.at[1, 1], near.at[1, 0], side_send.at[1], side_recv.at[1], at_y(1)),
    )
    start_halo(side_y, my, count_y)

    lane_z = lax.broadcasted_iota(jnp.int32, (cy, cz), 1)

    def pack(row, carry):
        mine = (lane_z >= row * 8) & (lane_z < row * 8 + 8)
        for field in range(nf):
            turned = pltpu.roll(ext_x[field, 3 + row], row * 8 + 3, 1)
            packed[field] = jnp.where(mine, turned, packed[field])
        return carry

    packed[...] = jnp.ones(packed.shape, jnp.float32)
    lax.fori_loop(0, cx, pack, 0)

    def end_stencil(field):
        value = packed[field]
        one = pltpu.roll(value, cz - 1, 1)
        two = pltpu.roll(value, cz - 2, 1)
        return value, one, two, two, two, two

    def end_emit(field, flux):
        packed_flux[field] = flux

    apply(prepare(end_stencil, 2), end_stencil, 2, nf, end_emit)

    def stencil_z(row):
        def stencil(field):
            value = ext_x[field, 3 + row]
            out = [value]
            for step in range(3):
                out.insert(0, jnp.where(lane_z < 1, value, pltpu.roll(out[0], 1, 1)))
            for step in range(2):
                out.append(jnp.where(lane_z == cz - 1, value, pltpu.roll(out[-1], cz - 1, 1)))
            return out

        return stencil

    def sweep_z(row, prepared):
        following = prepare(stencil_z(jnp.minimum(row + 1, cx - 1)), 2)

        def emit(field, flux):
            ending = pltpu.roll(packed_flux[field], cz - 1 - row * 8, 1)
            above = jnp.where(lane_z == cz - 1, ending, pltpu.roll(flux, cz - 1, 1))
            section[field, row] = above - flux

        apply(prepared, stencil_z(row), 2, nf, emit)
        return following

    lax.fori_loop(0, cx, sweep_z, prepare(stencil_z(0), 2))

    for step in range(1, count_y):
        arrived = tiles.at[mx, lax.rem(my - step + count_y, count_y)]
        copy = remote(arrived, arrived, first_send.at[step], first_recv.at[step], at_y(step))
        copy.wait_send()
        copy.wait_recv()

    def finish_side(pair, position, count, low, high):
        @pl.when(position > 0)
        def _():
            pair[0].wait_send()
            pair[1].wait_recv()

        @pl.when(position < count - 1)
        def _():
            pair[1].wait_send()
            pair[0].wait_recv()

        @pl.when(position == 0)
        def _():
            low[...] = jnp.zeros(low.shape, jnp.float32)

        @pl.when(position == count - 1)
        def _():
            high[...] = jnp.zeros(high.shape, jnp.float32)

    finish_side(side_y, my, count_y, near.at[1, 0], near.at[1, 2])
    for step in range(1, count_x):
        remote(
            tiles.at[mx], tiles.at[mx], second_send.at[step], second_recv.at[step], at_x(step)
        ).start()
    side_x = (
        remote(near.at[1], near.at[2], side_send.at[2], side_recv.at[2], at_x(-1)),
        remote(near.at[1], near.at[0], side_send.at[3], side_recv.at[3], at_x(1)),
    )
    start_halo(side_x, mx, count_x)

    def sweep(buffer, length, direction, store):
        def stencil_at(face):
            return lambda field: [buffer[field, face + i] for i in range(6)]

        def start_emit(field, flux):
            previous[field] = flux

        apply(prepare(stencil_at(0), direction), stencil_at(0), direction, nf, start_emit)

        def body(cell, prepared):
            following = prepare(stencil_at(jnp.minimum(cell + 2, length)), direction)

            def emit(field, flux):
                store(field, cell, flux - previous[field])
                previous[field] = flux

            apply(prepared, stencil_at(cell + 1), direction, nf, emit)
            return following

        lax.fori_loop(0, length, body, prepare(stencil_at(1), direction))

    finish_halo(pair_y, ext_y, cy, my, count_y)

    def store_y(field, cell, value):
        moved[field, cell] = value

    sweep(ext_y, cy, 1, store_y)

    for step in range(1, count_x):
        arrived = tiles.at[lax.rem(mx - step + count_x, count_x)]
        copy = remote(arrived, arrived, second_send.at[step], second_recv.at[step], at_x(step))
        copy.wait_send()
        copy.wait_recv()
    finish_side(side_x, mx, count_x, near.at[0], near.at[2])

    fastest = jnp.max(jnp.max(tiles[...], axis=(0, 1))[7:8, :])
    step_size = courant / (SUB * jnp.full((1, cz), fastest, jnp.float32))

    one_x, one_y = mx // 2, my // 2
    two_x, two_y = mx // 4, my // 4

    def united(ux, uy):
        return (
            tiles[2 * ux, 2 * uy] + tiles[2 * ux, 2 * uy + 1]
            + tiles[2 * ux + 1, 2 * uy] + tiles[2 * ux + 1, 2 * uy + 1]
        )

    def held(value, count):
        return jnp.clip(value, 0, count - 1), (value >= 0) & (value < count)

    for dx in range(3):
        for dy in range(3):
            base = (dx * 3 + dy) * 4 * slot
            window[0:8, base : base + 4 * slot] = near[dx, dy]
            for bx in range(2):
                for by in range(2):
                    at = base + (bx * 2 + by) * slot
                    gx, in_x = held(2 * (one_x + dx - 1) + bx, count_x)
                    gy, in_y = held(2 * (one_y + dy - 1) + by, count_y)
                    ux, in_ux = held(2 * (two_x + dx - 1) + bx, count_x // 2)
                    uy, in_uy = held(2 * (two_y + dy - 1) + by, count_y // 2)
                    own = jnp.where(in_x & in_y, tiles[gx, gy], 0.0)
                    joint = jnp.where(in_ux & in_uy, united(ux, uy), 0.0)
                    window[8:16, at : at + slot] = jnp.where(
                        row_index < 4, own, jnp.where(row_index < 6, joint, 0.0)
                    )

    for copy in tables:
        copy.wait()

    def tripled(left, high, low):
        left_high = left.astype(jnp.bfloat16)
        left_low = (left - left_high.astype(jnp.float32)).astype(jnp.bfloat16)
        both = jnp.concatenate([left_high, left_low], axis=0)
        wide_part = jnp.dot(both, high, preferred_element_type=jnp.float32)
        size = left.shape[0]
        return (
            wide_part[:size] + wide_part[size:]
            + jnp.dot(left_high, low, preferred_element_type=jnp.float32)
        )

    sums = tripled(window[...], mid_hi[...], mid_lo[...]) * scale[...]
    inner = jnp.concatenate(
        [window[:, column * slot : (column + 1) * slot] for column in inner_columns], axis=1
    )
    touching = tripled(inner, cls_hi[...], cls_lo[...])

    def select(values, which):
        total = jnp.zeros((values.shape[0], 64), jnp.float32)
        for child in range(4):
            total = total + jnp.where(which == child, values[:, child * 64 : child * 64 + 64], 0.0)
        return total

    lane_64 = lax.broadcasted_iota(jnp.int32, (8, 64), 1)
    same_half = (lane_64 >= 32) == (lax.rem(lax.broadcasted_iota(jnp.int32, (8, 64), 0), 2) == 1)
    which_two = lax.rem(one_x, 2) * 2 + lax.rem(one_y, 2)
    second_sum = select(sums, which_two)
    if top:
        nx3, ny3 = count_x // 4, count_y // 4
        grown = jnp.zeros((8, slot), jnp.float32)
        for sx in range(nx3):
            for sy in range(ny3):
                source = jnp.zeros((8, slot), jnp.float32)
                for bx in range(2):
                    for by in range(2):
                        source = source + exact(
                            united(2 * sx + bx, 2 * sy + by), raise_up[bx * 2 + by]
                        )
                source = jnp.where((row_index == 4) | (row_index == 5), source, 0.0)
                place = ((sx - two_x + nx3 - 1) * (2 * ny3 - 1) + (sy - two_y + ny3 - 1)) * 3
                for dz in range(3):
                    moved_rows = source if dz == 1 else pltpu.roll(source, 1 if dz == 0 else 7, 0)
                    grown = grown + exact(moved_rows, far[place + dz])
        grown = jnp.where((row_index == 4) | (row_index == 5), grown, 0.0)
        carried = exact(grown, lower_down[which_two])
        second_sum = second_sum + jnp.concatenate([jnp.zeros((8, 64), jnp.float32), carried], axis=0)
    from_two = jnp.where(same_half, exact(take_two[...], second_sum), 0.0)
    first_sum = exact(take_one[...], select(sums, px * 2 + py)) + exact(
        from_two, down_two[px * 2 + py]
    )
    from_one = jnp.where(same_half, exact(take_zero[...], first_sum), 0.0)
    expansion = sums[0:8] + touching[0:8] + exact(from_one, down_one[...])
    on_z = contract_rows(expansion, to_z[...])
    for k in range(3):
        parts = exact(fields[k], on_z * weights[1 if k == 2 else 0])
        for row in range(cx):
            bx, height = row // SUB, (row % SUB + 0.5) / SUB - 0.5
            base = bx * 6 * SUB
            accel[k, row] = (
                parts[base : base + 2 * SUB]
                + height * parts[base + 2 * SUB : base + 4 * SUB]
                + (height * height) * parts[base + 4 * SUB : base + 6 * SUB]
            )

    finish_halo(pair_x, ext_x, cx, mx, count_x)

    def store_x(field, cell, value):
        total = (value + section[field, cell] + moved[field, :, cell, :]) * (-float(SUB))
        if 1 <= field <= 3:
            total = total + ext_x[0, 3 + cell] * accel[field - 1, cell]
        if field == 4:
            for k in range(3):
                total = total + ext_x[1 + k, 3 + cell] * accel[k, cell]
        section[field, cell] = ext_x[field, 3 + cell] + step_size * total

    sweep(ext_x, cx, 0, store_x)


def shards(density, momentum, energy, entropy, tracers, leaf_flags):
    count_x, count_y = lax.axis_size("mx"), lax.axis_size("my")
    cx, cy, cz = density.shape
    nf = 6 + tracers.shape[0]
    middle, close = window_tables()
    top, raise_up, lower_down, far = top_tables(count_x // 4, count_y // 4)
    constants = [
        *split_pair(middle),
        *split_pair(close),
        *[jnp.asarray(t, jnp.float32) for t in moment_tables(cz)],
        *[jnp.asarray(t, jnp.float32) for t in down_tables(cz)],
        *[jnp.asarray(t, jnp.float32) for t in (raise_up, lower_down, far)],
    ]
    anywhere = pl.BlockSpec(memory_space=pl.ANY)
    local = pl.BlockSpec(memory_space=pltpu.VMEM)
    dma = pltpu.SemaphoreType.DMA
    f32 = jnp.float32
    return pl.pallas_call(
        functools.partial(section_kernel, (count_x, count_y, nf, cx, cy, cz), top),
        out_shape=(
            jax.ShapeDtypeStruct((nf, cx, cy, cz), f32),
            jax.ShapeDtypeStruct((3, cx, cy, cz), f32),
        ),
        in_specs=[anywhere] * 5 + [local] + [anywhere] * 4 + [local] * (len(constants) - 4),
        out_specs=(local, local),
        scratch_shapes=[
            pltpu.VMEM((nf, cx + 6, cy, cz), f32),
            pltpu.VMEM((nf, cy + 6, cx, cz), f32),
            pltpu.VMEM((nf, cy, cx, cz), f32),
            pltpu.VMEM((nf, cy, cz), f32),
            pltpu.VMEM((nf, cy, cz), f32),
            pltpu.VMEM((nf, cy, cz), f32),
            pltpu.VMEM((count_x, count_y, 8, slot), f32),
            pltpu.VMEM((3, 3, 8, 4 * slot), f32),
            pltpu.VMEM((16, 36 * slot), f32),
            pltpu.VMEM((128, cz), f32),
            pltpu.VMEM(middle.shape, jnp.bfloat16),
            pltpu.VMEM(middle.shape, jnp.bfloat16),
            pltpu.VMEM(close.shape, jnp.bfloat16),
            pltpu.VMEM(close.shape, jnp.bfloat16),
            dma((5,)), dma((4,)), dma((4,)), dma((4,)),
            dma((count_y,)), dma((count_y,)), dma((count_x,)), dma((count_x,)),
            dma((4,)), dma((4,)),
        ],
        compiler_params=pltpu.CompilerParams(
            collective_id=0, has_side_effects=True, vmem_limit_bytes=56 * 1024 * 1024
        ),
    )(density[None], momentum, energy[None], entropy[None], tracers, leaf_flags, *constants)


def solution(mesh):
    placed = (
        P("mx", "my", None),
        P(None, "mx", "my", None),
        P("mx", "my", None),
        P("mx", "my", None),
        P(None, "mx", "my", None),
        P("mx", "my", None),
    )
    return jax.shard_map(
        shards,
        mesh=mesh,
        in_specs=placed,
        out_specs=(P(None, "mx", "my", None), P(None, "mx", "my", None)),
        check_vma=False,
    )
```

```python
import functools
import math

import jax
import jax.numpy as jnp
import numpy as np
from jax import lax
from jax.experimental import pallas as pl
from jax.experimental.pallas import tpu as pltpu
from jax.sharding import PartitionSpec as P

MESH = pl.DeviceIdType.MESH
SUB = 8
LEVELS = 3


gamma_gas = 5.0 / 3.0
courant = 0.3
gravity = 0.02
highest = lax.Precision.HIGHEST
multi_index = [
    (power_x, power_y, degree_sum - power_x - power_y)
    for degree_sum in range(4)
    for power_x in range(degree_sum, -1, -1)
    for power_y in range(degree_sum - power_x, -1, -1)
]


def factorial_of(exponent):
    return math.factorial(exponent[0]) * math.factorial(exponent[1]) * math.factorial(exponent[2])


def inverse_derivative(exponent, vectors):
    axes_list = [0] * exponent[0] + [1] * exponent[1] + [2] * exponent[2]
    radius = np.sqrt(np.sum(vectors * vectors, axis=1))
    radius_safe = np.where(radius > 0.0, radius, 1.0)
    degree = len(axes_list)
    if degree == 0:
        result = 1.0 / radius_safe
    elif degree == 1:
        result = -vectors[:, axes_list[0]] / radius_safe**3
    elif degree == 2:
        index_one, index_two = axes_list
        result = (
            3.0 * vectors[:, index_one] * vectors[:, index_two] / radius_safe**5
            - float(index_one == index_two) / radius_safe**3
        )
    else:
        index_one, index_two, index_three = axes_list
        crossed = (
            float(index_one == index_two) * vectors[:, index_three]
            + float(index_one == index_three) * vectors[:, index_two]
            + float(index_two == index_three) * vectors[:, index_one]
        )
        result = (
            -15.0
            * vectors[:, index_one]
            * vectors[:, index_two]
            * vectors[:, index_three]
            / radius_safe**7
            + 3.0 * crossed / radius_safe**5
        )
    return np.where(radius > 0.0, result, 0.0)


def offset_grid(reach_x, reach_y, reach_z):
    return [
        (shift_x, shift_y, shift_z)
        for shift_x in range(-reach_x, reach_x + 1)
        for shift_y in range(-reach_y, reach_y + 1)
        for shift_z in range(-reach_z, reach_z + 1)
    ]


def translation_kernel(spacing, offsets):
    vectors = np.asarray(offsets) * (-1.0 * spacing)
    entries = np.zeros((len(offsets), len(multi_index), len(multi_index)))
    for row_index, target_power in enumerate(multi_index):
        for column_index, source_power in enumerate(multi_index):
            if sum(target_power) + sum(source_power) <= 3:
                joined = (
                    target_power[0] + source_power[0],
                    target_power[1] + source_power[1],
                    target_power[2] + source_power[2],
                )
                entries[:, row_index, column_index] = (
                    -gravity
                    * (-1.0) ** sum(source_power)
                    / factorial_of(source_power)
                    * inverse_derivative(joined, vectors)
                )
    return entries.astype(np.float32)


def upward_matrices(spacing):
    entries = np.zeros((2, 2, 2, len(multi_index), len(multi_index)))
    for octant in range(8):
        octant_bits = (octant >> 2 & 1, octant >> 1 & 1, octant & 1)
        displacement = [(octant_bits[dimension] - 0.5) * spacing for dimension in range(3)]
        for row_index, target_power in enumerate(multi_index):
            for column_index, source_power in enumerate(multi_index):
                if all(
                    (source_power[dimension] <= target_power[dimension] for dimension in range(3))
                ):
                    entry_value = 1.0
                    for dimension in range(3):
                        entry_value *= math.comb(
                            target_power[dimension], source_power[dimension]
                        ) * displacement[dimension] ** (
                            target_power[dimension] - source_power[dimension]
                        )
                    entries[
                        octant_bits[0], octant_bits[1], octant_bits[2], row_index, column_index
                    ] = entry_value
    return entries.astype(np.float32)


def downward_matrices(spacing):
    entries = np.zeros((2, 2, 2, len(multi_index), len(multi_index)))
    for octant in range(8):
        octant_bits = (octant >> 2 & 1, octant >> 1 & 1, octant & 1)
        displacement = [(octant_bits[dimension] - 0.5) * spacing for dimension in range(3)]
        for row_index, target_power in enumerate(multi_index):
            for column_index, source_power in enumerate(multi_index):
                if all(
                    (source_power[dimension] >= target_power[dimension] for dimension in range(3))
                ):
                    entry_value = 1.0
                    for dimension in range(3):
                        lifted = source_power[dimension] - target_power[dimension]
                        entry_value *= displacement[dimension] ** lifted / math.factorial(lifted)
                    entries[
                        octant_bits[0], octant_bits[1], octant_bits[2], row_index, column_index
                    ] = entry_value
    return entries.astype(np.float32)


slot = 128
wide = 256
count_m = len(multi_index)
degrees = np.array([sum(exponent) for exponent in multi_index])
inner_columns = [
    (dx * 3 + dy) * 4 + bx * 2 + by
    for dx in range(3)
    for dy in range(3)
    for bx in range(2)
    for by in range(2)
    if 1 <= 2 * dx + bx <= 4 and 1 <= 2 * dy + by <= 4
]


early_names = (
    "flag_z", "cell_rows", "along_z", "spread_hi", "spread_lo", "pick_up_hi", "pick_up_lo",
    "second_hi", "second_lo", "one_rows", "two_rows",
)


def split_pair(table):
    table = jnp.asarray(table, jnp.float32)
    high = table.astype(jnp.bfloat16)
    return high, (table - high.astype(jnp.float32)).astype(jnp.bfloat16)


def window_tables():
    columns = [
        (2 * dx - 2 + bx, 2 * dy - 2 + by)
        for dx in range(3)
        for dy in range(3)
        for bx in range(2)
        for by in range(2)
    ]
    children = [(i >> 2 & 1, i >> 1 & 1, i & 1) for i in range(8)]
    sources = [(cx, cy, sz - 2) for cx, cy in columns for sz in range(6)]
    offsets = np.array([[[s[k] - t[k] for k in range(3)] for t in children] for s in sources])
    kernels = np.asarray(translation_kernel(1.0, offsets.reshape(-1, 3)), np.float64)
    kernels = kernels.reshape(36, 6, 8, count_m, count_m)
    touching = (np.abs(offsets).max(axis=2) <= 1).reshape(36, 6, 8, 1, 1)

    def laid(part):
        out = np.zeros((36, slot, 8, 32))
        out[:, : 6 * count_m, :, :count_m] = part.transpose(0, 1, 4, 2, 3).reshape(
            36, 6 * count_m, 8, count_m
        )
        return out.reshape(36, slot, wide)

    middle = laid(np.where(touching, 0.0, kernels))
    close = laid(np.where(touching, kernels, 0.0))[np.array(inner_columns)]
    return middle.reshape(-1, wide), close.reshape(-1, wide)


def moment_tables(cells_z):
    centres = (np.arange(SUB) + 0.5) / SUB - 0.5
    spread = np.zeros((2, 4, 2, SUB, 4, slot))
    along_z = np.zeros((cells_z, 4, slot))
    pick_up = np.zeros((4, slot, slot))
    lift = np.asarray(upward_matrices(1.0), np.float64)
    lift_two = np.asarray(upward_matrices(2.0), np.float64)
    second = np.zeros((4, slot, 2 * slot))
    for sd in range(6):
        for index, power in enumerate(multi_index):
            lane = sd * count_m + index
            for bx in range(2):
                for by in range(2):
                    spread[bx, power[0], by, :, bx * 2 + by, lane] = (
                        centres ** power[1] / SUB**3
                    )
            along_z[:, :, lane] = (np.tile(centres, cells_z // SUB) ** power[2])[:, None]
            for bx in range(2):
                for by in range(2):
                    for dz in range(2):
                        for lower in range(count_m):
                            pick_up[bx * 2 + by, (2 + dz) * count_m + lower, lane] = (
                                lift[bx, by, dz, index, lower] * 0.5 ** sum(power)
                            )
                            second[bx * 2 + by, lower, dz * slot + lane] = (
                                lift_two[bx, by, dz, index, lower]
                                * 2.0 ** degrees[lower]
                                * 0.25 ** sum(power)
                            )
    parents = cells_z // SUB // 2
    rows = np.arange(8)
    cell_rows = np.zeros((6, 8, cells_z))
    one_rows = np.zeros((6, 8, 8))
    two_rows = np.zeros((2, 6, 8, 8))
    for s in range(3):
        for dz in range(2):
            sd = s * 2 + dz
            for row in rows:
                cell_rows[sd, row] = np.arange(cells_z) // SUB == 2 * (row + s - 1) + dz
                if row < parents // 2:
                    one_rows[sd, row] = rows == 2 * (row + s - 1) + dz
                if 4 <= row < 4 + parents // 4:
                    second_z = 2 * (row - 4 + s - 1) + dz
                    if 0 <= second_z < parents // 2:
                        for dz_one in range(2):
                            two_rows[dz_one, sd, row] = rows == 2 * second_z + dz_one
    return (
        spread.reshape(128, 4 * slot),
        along_z.reshape(cells_z, 4 * slot),
        cell_rows.reshape(48, cells_z),
        pick_up.reshape(4 * slot, slot),
        one_rows.reshape(48, 8),
        second,
        two_rows.reshape(96, 8),
        (np.arange(cells_z)[None, :] // SUB == np.arange(cells_z // SUB)[:, None]).astype(float),
    )


def down_tables(cells_z):
    def stacked(spacing):
        down = np.asarray(downward_matrices(spacing), np.float64)
        out = np.zeros((2, 2, 2, 32, 2, 32))
        for bz in range(2):
            for child in range(2):
                out[:, :, bz, :count_m, child, :count_m] = down[:, :, child].transpose(0, 1, 3, 2)
        return out

    scale = np.zeros((16, 8, 32))
    scale[:8, :, :count_m] = 1.0
    scale[8:12, :, :count_m] = 0.5 ** (degrees + 1)
    scale[12:14, :, :count_m] = 0.25 ** (degrees + 1)
    near = stacked(1.0)
    near = near.transpose(2, 3, 0, 1, 4, 5).reshape(64, wide)
    rows = np.arange(8)
    take_one = (np.arange(16)[None, :] == 8 + rows[:, None]) & (rows[:, None] < 4)
    take_two = (np.arange(16)[None, :] == 12 + rows[:, None] // 2) & (rows[:, None] < 4)
    take_zero = np.arange(8)[None, :] == rows[:, None] // 2
    centres = (np.arange(SUB) + 0.5) / SUB - 0.5
    to_z = np.arange(cells_z)[None, :] // (2 * SUB) == rows[:, None]
    heights = np.tile(centres, cells_z // SUB)
    bz_of = np.arange(cells_z) // SUB % 2
    weights = np.zeros((2, 2, 2, 2, 32, cells_z))
    fields = np.zeros((3, 2, 3, 2, SUB, 2, 2, 2, 32))
    for index, power in enumerate(multi_index):
        for bz in range(2):
            weights[0, :, :, bz, index] = (bz_of == bz) * heights ** power[2]
            if power[2] > 0:
                weights[1, :, :, bz, index] = (bz_of == bz) * heights ** (power[2] - 1)
        for k in range(3):
            if power[k] > 0:
                lowered = list(power)
                lowered[k] -= 1
                for bx in range(2):
                    for by in range(2):
                        fields[k, bx, lowered[0], by, :, bx, by, :, index] = (
                            -power[k] / factorial_of(power) * centres ** lowered[1]
                        )[:, None]
    return (
        scale.reshape(16, wide),
        stacked(2.0).reshape(4, 64, 64),
        near,
        take_one.astype(float),
        take_two.astype(float),
        take_zero.astype(float),
        to_z.astype(float),
        weights.reshape(2, wide, cells_z),
        fields.reshape(3, 96, wide),
    )


def top_tables(nx, ny):
    lift = np.asarray(upward_matrices(4.0), np.float64)
    raise_up = np.zeros((4, slot, slot))
    lower_down = np.zeros((4, slot, 64))
    down = np.asarray(downward_matrices(4.0), np.float64)
    for bx in range(2):
        for by in range(2):
            for dz in range(2):
                raise_up[bx * 2 + by, (2 + dz) * count_m : (3 + dz) * count_m, :count_m] = (
                    lift[bx, by, dz] * 4.0 ** degrees[None, :]
                ).T
                lower_down[bx * 2 + by, :count_m, dz * 32 : dz * 32 + count_m] = down[bx, by, dz].T
    offsets = np.array(offset_grid(nx - 1, ny - 1, 1))
    kernels = np.asarray(translation_kernel(8.0, offsets), np.float64)
    counting = np.abs(offsets).max(axis=1) > 1
    far = np.zeros((len(offsets), slot, slot))
    far[:, :count_m, :count_m] = (kernels * counting[:, None, None]).transpose(0, 2, 1)
    return bool(counting.any()), raise_up, lower_down, far


def halves(value):
    high = value.astype(jnp.bfloat16)
    return high, (value - high.astype(jnp.float32)).astype(jnp.bfloat16)


def product(left, right):
    return jnp.dot(left, right, preferred_element_type=jnp.float32)


def times(value, table_hi, table_lo):
    high, low = halves(value)
    size = value.shape[0]
    both = product(jnp.concatenate([high, low], axis=0), table_hi)
    return both[:size] + both[size:] + product(high, table_lo)


def wholly(left, right):
    return jnp.dot(left, right, precision=highest, preferred_element_type=jnp.float32)


def picked(zero_one, value):
    high, low = halves(value)
    pick = zero_one.astype(jnp.bfloat16)
    return product(pick, high) + product(pick, low)


def sound(entropy, inverse):
    pressure = (gamma_gas - 1.0) * jnp.exp(gamma_gas * jnp.log(entropy))
    return pressure, jnp.sqrt(gamma_gas * pressure * inverse)


def states_of(stencil):
    a, b, c, d, e, f = stencil
    interface = (37.0 / 60.0) * (c + d) - (8.0 / 60.0) * (b + e) + (1.0 / 60.0) * (a + f)
    low, high = jnp.minimum(c, d), jnp.maximum(c, d)
    left = jnp.minimum(jnp.maximum(interface, jnp.minimum(b, low)), jnp.maximum(b, high))
    right = jnp.minimum(jnp.maximum(interface, jnp.minimum(e, low)), jnp.maximum(e, high))
    return left, right


def prepare(stencil_of, direction):
    mass = states_of(stencil_of(0))
    push = states_of(stencil_of(1 + direction))
    heat = states_of(stencil_of(5))
    inverse = [1.0 / value for value in mass]
    speed = [push[i] * inverse[i] for i in range(2)]
    gas = [sound(heat[i], inverse[i]) for i in range(2)]
    fastest = jnp.maximum(jnp.abs(speed[0]) + gas[0][1], jnp.abs(speed[1]) + gas[1][1])
    weights = 0.5 * (speed[0] + fastest), 0.5 * (speed[1] - fastest)
    flux = [left * weights[0] + right * weights[1] for left, right in (mass, push, heat)]
    flux[1] = flux[1] + 0.5 * (gas[0][0] + gas[1][0])
    work = 0.5 * (gas[0][0] * speed[0] + gas[1][0] * speed[1])
    return (*flux, *weights, work)


def apply(prepared, stencil_of, direction, count_fields, emit):
    known = dict(zip((0, 1 + direction, 5), prepared[:3]))
    for field in range(count_fields):
        if field in known:
            emit(field, known[field])
            continue
        left, right = states_of(stencil_of(field))
        flux = left * prepared[3] + right * prepared[4]
        emit(field, flux + prepared[5] if field == 4 else flux)


def section_kernel(
    sizes, top, names, density, momentum, energy, entropy, tracers, flags, *rest
):
    held_tables = dict(zip(names, rest[: len(names)]))
    section, accel = rest[len(names) : len(names) + 2]
    table = dict(zip(names, rest[len(names) + 2 : 2 * len(names) + 2]))
    (
        ext_x, ext_y, moved, previous, packed, packed_flux, tiles, near, window, rows_p, splits,
        load_sem, table_sem, halo_send, halo_recv, first_send, first_recv,
        second_send, second_recv, side_send, side_recv,
    ) = rest[2 * len(names) + 2 :]
    count_x, count_y, nf, cx, cy, cz = sizes
    mx, my = lax.axis_index("mx"), lax.axis_index("my")
    loads = [
        pltpu.make_async_copy(source, ext_x.at[pl.ds(begin, size), pl.ds(3, cx)], load_sem.at[i])
        for i, (source, begin, size) in enumerate(
            [(density, 0, 1), (momentum, 1, 3), (energy, 4, 1), (entropy, 5, 1), (tracers, 6, nf - 6)]
        )
    ]
    px, py = lax.rem(mx, 2), lax.rem(my, 2)
    tables = {}
    for i, name in enumerate(names):
        source = held_tables[name]
        if name.startswith("second"):
            source = source.at[px * 2 + py]
        tables[name] = pltpu.make_async_copy(source, table[name], table_sem.at[i])
    for copy in loads:
        copy.start()
    for copy in tables.values():
        copy.start()

    def at_x(step):
        return (lax.rem(mx + step + count_x, count_x), my)

    def at_y(step):
        return (mx, lax.rem(my + step + count_y, count_y))

    barrier = pltpu.get_barrier_semaphore()
    for step in range(1, count_x):
        pl.semaphore_signal(barrier, inc=1, device_id=at_x(step), device_id_type=MESH)
    for step in range(1, count_y):
        pl.semaphore_signal(barrier, inc=1, device_id=at_y(step), device_id_type=MESH)
    for copy in loads:
        copy.wait()

    def remote(source, target, send, recv, device):
        return pltpu.make_async_remote_copy(
            src_ref=source, dst_ref=target, send_sem=send, recv_sem=recv,
            device_id=device, device_id_type=MESH,
        )

    def halo_pair(buffer, length, base, place):
        lower = remote(
            buffer.at[:, pl.ds(3, 3)], buffer.at[:, pl.ds(length + 3, 3)],
            halo_send.at[base], halo_recv.at[base], place(-1),
        )
        upper = remote(
            buffer.at[:, pl.ds(length, 3)], buffer.at[:, pl.ds(0, 3)],
            halo_send.at[base + 1], halo_recv.at[base + 1], place(1),
        )
        return lower, upper

    def start_halo(pair, position, count):
        @pl.when(position > 0)
        def _():
            pair[0].start()

        @pl.when(position < count - 1)
        def _():
            pair[1].start()

    def finish_halo(pair, buffer, length, position, count):
        @pl.when(position > 0)
        def _():
            pair[0].wait_send()
            pair[1].wait_recv()

        @pl.when(position < count - 1)
        def _():
            pair[1].wait_send()
            pair[0].wait_recv()

        @pl.when(position == 0)
        def _():
            for row in range(3):
                buffer[:, row] = buffer[:, 3]

        @pl.when(position == count - 1)
        def _():
            for row in range(3):
                buffer[:, length + 3 + row] = buffer[:, length + 2]

    pair_x = halo_pair(ext_x, cx, 0, at_x)
    pair_y = halo_pair(ext_y, cy, 2, at_y)

    def turn(field, carry):
        for row in range(cy):
            ext_y[field, 3 + row] = ext_x[field, pl.ds(3, cx), row, :]
        return carry

    lax.fori_loop(0, nf, turn, 0)
    pl.semaphore_wait(barrier, count_x + count_y - 2)
    start_halo(pair_y, my, count_y)
    start_halo(pair_x, mx, count_x)

    planes = 4

    def cell_speed(step, best):
        rows = pl.ds(3 + step * planes, planes)
        inverse = 1.0 / ext_x[0, rows]
        largest = jnp.maximum(
            jnp.maximum(jnp.abs(ext_x[1, rows]), jnp.abs(ext_x[2, rows])), jnp.abs(ext_x[3, rows])
        )
        _, speed = sound(ext_x[5, rows], inverse)
        return jnp.maximum(best, jnp.max(largest * inverse + speed, axis=0))

    best = lax.fori_loop(0, cx // planes, cell_speed, jnp.zeros((cy, cz), jnp.float32))
    best = jnp.max(best)

    for name in early_names:
        tables[name].wait()
    flagged = product(
        jnp.concatenate(
            [
                jnp.broadcast_to(
                    flags[bx, by : by + 1, :].astype(jnp.float32), (SUB, flags.shape[2])
                )
                for bx in range(2)
                for by in range(2)
            ],
            axis=0,
        ).astype(jnp.bfloat16),
        table["flag_z"][...].astype(jnp.bfloat16),
    )
    for bx in range(2):
        rows = [ext_x[0, 3 + bx * SUB + i] for i in range(SUB)]
        for power in range(4):
            total = rows[0] * ((0.5 / SUB - 0.5) ** power)
            for i in range(1, SUB):
                total = total + rows[i] * (((i + 0.5) / SUB - 0.5) ** power)
            rows_p[pl.ds((bx * 4 + power) * 2 * SUB, 2 * SUB), :] = (
                total * flagged[bx * 2 * SUB : (bx + 1) * 2 * SUB]
            )
    weighted = times(rows_p[...].T, table["spread_hi"][...], table["spread_lo"][...])
    shifted = picked(table["cell_rows"][...], weighted * table["along_z"][...])

    def choose(stack, lanes):
        lane = lax.rem(lax.broadcasted_iota(jnp.int32, (8, lanes), 1), slot)
        total = jnp.zeros((8, lanes), jnp.float32)
        for sd in range(6):
            inside = (lane >= sd * count_m) & (lane < (sd + 1) * count_m)
            total = total + jnp.where(inside, stack[sd * 8 : sd * 8 + 8], 0.0)
        return total

    block = choose(shifted, 4 * slot)
    near[1, 1] = block
    first = times(block, table["pick_up_hi"][...], table["pick_up_lo"][...])
    tile = choose(picked(table["one_rows"][...], first), slot)
    lifted = times(first, table["second_hi"][...], table["second_lo"][...])
    for dz in range(2):
        part = picked(
            table["two_rows"][dz * 48 : dz * 48 + 48], lifted[:, dz * slot : (dz + 1) * slot]
        )
        tile = tile + choose(part, slot)
    row_index = lax.broadcasted_iota(jnp.int32, (8, slot), 0)
    tiles[mx, my] = jnp.where(row_index == 7, best, tile)

    for step in range(1, count_y):
        remote(
            tiles.at[mx, my], tiles.at[mx, my],
            first_send.at[step], first_recv.at[step], at_y(step),
        ).start()
    side_y = (
        remote(near.at[1, 1], near.at[1, 2], side_send.at[0], side_recv.at[0], at_y(-1)),
        remote(near.at[1, 1], near.at[1, 0], side_send.at[1], side_recv.at[1], at_y(1)),
    )
    start_halo(side_y, my, count_y)

    lane_z = lax.broadcasted_iota(jnp.int32, (cy, cz), 1)

    def pack(row, carry):
        mine = (lane_z >= row * 8) & (lane_z < row * 8 + 8)
        for field in range(nf):
            turned = pltpu.roll(ext_x[field, 3 + row], row * 8 + 3, 1)
            packed[field] = jnp.where(mine, turned, packed[field])
        return carry

    packed[...] = jnp.ones(packed.shape, jnp.float32)
    lax.fori_loop(0, cx, pack, 0)

    def end_stencil(field):
        value = packed[field]
        one = pltpu.roll(value, cz - 1, 1)
        two = pltpu.roll(value, cz - 2, 1)
        return value, one, two, two, two, two

    def end_emit(field, flux):
        packed_flux[field] = flux

    apply(prepare(end_stencil, 2), end_stencil, 2, nf, end_emit)

    def stencil_z(row):
        def stencil(field):
            value = ext_x[field, 3 + row]
            out = [value]
            for step in range(3):
                out.insert(0, jnp.where(lane_z < 1, value, pltpu.roll(out[0], 1, 1)))
            for step in range(2):
                out.append(jnp.where(lane_z == cz - 1, value, pltpu.roll(out[-1], cz - 1, 1)))
            return out

        return stencil

    def sweep_z(row, prepared):
        following = prepare(stencil_z(jnp.minimum(row + 1, cx - 1)), 2)

        def emit(field, flux):
            ending = pltpu.roll(packed_flux[field], cz - 1 - row * 8, 1)
            above = jnp.where(lane_z == cz - 1, ending, pltpu.roll(flux, cz - 1, 1))
            section[field, row] = above - flux

        apply(prepared, stencil_z(row), 2, nf, emit)
        return following

    half_way = lax.fori_loop(0, cx // 2, sweep_z, prepare(stencil_z(0), 2))

    for step in range(1, count_y):
        arrived = tiles.at[mx, lax.rem(my - step + count_y, count_y)]
        copy = remote(arrived, arrived, first_send.at[step], first_recv.at[step], at_y(step))
        copy.wait_send()
        copy.wait_recv()

    def finish_side(pair, position, count, low, high):
        @pl.when(position > 0)
        def _():
            pair[0].wait_send()
            pair[1].wait_recv()

        @pl.when(position < count - 1)
        def _():
            pair[1].wait_send()
            pair[0].wait_recv()

        @pl.when(position == 0)
        def _():
            low[...] = jnp.zeros(low.shape, jnp.float32)

        @pl.when(position == count - 1)
        def _():
            high[...] = jnp.zeros(high.shape, jnp.float32)

    finish_side(side_y, my, count_y, near.at[1, 0], near.at[1, 2])
    for step in range(1, count_x):
        remote(
            tiles.at[mx], tiles.at[mx], second_send.at[step], second_recv.at[step], at_x(step)
        ).start()
    side_x = (
        remote(near.at[1], near.at[2], side_send.at[2], side_recv.at[2], at_x(-1)),
        remote(near.at[1], near.at[0], side_send.at[3], side_recv.at[3], at_x(1)),
    )
    start_halo(side_x, mx, count_x)

    lax.fori_loop(cx // 2, cx, sweep_z, half_way)

    def sweep(buffer, length, direction, store, beside=None, total=(), parts=0):
        def stencil_at(face):
            return lambda field: [buffer[field, face + i] for i in range(6)]

        def start_emit(field, flux):
            previous[field] = flux

        apply(prepare(stencil_at(0), direction), stencil_at(0), direction, nf, start_emit)

        def body(cell, carry):
            prepared, total = carry
            following = prepare(stencil_at(jnp.minimum(cell + 2, length)), direction)

            def emit(field, flux):
                store(field, cell, flux - previous[field])
                previous[field] = flux

            apply(prepared, stencil_at(cell + 1), direction, nf, emit)
            return following, total

        def fuller(cell, carry):
            prepared, total = body(cell, carry)
            for part in range(2):
                total = beside(cell * 2 + part, total)
            return prepared, total

        carry = prepare(stencil_at(1), direction), total
        if parts > 0:
            carry = lax.fori_loop(0, parts // 2, fuller, carry)
        return lax.fori_loop(parts // 2, length, body, carry)[1]

    for step in range(1, count_x):
        arrived = tiles.at[lax.rem(mx - step + count_x, count_x)]
        copy = remote(arrived, arrived, second_send.at[step], second_recv.at[step], at_x(step))
        copy.wait_send()
        copy.wait_recv()
    finish_side(side_x, mx, count_x, near.at[0], near.at[2])

    fastest = jnp.max(jnp.max(tiles[...], axis=(0, 1))[7:8, :])
    step_size = courant / (SUB * jnp.full((1, cz), fastest, jnp.float32))

    one_x, one_y = mx // 2, my // 2
    two_x, two_y = mx // 4, my // 4

    def united(ux, uy):
        return (
            tiles[2 * ux, 2 * uy] + tiles[2 * ux, 2 * uy + 1]
            + tiles[2 * ux + 1, 2 * uy] + tiles[2 * ux + 1, 2 * uy + 1]
        )

    def held(value, count):
        return jnp.clip(value, 0, count - 1), (value >= 0) & (value < count)

    for dx in range(3):
        for dy in range(3):
            base = (dx * 3 + dy) * 4 * slot
            window[0:8, base : base + 4 * slot] = near[dx, dy]
            for bx in range(2):
                for by in range(2):
                    at = base + (bx * 2 + by) * slot
                    gx, in_x = held(2 * (one_x + dx - 1) + bx, count_x)
                    gy, in_y = held(2 * (one_y + dy - 1) + by, count_y)
                    ux, in_ux = held(2 * (two_x + dx - 1) + bx, count_x // 2)
                    uy, in_uy = held(2 * (two_y + dy - 1) + by, count_y // 2)
                    own = jnp.where(in_x & in_y, tiles[gx, gy], 0.0)
                    joint = jnp.where(in_ux & in_uy, united(ux, uy), 0.0)
                    window[8:16, at : at + slot] = jnp.where(
                        row_index < 4, own, jnp.where(row_index < 6, joint, 0.0)
                    )

    for name in names:
        if name not in early_names:
            tables[name].wait()

    keep = (lax.broadcasted_iota(jnp.int32, (16, wide), 0) < 8).astype(jnp.float32)
    middle_chunks = 36 * slot // wide
    chunks = middle_chunks + len(inner_columns) * slot // wide
    for index in range(chunks):
        if index < middle_chunks:
            value = window[:, index * wide : (index + 1) * wide]
        else:
            pair = inner_columns[2 * (index - middle_chunks) :][:2]
            value = keep * jnp.concatenate(
                [window[:, column * slot : (column + 1) * slot] for column in pair], axis=1
            )
        high, low = halves(value)
        splits[index, 0:16] = high
        splits[index, 16:32] = low

    finish_halo(pair_y, ext_y, cy, my, count_y)

    def store_y(field, cell, value):
        moved[field, cell] = value

    def partial_sum(index, total):
        both = splits[index]
        return (
            total[0] + product(both, table["window_hi"][index]),
            total[1] + product(both[:16], table["window_lo"][index]),
        )

    zeros = jnp.zeros((32, wide), jnp.float32), jnp.zeros((16, wide), jnp.float32)
    upper, lower = sweep(ext_y, cy, 1, store_y, partial_sum, zeros, chunks)
    sums = (upper[:16] + upper[16:] + lower) * table["scale"][...]


    def select(values, which):
        total = jnp.zeros((values.shape[0], 64), jnp.float32)
        for child in range(4):
            total = total + jnp.where(which == child, values[:, child * 64 : child * 64 + 64], 0.0)
        return total

    lane_64 = lax.broadcasted_iota(jnp.int32, (8, 64), 1)
    same_half = (lane_64 >= 32) == (lax.rem(lax.broadcasted_iota(jnp.int32, (8, 64), 0), 2) == 1)
    which_two = lax.rem(one_x, 2) * 2 + lax.rem(one_y, 2)
    second_sum = select(sums, which_two)
    if top:
        nx3, ny3 = count_x // 4, count_y // 4
        grown = jnp.zeros((8, slot), jnp.float32)
        for sx in range(nx3):
            for sy in range(ny3):
                source = jnp.zeros((8, slot), jnp.float32)
                for bx in range(2):
                    for by in range(2):
                        source = source + wholly(
                            united(2 * sx + bx, 2 * sy + by), table["raise_up"][bx * 2 + by]
                        )
                source = jnp.where((row_index == 4) | (row_index == 5), source, 0.0)
                place = ((sx - two_x + nx3 - 1) * (2 * ny3 - 1) + (sy - two_y + ny3 - 1)) * 3
                for dz in range(3):
                    moved_rows = source if dz == 1 else pltpu.roll(source, 1 if dz == 0 else 7, 0)
                    grown = grown + wholly(moved_rows, table["far"][place + dz])
        grown = jnp.where((row_index == 4) | (row_index == 5), grown, 0.0)
        carried = wholly(grown, table["lower_down"][which_two])
        second_sum = second_sum + jnp.concatenate([jnp.zeros((8, 64), jnp.float32), carried], axis=0)
    from_two = jnp.where(same_half, picked(table["take_two"][...], second_sum), 0.0)
    which_one = px * 2 + py
    first_sum = picked(table["take_one"][...], select(sums, which_one)) + times(
        from_two, table["down_two_hi"][which_one], table["down_two_lo"][which_one]
    )
    from_one = jnp.where(same_half, picked(table["take_zero"][...], first_sum), 0.0)
    expansion = sums[0:8] + times(from_one, table["down_one_hi"][...], table["down_one_lo"][...])
    turned_hi, turned_lo = halves(expansion.T)
    to_z = table["to_z"][...].astype(jnp.bfloat16)
    on_z = product(turned_hi, to_z) + product(turned_lo, to_z)
    pieces = []
    for which, first_row, last_row in ((0, 0, 192), (1, 192, 288)):
        high, low = halves(on_z * table["weights"][which])
        field_hi = table["fields_hi"][first_row:last_row]
        piece = product(field_hi, high) + product(field_hi, low)
        pieces.append(piece + product(table["fields_lo"][first_row:last_row], high))
    for k in range(3):
        parts = pieces[0][k * 96 : k * 96 + 96] if k < 2 else pieces[1]
        for row in range(cx):
            bx, height = row // SUB, (row % SUB + 0.5) / SUB - 0.5
            base = bx * 6 * SUB
            accel[k, row] = (
                parts[base : base + 2 * SUB]
                + height * parts[base + 2 * SUB : base + 4 * SUB]
                + (height * height) * parts[base + 4 * SUB : base + 6 * SUB]
            )

    finish_halo(pair_x, ext_x, cx, mx, count_x)

    def store_x(field, cell, value):
        total = (value + section[field, cell] + moved[field, :, cell, :]) * (-float(SUB))
        if 1 <= field <= 3:
            total = total + ext_x[0, 3 + cell] * accel[field - 1, cell]
        if field == 4:
            for k in range(3):
                total = total + ext_x[1 + k, 3 + cell] * accel[k, cell]
        section[field, cell] = ext_x[field, 3 + cell] + step_size * total

    sweep(ext_x, cx, 0, store_x)


def shards(density, momentum, energy, entropy, tracers, leaf_flags):
    count_x, count_y = lax.axis_size("mx"), lax.axis_size("my")
    cx, cy, cz = density.shape
    nf = 6 + tracers.shape[0]
    middle, close = window_tables()
    top, raise_up, lower_down, far = top_tables(count_x // 4, count_y // 4)
    spread, along_z, cell_rows, pick_up, one_rows, second, two_rows, flag_z = moment_tables(cz)
    scale, down_two, down_one, take_one, take_two, take_zero, to_z, weights, fields = down_tables(cz)
    constants = {}
    for name, array in (("flag_z", flag_z), ("cell_rows", cell_rows), ("along_z", along_z)):
        constants[name] = jnp.asarray(array, jnp.float32)
    for name, array in (("spread", spread), ("pick_up", pick_up), ("second", second)):
        constants[name + "_hi"], constants[name + "_lo"] = split_pair(array)
    for name, array in (("one_rows", one_rows), ("two_rows", two_rows)):
        constants[name] = jnp.asarray(array, jnp.float32)
    joined = np.concatenate([middle, close]).reshape(-1, wide, wide)
    for name, array in (
        ("window", joined), ("down_two", down_two), ("down_one", down_one),
        ("fields", fields.reshape(-1, wide)),
    ):
        constants[name + "_hi"], constants[name + "_lo"] = split_pair(array)
    for name, array in (
        ("scale", scale), ("take_one", take_one), ("take_two", take_two),
        ("take_zero", take_zero), ("to_z", to_z), ("weights", weights),
    ):
        constants[name] = jnp.asarray(array, jnp.float32)
    if top:
        for name, array in (("raise_up", raise_up), ("lower_down", lower_down), ("far", far)):
            constants[name] = jnp.asarray(array, jnp.float32)
    names = tuple(constants)
    shapes = [
        pltpu.VMEM(
            array.shape[1:] if name.startswith("second") else array.shape, array.dtype
        )
        for name, array in constants.items()
    ]
    anywhere = pl.BlockSpec(memory_space=pl.ANY)
    local = pl.BlockSpec(memory_space=pltpu.VMEM)
    dma = pltpu.SemaphoreType.DMA
    f32 = jnp.float32
    return pl.pallas_call(
        functools.partial(section_kernel, (count_x, count_y, nf, cx, cy, cz), top, names),
        out_shape=(
            jax.ShapeDtypeStruct((nf, cx, cy, cz), f32),
            jax.ShapeDtypeStruct((3, cx, cy, cz), f32),
        ),
        in_specs=[anywhere] * 5 + [local] + [anywhere] * len(names),
        out_specs=(local, local),
        scratch_shapes=shapes
        + [
            pltpu.VMEM((nf, cx + 6, cy, cz), f32),
            pltpu.VMEM((nf, cy + 6, cx, cz), f32),
            pltpu.VMEM((nf, cy, cx, cz), f32),
            pltpu.VMEM((nf, cy, cz), f32),
            pltpu.VMEM((nf, cy, cz), f32),
            pltpu.VMEM((nf, cy, cz), f32),
            pltpu.VMEM((count_x, count_y, 8, slot), f32),
            pltpu.VMEM((3, 3, 8, 4 * slot), f32),
            pltpu.VMEM((16, 36 * slot), f32),
            pltpu.VMEM((128, cz), f32),
            pltpu.VMEM((joined.shape[0], 32, wide), jnp.bfloat16),
            dma((5,)), dma((len(names),)), dma((4,)), dma((4,)),
            dma((count_y,)), dma((count_y,)), dma((count_x,)), dma((count_x,)),
            dma((4,)), dma((4,)),
        ],
        compiler_params=pltpu.CompilerParams(
            collective_id=0, has_side_effects=True, vmem_limit_bytes=56 * 1024 * 1024
        ),
    )(density[None], momentum, energy[None], entropy[None], tracers, leaf_flags, *constants.values())


def solution(mesh):
    placed = (
        P("mx", "my", None),
        P(None, "mx", "my", None),
        P("mx", "my", None),
        P("mx", "my", None),
        P(None, "mx", "my", None),
        P("mx", "my", None),
    )
    return jax.shard_map(
        shards,
        mesh=mesh,
        in_specs=placed,
        out_specs=(P(None, "mx", "my", None), P(None, "mx", "my", None)),
        check_vma=False,
    )
```

```python
import functools
import math

import jax
import jax.numpy as jnp
import numpy as np
from jax import lax
from jax.experimental import pallas as pl
from jax.experimental.pallas import tpu as pltpu
from jax.sharding import PartitionSpec as P

MESH = pl.DeviceIdType.MESH
SUB = 8
LEVELS = 3


gamma_gas = 5.0 / 3.0
courant = 0.3
gravity = 0.02
highest = lax.Precision.HIGHEST
multi_index = [
    (power_x, power_y, degree_sum - power_x - power_y)
    for degree_sum in range(4)
    for power_x in range(degree_sum, -1, -1)
    for power_y in range(degree_sum - power_x, -1, -1)
]


def factorial_of(exponent):
    return math.factorial(exponent[0]) * math.factorial(exponent[1]) * math.factorial(exponent[2])


def inverse_derivative(exponent, vectors):
    axes_list = [0] * exponent[0] + [1] * exponent[1] + [2] * exponent[2]
    radius = np.sqrt(np.sum(vectors * vectors, axis=1))
    radius_safe = np.where(radius > 0.0, radius, 1.0)
    degree = len(axes_list)
    if degree == 0:
        result = 1.0 / radius_safe
    elif degree == 1:
        result = -vectors[:, axes_list[0]] / radius_safe**3
    elif degree == 2:
        index_one, index_two = axes_list
        result = (
            3.0 * vectors[:, index_one] * vectors[:, index_two] / radius_safe**5
            - float(index_one == index_two) / radius_safe**3
        )
    else:
        index_one, index_two, index_three = axes_list
        crossed = (
            float(index_one == index_two) * vectors[:, index_three]
            + float(index_one == index_three) * vectors[:, index_two]
            + float(index_two == index_three) * vectors[:, index_one]
        )
        result = (
            -15.0
            * vectors[:, index_one]
            * vectors[:, index_two]
            * vectors[:, index_three]
            / radius_safe**7
            + 3.0 * crossed / radius_safe**5
        )
    return np.where(radius > 0.0, result, 0.0)


def offset_grid(reach_x, reach_y, reach_z):
    return [
        (shift_x, shift_y, shift_z)
        for shift_x in range(-reach_x, reach_x + 1)
        for shift_y in range(-reach_y, reach_y + 1)
        for shift_z in range(-reach_z, reach_z + 1)
    ]


def translation_kernel(spacing, offsets):
    vectors = np.asarray(offsets) * (-1.0 * spacing)
    entries = np.zeros((len(offsets), len(multi_index), len(multi_index)))
    for row_index, target_power in enumerate(multi_index):
        for column_index, source_power in enumerate(multi_index):
            if sum(target_power) + sum(source_power) <= 3:
                joined = (
                    target_power[0] + source_power[0],
                    target_power[1] + source_power[1],
                    target_power[2] + source_power[2],
                )
                entries[:, row_index, column_index] = (
                    -gravity
                    * (-1.0) ** sum(source_power)
                    / factorial_of(source_power)
                    * inverse_derivative(joined, vectors)
                )
    return entries.astype(np.float32)


def upward_matrices(spacing):
    entries = np.zeros((2, 2, 2, len(multi_index), len(multi_index)))
    for octant in range(8):
        octant_bits = (octant >> 2 & 1, octant >> 1 & 1, octant & 1)
        displacement = [(octant_bits[dimension] - 0.5) * spacing for dimension in range(3)]
        for row_index, target_power in enumerate(multi_index):
            for column_index, source_power in enumerate(multi_index):
                if all(
                    (source_power[dimension] <= target_power[dimension] for dimension in range(3))
                ):
                    entry_value = 1.0
                    for dimension in range(3):
                        entry_value *= math.comb(
                            target_power[dimension], source_power[dimension]
                        ) * displacement[dimension] ** (
                            target_power[dimension] - source_power[dimension]
                        )
                    entries[
                        octant_bits[0], octant_bits[1], octant_bits[2], row_index, column_index
                    ] = entry_value
    return entries.astype(np.float32)


def downward_matrices(spacing):
    entries = np.zeros((2, 2, 2, len(multi_index), len(multi_index)))
    for octant in range(8):
        octant_bits = (octant >> 2 & 1, octant >> 1 & 1, octant & 1)
        displacement = [(octant_bits[dimension] - 0.5) * spacing for dimension in range(3)]
        for row_index, target_power in enumerate(multi_index):
            for column_index, source_power in enumerate(multi_index):
                if all(
                    (source_power[dimension] >= target_power[dimension] for dimension in range(3))
                ):
                    entry_value = 1.0
                    for dimension in range(3):
                        lifted = source_power[dimension] - target_power[dimension]
                        entry_value *= displacement[dimension] ** lifted / math.factorial(lifted)
                    entries[
                        octant_bits[0], octant_bits[1], octant_bits[2], row_index, column_index
                    ] = entry_value
    return entries.astype(np.float32)


slot = 128
wide = 256
count_m = len(multi_index)
degrees = np.array([sum(exponent) for exponent in multi_index])
inner_columns = [
    (dx * 3 + dy) * 4 + bx * 2 + by
    for dx in range(3)
    for dy in range(3)
    for bx in range(2)
    for by in range(2)
    if 1 <= 2 * dx + bx <= 4 and 1 <= 2 * dy + by <= 4
]


early_names = (
    "flag_z", "cell_rows", "along_z", "spread_hi", "spread_lo", "pick_up_hi", "pick_up_lo",
    "second_hi", "second_lo", "one_rows", "two_rows",
)


def split_pair(table):
    table = np.asarray(table, np.float32)
    high = table.astype(jnp.bfloat16)
    low = (table - high.astype(np.float32)).astype(jnp.bfloat16)
    return [("_hi", high)] + ([("_lo", low)] if np.any(low.astype(np.float32)) else [])


def window_tables():
    columns = [
        (2 * dx - 2 + bx, 2 * dy - 2 + by)
        for dx in range(3)
        for dy in range(3)
        for bx in range(2)
        for by in range(2)
    ]
    children = [(i >> 2 & 1, i >> 1 & 1, i & 1) for i in range(8)]
    sources = [(cx, cy, sz - 2) for cx, cy in columns for sz in range(6)]
    offsets = np.array([[[s[k] - t[k] for k in range(3)] for t in children] for s in sources])
    kernels = np.asarray(translation_kernel(1.0, offsets.reshape(-1, 3)), np.float64)
    kernels = kernels.reshape(36, 6, 8, count_m, count_m)
    touching = (np.abs(offsets).max(axis=2) <= 1).reshape(36, 6, 8, 1, 1)

    def laid(part):
        out = np.zeros((36, slot, 8, 32))
        out[:, : 6 * count_m, :, :count_m] = part.transpose(0, 1, 4, 2, 3).reshape(
            36, 6 * count_m, 8, count_m
        )
        return out.reshape(36, slot, wide)

    middle = laid(np.where(touching, 0.0, kernels))
    close = laid(np.where(touching, kernels, 0.0))[np.array(inner_columns)]
    return middle.reshape(-1, wide), close.reshape(-1, wide)


def moment_tables(cells_z):
    centres = (np.arange(SUB) + 0.5) / SUB - 0.5
    spread = np.zeros((2, 4, 2, SUB, 4, slot))
    along_z = np.zeros((cells_z, 4, slot))
    pick_up = np.zeros((4, slot, slot))
    lift = np.asarray(upward_matrices(1.0), np.float64)
    lift_two = np.asarray(upward_matrices(2.0), np.float64)
    second = np.zeros((4, slot, 2 * slot))
    for sd in range(6):
        for index, power in enumerate(multi_index):
            lane = sd * count_m + index
            for bx in range(2):
                for by in range(2):
                    spread[bx, power[0], by, :, bx * 2 + by, lane] = (
                        centres ** power[1] / SUB**3
                    )
            along_z[:, :, lane] = (np.tile(centres, cells_z // SUB) ** power[2])[:, None]
            for bx in range(2):
                for by in range(2):
                    for dz in range(2):
                        for lower in range(count_m):
                            pick_up[bx * 2 + by, (2 + dz) * count_m + lower, lane] = (
                                lift[bx, by, dz, index, lower] * 0.5 ** sum(power)
                            )
                            second[bx * 2 + by, lower, dz * slot + lane] = (
                                lift_two[bx, by, dz, index, lower]
                                * 2.0 ** degrees[lower]
                                * 0.25 ** sum(power)
                            )
    parents = cells_z // SUB // 2
    rows = np.arange(8)
    cell_rows = np.zeros((6, 8, cells_z))
    one_rows = np.zeros((6, 8, 8))
    two_rows = np.zeros((2, 6, 8, 8))
    for s in range(3):
        for dz in range(2):
            sd = s * 2 + dz
            for row in rows:
                cell_rows[sd, row] = np.arange(cells_z) // SUB == 2 * (row + s - 1) + dz
                if row < parents // 2:
                    one_rows[sd, row] = rows == 2 * (row + s - 1) + dz
                if 4 <= row < 4 + parents // 4:
                    second_z = 2 * (row - 4 + s - 1) + dz
                    if 0 <= second_z < parents // 2:
                        for dz_one in range(2):
                            two_rows[dz_one, sd, row] = rows == 2 * second_z + dz_one
    return (
        spread.reshape(128, 4 * slot),
        along_z.reshape(cells_z, 4 * slot),
        cell_rows.reshape(48, cells_z),
        pick_up.reshape(4 * slot, slot),
        one_rows.reshape(48, 8),
        second,
        two_rows.reshape(96, 8),
        (np.arange(cells_z)[None, :] // SUB == np.arange(cells_z // SUB)[:, None]).astype(float),
    )


def down_tables(cells_z):
    def stacked(spacing):
        down = np.asarray(downward_matrices(spacing), np.float64)
        out = np.zeros((2, 2, 2, 32, 2, 32))
        for bz in range(2):
            for child in range(2):
                out[:, :, bz, :count_m, child, :count_m] = down[:, :, child].transpose(0, 1, 3, 2)
        return out

    scale = np.zeros((16, 8, 32))
    scale[:8, :, :count_m] = 1.0
    scale[8:12, :, :count_m] = 0.5 ** (degrees + 1)
    scale[12:14, :, :count_m] = 0.25 ** (degrees + 1)
    near = stacked(1.0)
    near = near.transpose(2, 3, 0, 1, 4, 5).reshape(64, wide)
    rows = np.arange(8)
    take_one = (np.arange(16)[None, :] == 8 + rows[:, None]) & (rows[:, None] < 4)
    take_two = (np.arange(16)[None, :] == 12 + rows[:, None] // 2) & (rows[:, None] < 4)
    take_zero = np.arange(8)[None, :] == rows[:, None] // 2
    centres = (np.arange(SUB) + 0.5) / SUB - 0.5
    to_z = np.arange(cells_z)[None, :] // (2 * SUB) == rows[:, None]
    heights = np.tile(centres, cells_z // SUB)
    bz_of = np.arange(cells_z) // SUB % 2
    weights = np.zeros((2, 2, 2, 2, 32, cells_z))
    fields = np.zeros((3, 2, 3, 2, SUB, 2, 2, 2, 32))
    for index, power in enumerate(multi_index):
        for bz in range(2):
            weights[0, :, :, bz, index] = (bz_of == bz) * heights ** power[2]
            if power[2] > 0:
                weights[1, :, :, bz, index] = (bz_of == bz) * heights ** (power[2] - 1)
        for k in range(3):
            if power[k] > 0:
                lowered = list(power)
                lowered[k] -= 1
                for bx in range(2):
                    for by in range(2):
                        fields[k, bx, lowered[0], by, :, bx, by, :, index] = (
                            -power[k] / factorial_of(power) * centres ** lowered[1]
                        )[:, None]
    return (
        scale.reshape(16, wide),
        stacked(2.0).reshape(4, 64, 64),
        near,
        take_one.astype(float),
        take_two.astype(float),
        take_zero.astype(float),
        to_z.astype(float),
        weights.reshape(2, wide, cells_z),
        fields.reshape(3, 96, wide),
    )


def top_tables(nx, ny):
    lift = np.asarray(upward_matrices(4.0), np.float64)
    raise_up = np.zeros((4, slot, slot))
    lower_down = np.zeros((4, slot, 64))
    down = np.asarray(downward_matrices(4.0), np.float64)
    for bx in range(2):
        for by in range(2):
            for dz in range(2):
                raise_up[bx * 2 + by, (2 + dz) * count_m : (3 + dz) * count_m, :count_m] = (
                    lift[bx, by, dz] * 4.0 ** degrees[None, :]
                ).T
                lower_down[bx * 2 + by, :count_m, dz * 32 : dz * 32 + count_m] = down[bx, by, dz].T
    offsets = np.array(offset_grid(nx - 1, ny - 1, 1))
    kernels = np.asarray(translation_kernel(8.0, offsets), np.float64)
    counting = np.abs(offsets).max(axis=1) > 1
    far = np.zeros((len(offsets), slot, slot))
    far[:, :count_m, :count_m] = (kernels * counting[:, None, None]).transpose(0, 2, 1)
    return bool(counting.any()), raise_up, lower_down, far


def halves(value):
    high = value.astype(jnp.bfloat16)
    return high, (value - high.astype(jnp.float32)).astype(jnp.bfloat16)


def product(left, right):
    return jnp.dot(left, right, preferred_element_type=jnp.float32)


def times(value, table_hi, table_lo):
    high, low = halves(value)
    size = value.shape[0]
    both = product(jnp.concatenate([high, low], axis=0), table_hi)
    both = both[:size] + both[size:]
    return both if table_lo is None else both + product(high, table_lo)


def wholly(left, right):
    return jnp.dot(left, right, precision=highest, preferred_element_type=jnp.float32)


def picked(zero_one, value):
    high, low = halves(value)
    pick = zero_one.astype(jnp.bfloat16)
    return product(pick, high) + product(pick, low)


def sound(entropy, inverse):
    pressure = (gamma_gas - 1.0) * jnp.exp(gamma_gas * jnp.log(entropy))
    return pressure, jnp.sqrt(gamma_gas * pressure * inverse)


def states_of(stencil):
    a, b, c, d, e, f = stencil
    interface = (37.0 / 60.0) * (c + d) - (8.0 / 60.0) * (b + e) + (1.0 / 60.0) * (a + f)
    low, high = jnp.minimum(c, d), jnp.maximum(c, d)
    left = jnp.minimum(jnp.maximum(interface, jnp.minimum(b, low)), jnp.maximum(b, high))
    right = jnp.minimum(jnp.maximum(interface, jnp.minimum(e, low)), jnp.maximum(e, high))
    return left, right


def prepare(stencil_of, direction):
    mass = states_of(stencil_of(0))
    push = states_of(stencil_of(1 + direction))
    heat = states_of(stencil_of(5))
    inverse = [1.0 / value for value in mass]
    speed = [push[i] * inverse[i] for i in range(2)]
    gas = [sound(heat[i], inverse[i]) for i in range(2)]
    fastest = jnp.maximum(jnp.abs(speed[0]) + gas[0][1], jnp.abs(speed[1]) + gas[1][1])
    weights = 0.5 * (speed[0] + fastest), 0.5 * (speed[1] - fastest)
    flux = [left * weights[0] + right * weights[1] for left, right in (mass, push, heat)]
    flux[1] = flux[1] + 0.5 * (gas[0][0] + gas[1][0])
    work = 0.5 * (gas[0][0] * speed[0] + gas[1][0] * speed[1])
    return (*flux, *weights, work)


def apply(prepared, stencil_of, direction, count_fields, emit):
    known = dict(zip((0, 1 + direction, 5), prepared[:3]))
    for field in range(count_fields):
        if field in known:
            emit(field, known[field])
            continue
        left, right = states_of(stencil_of(field))
        flux = left * prepared[3] + right * prepared[4]
        emit(field, flux + prepared[5] if field == 4 else flux)


def section_kernel(
    sizes, top, names, density, momentum, energy, entropy, tracers, flags, *rest
):
    held_tables = dict(zip(names, rest[: len(names)]))
    section, accel = rest[len(names) : len(names) + 2]
    table = dict(zip(names, rest[len(names) + 2 : 2 * len(names) + 2]))
    (
        ext_x, ext_y, moved, previous, packed, packed_flux, tiles, near, window, rows_p, splits,
        load_sem, table_sem, halo_send, halo_recv, first_send, first_recv,
        second_send, second_recv, side_send, side_recv,
    ) = rest[2 * len(names) + 2 :]
    count_x, count_y, nf, cx, cy, cz = sizes
    mx, my = lax.axis_index("mx"), lax.axis_index("my")
    loads = [
        pltpu.make_async_copy(source, ext_x.at[pl.ds(begin, size), pl.ds(3, cx)], load_sem.at[i])
        for i, (source, begin, size) in enumerate(
            [(density, 0, 1), (momentum, 1, 3), (energy, 4, 1), (entropy, 5, 1), (tracers, 6, nf - 6)]
        )
    ]
    px, py = lax.rem(mx, 2), lax.rem(my, 2)
    tables = {}
    for i, name in enumerate(names):
        source = held_tables[name]
        if name.startswith("second"):
            source = source.at[px * 2 + py]
        tables[name] = pltpu.make_async_copy(source, table[name], table_sem.at[i])
    for copy in loads:
        copy.start()
    for copy in tables.values():
        copy.start()

    def at_x(step):
        return (lax.rem(mx + step + count_x, count_x), my)

    def at_y(step):
        return (mx, lax.rem(my + step + count_y, count_y))

    barrier = pltpu.get_barrier_semaphore()
    for step in range(1, count_x):
        pl.semaphore_signal(barrier, inc=1, device_id=at_x(step), device_id_type=MESH)
    for step in range(1, count_y):
        pl.semaphore_signal(barrier, inc=1, device_id=at_y(step), device_id_type=MESH)
    for copy in loads:
        copy.wait()

    def remote(source, target, send, recv, device):
        return pltpu.make_async_remote_copy(
            src_ref=source, dst_ref=target, send_sem=send, recv_sem=recv,
            device_id=device, device_id_type=MESH,
        )

    def halo_pair(buffer, length, base, place):
        lower = remote(
            buffer.at[:, pl.ds(3, 3)], buffer.at[:, pl.ds(length + 3, 3)],
            halo_send.at[base], halo_recv.at[base], place(-1),
        )
        upper = remote(
            buffer.at[:, pl.ds(length, 3)], buffer.at[:, pl.ds(0, 3)],
            halo_send.at[base + 1], halo_recv.at[base + 1], place(1),
        )
        return lower, upper

    def start_halo(pair, position, count):
        @pl.when(position > 0)
        def _():
            pair[0].start()

        @pl.when(position < count - 1)
        def _():
            pair[1].start()

    def finish_halo(pair, buffer, length, position, count):
        @pl.when(position > 0)
        def _():
            pair[0].wait_send()
            pair[1].wait_recv()

        @pl.when(position < count - 1)
        def _():
            pair[1].wait_send()
            pair[0].wait_recv()

        @pl.when(position == 0)
        def _():
            for row in range(3):
                buffer[:, row] = buffer[:, 3]

        @pl.when(position == count - 1)
        def _():
            for row in range(3):
                buffer[:, length + 3 + row] = buffer[:, length + 2]

    pair_x = halo_pair(ext_x, cx, 0, at_x)
    pair_y = halo_pair(ext_y, cy, 2, at_y)

    def turn(field, carry):
        for row in range(cy):
            ext_y[field, 3 + row] = ext_x[field, pl.ds(3, cx), row, :]
        return carry

    lax.fori_loop(0, nf, turn, 0)
    pl.semaphore_wait(barrier, count_x + count_y - 2)
    start_halo(pair_y, my, count_y)
    start_halo(pair_x, mx, count_x)

    planes = 4

    def cell_speed(step, best):
        rows = pl.ds(3 + step * planes, planes)
        inverse = 1.0 / ext_x[0, rows]
        largest = jnp.maximum(
            jnp.maximum(jnp.abs(ext_x[1, rows]), jnp.abs(ext_x[2, rows])), jnp.abs(ext_x[3, rows])
        )
        _, speed = sound(ext_x[5, rows], inverse)
        return jnp.maximum(best, jnp.max(largest * inverse + speed, axis=0))

    best = lax.fori_loop(0, cx // planes, cell_speed, jnp.zeros((cy, cz), jnp.float32))
    best = jnp.max(best)

    for name in names:
        if name in early_names:
            tables[name].wait()

    def pair_of(name, *at):
        low = name + "_lo"
        return [table[name + "_hi"][(*at, ...)], table[low][(*at, ...)] if low in names else None]

    flagged = product(
        jnp.concatenate(
            [
                jnp.broadcast_to(
                    flags[bx, by : by + 1, :].astype(jnp.float32), (SUB, flags.shape[2])
                )
                for bx in range(2)
                for by in range(2)
            ],
            axis=0,
        ).astype(jnp.bfloat16),
        table["flag_z"][...].astype(jnp.bfloat16),
    )
    for bx in range(2):
        rows = [ext_x[0, 3 + bx * SUB + i] for i in range(SUB)]
        for power in range(4):
            total = rows[0] * ((0.5 / SUB - 0.5) ** power)
            for i in range(1, SUB):
                total = total + rows[i] * (((i + 0.5) / SUB - 0.5) ** power)
            rows_p[pl.ds((bx * 4 + power) * 2 * SUB, 2 * SUB), :] = (
                total * flagged[bx * 2 * SUB : (bx + 1) * 2 * SUB]
            )
    weighted = times(rows_p[...].T, *pair_of("spread"))
    shifted = picked(table["cell_rows"][...], weighted * table["along_z"][...])

    def choose(stack, lanes):
        lane = lax.rem(lax.broadcasted_iota(jnp.int32, (8, lanes), 1), slot)
        total = jnp.zeros((8, lanes), jnp.float32)
        for sd in range(6):
            inside = (lane >= sd * count_m) & (lane < (sd + 1) * count_m)
            total = total + jnp.where(inside, stack[sd * 8 : sd * 8 + 8], 0.0)
        return total

    block = choose(shifted, 4 * slot)
    near[1, 1] = block
    first = times(block, *pair_of("pick_up"))
    tile = choose(picked(table["one_rows"][...], first), slot)
    lifted = times(first, *pair_of("second"))
    for dz in range(2):
        part = picked(
            table["two_rows"][dz * 48 : dz * 48 + 48], lifted[:, dz * slot : (dz + 1) * slot]
        )
        tile = tile + choose(part, slot)
    row_index = lax.broadcasted_iota(jnp.int32, (8, slot), 0)
    tiles[mx, my] = jnp.where(row_index == 7, best, tile)

    for step in range(1, count_y):
        remote(
            tiles.at[mx, my], tiles.at[mx, my],
            first_send.at[step], first_recv.at[step], at_y(step),
        ).start()
    side_y = (
        remote(near.at[1, 1], near.at[1, 2], side_send.at[0], side_recv.at[0], at_y(-1)),
        remote(near.at[1, 1], near.at[1, 0], side_send.at[1], side_recv.at[1], at_y(1)),
    )
    start_halo(side_y, my, count_y)

    lane_z = lax.broadcasted_iota(jnp.int32, (cy, cz), 1)

    def pack(row, carry):
        mine = (lane_z >= row * 8) & (lane_z < row * 8 + 8)
        for field in range(nf):
            turned = pltpu.roll(ext_x[field, 3 + row], row * 8 + 3, 1)
            packed[field] = jnp.where(mine, turned, packed[field])
        return carry

    packed[...] = jnp.ones(packed.shape, jnp.float32)
    lax.fori_loop(0, cx, pack, 0)

    def end_stencil(field):
        value = packed[field]
        one = pltpu.roll(value, cz - 1, 1)
        two = pltpu.roll(value, cz - 2, 1)
        return value, one, two, two, two, two

    def end_emit(field, flux):
        packed_flux[field] = flux

    apply(prepare(end_stencil, 2), end_stencil, 2, nf, end_emit)

    def stencil_z(row):
        def stencil(field):
            value = ext_x[field, 3 + row]
            out = [value]
            for step in range(3):
                out.insert(0, jnp.where(lane_z < 1, value, pltpu.roll(out[0], 1, 1)))
            for step in range(2):
                out.append(jnp.where(lane_z == cz - 1, value, pltpu.roll(out[-1], cz - 1, 1)))
            return out

        return stencil

    def sweep_z(row, prepared):
        following = prepare(stencil_z(jnp.minimum(row + 1, cx - 1)), 2)

        def emit(field, flux):
            ending = pltpu.roll(packed_flux[field], cz - 1 - row * 8, 1)
            above = jnp.where(lane_z == cz - 1, ending, pltpu.roll(flux, cz - 1, 1))
            section[field, row] = above - flux

        apply(prepared, stencil_z(row), 2, nf, emit)
        return following

    half_way = lax.fori_loop(0, cx // 2, sweep_z, prepare(stencil_z(0), 2))

    for step in range(1, count_y):
        arrived = tiles.at[mx, lax.rem(my - step + count_y, count_y)]
        copy = remote(arrived, arrived, first_send.at[step], first_recv.at[step], at_y(step))
        copy.wait_send()
        copy.wait_recv()

    def finish_side(pair, position, count, low, high):
        @pl.when(position > 0)
        def _():
            pair[0].wait_send()
            pair[1].wait_recv()

        @pl.when(position < count - 1)
        def _():
            pair[1].wait_send()
            pair[0].wait_recv()

        @pl.when(position == 0)
        def _():
            low[...] = jnp.zeros(low.shape, jnp.float32)

        @pl.when(position == count - 1)
        def _():
            high[...] = jnp.zeros(high.shape, jnp.float32)

    finish_side(side_y, my, count_y, near.at[1, 0], near.at[1, 2])
    for step in range(1, count_x):
        remote(
            tiles.at[mx], tiles.at[mx], second_send.at[step], second_recv.at[step], at_x(step)
        ).start()
    side_x = (
        remote(near.at[1], near.at[2], side_send.at[2], side_recv.at[2], at_x(-1)),
        remote(near.at[1], near.at[0], side_send.at[3], side_recv.at[3], at_x(1)),
    )
    start_halo(side_x, mx, count_x)

    lax.fori_loop(cx // 2, cx, sweep_z, half_way)

    def sweep(buffer, length, direction, store):
        def stencil_at(face):
            return lambda field: [buffer[field, face + i] for i in range(6)]

        def start_emit(field, flux):
            previous[field] = flux

        apply(prepare(stencil_at(0), direction), stencil_at(0), direction, nf, start_emit)

        def body(cell, prepared):
            following = prepare(stencil_at(jnp.minimum(cell + 2, length)), direction)

            def emit(field, flux):
                store(field, cell, flux - previous[field])
                previous[field] = flux

            apply(prepared, stencil_at(cell + 1), direction, nf, emit)
            return following

        lax.fori_loop(0, length, body, prepare(stencil_at(1), direction))

    finish_halo(pair_y, ext_y, cy, my, count_y)

    def store_y(field, cell, value):
        moved[field, cell] = value

    sweep(ext_y, cy, 1, store_y)

    for step in range(1, count_x):
        arrived = tiles.at[lax.rem(mx - step + count_x, count_x)]
        copy = remote(arrived, arrived, second_send.at[step], second_recv.at[step], at_x(step))
        copy.wait_send()
        copy.wait_recv()
    finish_side(side_x, mx, count_x, near.at[0], near.at[2])

    fastest = jnp.max(jnp.max(tiles[...], axis=(0, 1))[7:8, :])
    step_size = courant / (SUB * jnp.full((1, cz), fastest, jnp.float32))

    one_x, one_y = mx // 2, my // 2
    two_x, two_y = mx // 4, my // 4

    def united(ux, uy):
        return (
            tiles[2 * ux, 2 * uy] + tiles[2 * ux, 2 * uy + 1]
            + tiles[2 * ux + 1, 2 * uy] + tiles[2 * ux + 1, 2 * uy + 1]
        )

    def held(value, count):
        return jnp.clip(value, 0, count - 1), (value >= 0) & (value < count)

    for dx in range(3):
        for dy in range(3):
            base = (dx * 3 + dy) * 4 * slot
            window[0:8, base : base + 4 * slot] = near[dx, dy]
            for bx in range(2):
                for by in range(2):
                    at = base + (bx * 2 + by) * slot
                    gx, in_x = held(2 * (one_x + dx - 1) + bx, count_x)
                    gy, in_y = held(2 * (one_y + dy - 1) + by, count_y)
                    ux, in_ux = held(2 * (two_x + dx - 1) + bx, count_x // 2)
                    uy, in_uy = held(2 * (two_y + dy - 1) + by, count_y // 2)
                    own = jnp.where(in_x & in_y, tiles[gx, gy], 0.0)
                    joint = jnp.where(in_ux & in_uy, united(ux, uy), 0.0)
                    window[8:16, at : at + slot] = jnp.where(
                        row_index < 4, own, jnp.where(row_index < 6, joint, 0.0)
                    )

    for name in names:
        if name not in early_names:
            tables[name].wait()

    keep = (lax.broadcasted_iota(jnp.int32, (16, wide), 0) < 8).astype(jnp.float32)
    middle_chunks = 36 * slot // wide
    chunks = middle_chunks + len(inner_columns) * slot // wide
    for index in range(chunks):
        if index < middle_chunks:
            value = window[:, index * wide : (index + 1) * wide]
        else:
            pair = inner_columns[2 * (index - middle_chunks) :][:2]
            value = keep * jnp.concatenate(
                [window[:, column * slot : (column + 1) * slot] for column in pair], axis=1
            )
        high, low = halves(value)
        splits[index, 0:16] = high
        splits[index, 16:32] = low

    upper = jnp.zeros((32, wide), jnp.float32)
    lower = jnp.zeros((16, wide), jnp.float32)
    for index in range(chunks):
        both = splits[index]
        upper = upper + product(both, table["window_hi"][index])
        lower = lower + product(both[:16], table["window_lo"][index])
    sums = (upper[:16] + upper[16:] + lower) * table["scale"][...]


    def select(values, which):
        total = jnp.zeros((values.shape[0], 64), jnp.float32)
        for child in range(4):
            total = total + jnp.where(which == child, values[:, child * 64 : child * 64 + 64], 0.0)
        return total

    lane_64 = lax.broadcasted_iota(jnp.int32, (8, 64), 1)
    same_half = (lane_64 >= 32) == (lax.rem(lax.broadcasted_iota(jnp.int32, (8, 64), 0), 2) == 1)
    which_two = lax.rem(one_x, 2) * 2 + lax.rem(one_y, 2)
    second_sum = select(sums, which_two)
    if top:
        nx3, ny3 = count_x // 4, count_y // 4
        grown = jnp.zeros((8, slot), jnp.float32)
        for sx in range(nx3):
            for sy in range(ny3):
                source = jnp.zeros((8, slot), jnp.float32)
                for bx in range(2):
                    for by in range(2):
                        source = source + wholly(
                            united(2 * sx + bx, 2 * sy + by), table["raise_up"][bx * 2 + by]
                        )
                source = jnp.where((row_index == 4) | (row_index == 5), source, 0.0)
                place = ((sx - two_x + nx3 - 1) * (2 * ny3 - 1) + (sy - two_y + ny3 - 1)) * 3
                for dz in range(3):
                    moved_rows = source if dz == 1 else pltpu.roll(source, 1 if dz == 0 else 7, 0)
                    grown = grown + wholly(moved_rows, table["far"][place + dz])
        grown = jnp.where((row_index == 4) | (row_index == 5), grown, 0.0)
        carried = wholly(grown, table["lower_down"][which_two])
        second_sum = second_sum + jnp.concatenate([jnp.zeros((8, 64), jnp.float32), carried], axis=0)
    from_two = jnp.where(same_half, picked(table["take_two"][...], second_sum), 0.0)
    which_one = px * 2 + py
    first_sum = picked(table["take_one"][...], select(sums, which_one)) + times(
        from_two, *pair_of("down_two", which_one)
    )
    from_one = jnp.where(same_half, picked(table["take_zero"][...], first_sum), 0.0)
    expansion = sums[0:8] + times(from_one, *pair_of("down_one"))
    turned_hi, turned_lo = halves(expansion.T)
    to_z = table["to_z"][...].astype(jnp.bfloat16)
    on_z = product(turned_hi, to_z) + product(turned_lo, to_z)
    pieces = []
    for which, first_row, last_row in ((0, 0, 192), (1, 192, 288)):
        high, low = halves(on_z * table["weights"][which])
        field_hi = table["fields_hi"][first_row:last_row]
        piece = product(field_hi, high) + product(field_hi, low)
        if "fields_lo" in names:
            piece = piece + product(table["fields_lo"][first_row:last_row], high)
        pieces.append(piece)
    for k in range(3):
        parts = pieces[0][k * 96 : k * 96 + 96] if k < 2 else pieces[1]
        for row in range(cx):
            bx, height = row // SUB, (row % SUB + 0.5) / SUB - 0.5
            base = bx * 6 * SUB
            accel[k, row] = (
                parts[base : base + 2 * SUB]
                + height * parts[base + 2 * SUB : base + 4 * SUB]
                + (height * height) * parts[base + 4 * SUB : base + 6 * SUB]
            )

    finish_halo(pair_x, ext_x, cx, mx, count_x)

    def store_x(field, cell, value):
        total = (value + section[field, cell] + moved[field, :, cell, :]) * (-float(SUB))
        if 1 <= field <= 3:
            total = total + ext_x[0, 3 + cell] * accel[field - 1, cell]
        if field == 4:
            for k in range(3):
                total = total + ext_x[1 + k, 3 + cell] * accel[k, cell]
        section[field, cell] = ext_x[field, 3 + cell] + step_size * total

    sweep(ext_x, cx, 0, store_x)


def shards(density, momentum, energy, entropy, tracers, leaf_flags):
    count_x, count_y = lax.axis_size("mx"), lax.axis_size("my")
    cx, cy, cz = density.shape
    nf = 6 + tracers.shape[0]
    middle, close = window_tables()
    top, raise_up, lower_down, far = top_tables(count_x // 4, count_y // 4)
    spread, along_z, cell_rows, pick_up, one_rows, second, two_rows, flag_z = moment_tables(cz)
    scale, down_two, down_one, take_one, take_two, take_zero, to_z, weights, fields = down_tables(cz)
    constants = {}
    for name, array in (("flag_z", flag_z), ("cell_rows", cell_rows), ("along_z", along_z)):
        constants[name] = jnp.asarray(array, jnp.float32)
    for name, array in (("spread", spread), ("pick_up", pick_up), ("second", second)):
        for ending, part in split_pair(array):
            constants[name + ending] = jnp.asarray(part)
    for name, array in (("one_rows", one_rows), ("two_rows", two_rows)):
        constants[name] = jnp.asarray(array, jnp.float32)
    joined = np.concatenate([middle, close]).reshape(-1, wide, wide)
    for name, array in (
        ("window", joined), ("down_two", down_two), ("down_one", down_one),
        ("fields", fields.reshape(-1, wide)),
    ):
        for ending, part in split_pair(array):
            constants[name + ending] = jnp.asarray(part)
    for name, array in (
        ("scale", scale), ("take_one", take_one), ("take_two", take_two),
        ("take_zero", take_zero), ("to_z", to_z), ("weights", weights),
    ):
        constants[name] = jnp.asarray(array, jnp.float32)
    if top:
        for name, array in (("raise_up", raise_up), ("lower_down", lower_down), ("far", far)):
            constants[name] = jnp.asarray(array, jnp.float32)
    names = tuple(constants)
    shapes = [
        pltpu.VMEM(
            array.shape[1:] if name.startswith("second") else array.shape, array.dtype
        )
        for name, array in constants.items()
    ]
    anywhere = pl.BlockSpec(memory_space=pl.ANY)
    local = pl.BlockSpec(memory_space=pltpu.VMEM)
    dma = pltpu.SemaphoreType.DMA
    f32 = jnp.float32
    return pl.pallas_call(
        functools.partial(section_kernel, (count_x, count_y, nf, cx, cy, cz), top, names),
        out_shape=(
            jax.ShapeDtypeStruct((nf, cx, cy, cz), f32),
            jax.ShapeDtypeStruct((3, cx, cy, cz), f32),
        ),
        in_specs=[anywhere] * 5 + [local] + [anywhere] * len(names),
        out_specs=(local, local),
        scratch_shapes=shapes
        + [
            pltpu.VMEM((nf, cx + 6, cy, cz), f32),
            pltpu.VMEM((nf, cy + 6, cx, cz), f32),
            pltpu.VMEM((nf, cy, cx, cz), f32),
            pltpu.VMEM((nf, cy, cz), f32),
            pltpu.VMEM((nf, cy, cz), f32),
            pltpu.VMEM((nf, cy, cz), f32),
            pltpu.VMEM((count_x, count_y, 8, slot), f32),
            pltpu.VMEM((3, 3, 8, 4 * slot), f32),
            pltpu.VMEM((16, 36 * slot), f32),
            pltpu.VMEM((128, cz), f32),
            pltpu.VMEM((joined.shape[0], 32, wide), jnp.bfloat16),
            dma((5,)), dma((len(names),)), dma((4,)), dma((4,)),
            dma((count_y,)), dma((count_y,)), dma((count_x,)), dma((count_x,)),
            dma((4,)), dma((4,)),
        ],
        compiler_params=pltpu.CompilerParams(
            collective_id=0, has_side_effects=True, vmem_limit_bytes=56 * 1024 * 1024
        ),
    )(density[None], momentum, energy[None], entropy[None], tracers, leaf_flags, *constants.values())


def solution(mesh):
    placed = (
        P("mx", "my", None),
        P(None, "mx", "my", None),
        P("mx", "my", None),
        P("mx", "my", None),
        P(None, "mx", "my", None),
        P("mx", "my", None),
    )
    return jax.shard_map(
        shards,
        mesh=mesh,
        in_specs=placed,
        out_specs=(P(None, "mx", "my", None), P(None, "mx", "my", None)),
        check_vma=False,
    )
```

```python
import functools
import math

import jax
import jax.numpy as jnp
import numpy as np
from jax import lax
from jax.experimental import pallas as pl
from jax.experimental.pallas import tpu as pltpu
from jax.sharding import PartitionSpec as P

MESH = pl.DeviceIdType.MESH
SUB = 8
LEVELS = 3


gamma_gas = 5.0 / 3.0
courant = 0.3
gravity = 0.02
highest = lax.Precision.HIGHEST
multi_index = [
    (power_x, power_y, degree_sum - power_x - power_y)
    for degree_sum in range(4)
    for power_x in range(degree_sum, -1, -1)
    for power_y in range(degree_sum - power_x, -1, -1)
]


def factorial_of(exponent):
    return math.factorial(exponent[0]) * math.factorial(exponent[1]) * math.factorial(exponent[2])


def inverse_derivative(exponent, vectors):
    axes_list = [0] * exponent[0] + [1] * exponent[1] + [2] * exponent[2]
    radius = np.sqrt(np.sum(vectors * vectors, axis=1))
    radius_safe = np.where(radius > 0.0, radius, 1.0)
    degree = len(axes_list)
    if degree == 0:
        result = 1.0 / radius_safe
    elif degree == 1:
        result = -vectors[:, axes_list[0]] / radius_safe**3
    elif degree == 2:
        index_one, index_two = axes_list
        result = (
            3.0 * vectors[:, index_one] * vectors[:, index_two] / radius_safe**5
            - float(index_one == index_two) / radius_safe**3
        )
    else:
        index_one, index_two, index_three = axes_list
        crossed = (
            float(index_one == index_two) * vectors[:, index_three]
            + float(index_one == index_three) * vectors[:, index_two]
            + float(index_two == index_three) * vectors[:, index_one]
        )
        result = (
            -15.0
            * vectors[:, index_one]
            * vectors[:, index_two]
            * vectors[:, index_three]
            / radius_safe**7
            + 3.0 * crossed / radius_safe**5
        )
    return np.where(radius > 0.0, result, 0.0)


def offset_grid(reach_x, reach_y, reach_z):
    return [
        (shift_x, shift_y, shift_z)
        for shift_x in range(-reach_x, reach_x + 1)
        for shift_y in range(-reach_y, reach_y + 1)
        for shift_z in range(-reach_z, reach_z + 1)
    ]


def translation_kernel(spacing, offsets):
    vectors = np.asarray(offsets) * (-1.0 * spacing)
    entries = np.zeros((len(offsets), len(multi_index), len(multi_index)))
    for row_index, target_power in enumerate(multi_index):
        for column_index, source_power in enumerate(multi_index):
            if sum(target_power) + sum(source_power) <= 3:
                joined = (
                    target_power[0] + source_power[0],
                    target_power[1] + source_power[1],
                    target_power[2] + source_power[2],
                )
                entries[:, row_index, column_index] = (
                    -gravity
                    * (-1.0) ** sum(source_power)
                    / factorial_of(source_power)
                    * inverse_derivative(joined, vectors)
                )
    return entries.astype(np.float32)


def upward_matrices(spacing):
    entries = np.zeros((2, 2, 2, len(multi_index), len(multi_index)))
    for octant in range(8):
        octant_bits = (octant >> 2 & 1, octant >> 1 & 1, octant & 1)
        displacement = [(octant_bits[dimension] - 0.5) * spacing for dimension in range(3)]
        for row_index, target_power in enumerate(multi_index):
            for column_index, source_power in enumerate(multi_index):
                if all(
                    (source_power[dimension] <= target_power[dimension] for dimension in range(3))
                ):
                    entry_value = 1.0
                    for dimension in range(3):
                        entry_value *= math.comb(
                            target_power[dimension], source_power[dimension]
                        ) * displacement[dimension] ** (
                            target_power[dimension] - source_power[dimension]
                        )
                    entries[
                        octant_bits[0], octant_bits[1], octant_bits[2], row_index, column_index
                    ] = entry_value
    return entries.astype(np.float32)


def downward_matrices(spacing):
    entries = np.zeros((2, 2, 2, len(multi_index), len(multi_index)))
    for octant in range(8):
        octant_bits = (octant >> 2 & 1, octant >> 1 & 1, octant & 1)
        displacement = [(octant_bits[dimension] - 0.5) * spacing for dimension in range(3)]
        for row_index, target_power in enumerate(multi_index):
            for column_index, source_power in enumerate(multi_index):
                if all(
                    (source_power[dimension] >= target_power[dimension] for dimension in range(3))
                ):
                    entry_value = 1.0
                    for dimension in range(3):
                        lifted = source_power[dimension] - target_power[dimension]
                        entry_value *= displacement[dimension] ** lifted / math.factorial(lifted)
                    entries[
                        octant_bits[0], octant_bits[1], octant_bits[2], row_index, column_index
                    ] = entry_value
    return entries.astype(np.float32)


slot = 128
wide = 256
count_m = len(multi_index)
degrees = np.array([sum(exponent) for exponent in multi_index])
inner_columns = [
    (dx * 3 + dy) * 4 + bx * 2 + by
    for dx in range(3)
    for dy in range(3)
    for bx in range(2)
    for by in range(2)
    if 1 <= 2 * dx + bx <= 4 and 1 <= 2 * dy + by <= 4
]


early_names = (
    "flag_z", "cell_rows", "along_z", "spread_hi", "spread_lo", "pick_up_hi", "pick_up_lo",
    "second_hi", "second_lo", "one_rows", "two_rows",
)


def split_pair(table):
    table = np.asarray(table, np.float32)
    high = table.astype(jnp.bfloat16)
    low = (table - high.astype(np.float32)).astype(jnp.bfloat16)
    return [("_hi", high)] + ([("_lo", low)] if np.any(low.astype(np.float32)) else [])


def window_tables():
    columns = [
        (2 * dx - 2 + bx, 2 * dy - 2 + by)
        for dx in range(3)
        for dy in range(3)
        for bx in range(2)
        for by in range(2)
    ]
    children = [(i >> 2 & 1, i >> 1 & 1, i & 1) for i in range(8)]
    sources = [(cx, cy, sz - 2) for cx, cy in columns for sz in range(6)]
    offsets = np.array([[[s[k] - t[k] for k in range(3)] for t in children] for s in sources])
    kernels = np.asarray(translation_kernel(1.0, offsets.reshape(-1, 3)), np.float64)
    kernels = kernels.reshape(36, 6, 8, count_m, count_m)
    touching = (np.abs(offsets).max(axis=2) <= 1).reshape(36, 6, 8, 1, 1)

    def laid(part):
        out = np.zeros((36, slot, 8, 32))
        out[:, : 6 * count_m, :, :count_m] = part.transpose(0, 1, 4, 2, 3).reshape(
            36, 6 * count_m, 8, count_m
        )
        return out.reshape(36, slot, wide)

    middle = laid(np.where(touching, 0.0, kernels))
    close = laid(np.where(touching, kernels, 0.0))[np.array(inner_columns)]
    return middle.reshape(-1, wide), close.reshape(-1, wide)


def moment_tables(cells_z):
    centres = (np.arange(SUB) + 0.5) / SUB - 0.5
    spread = np.zeros((2, 4, 2, SUB, 4, slot))
    along_z = np.zeros((cells_z, 4, slot))
    pick_up = np.zeros((4, slot, slot))
    lift = np.asarray(upward_matrices(1.0), np.float64)
    lift_two = np.asarray(upward_matrices(2.0), np.float64)
    second = np.zeros((4, slot, 2 * slot))
    for sd in range(6):
        for index, power in enumerate(multi_index):
            lane = sd * count_m + index
            for bx in range(2):
                for by in range(2):
                    spread[bx, power[0], by, :, bx * 2 + by, lane] = (
                        centres ** power[1] / SUB**3
                    )
            along_z[:, :, lane] = (np.tile(centres, cells_z // SUB) ** power[2])[:, None]
            for bx in range(2):
                for by in range(2):
                    for dz in range(2):
                        for lower in range(count_m):
                            pick_up[bx * 2 + by, (2 + dz) * count_m + lower, lane] = (
                                lift[bx, by, dz, index, lower] * 0.5 ** sum(power)
                            )
                            second[bx * 2 + by, lower, dz * slot + lane] = (
                                lift_two[bx, by, dz, index, lower]
                                * 2.0 ** degrees[lower]
                                * 0.25 ** sum(power)
                            )
    parents = cells_z // SUB // 2
    rows = np.arange(8)
    cell_rows = np.zeros((6, 8, cells_z))
    one_rows = np.zeros((6, 8, 8))
    two_rows = np.zeros((2, 6, 8, 8))
    for s in range(3):
        for dz in range(2):
            sd = s * 2 + dz
            for row in rows:
                cell_rows[sd, row] = np.arange(cells_z) // SUB == 2 * (row + s - 1) + dz
                if row < parents // 2:
                    one_rows[sd, row] = rows == 2 * (row + s - 1) + dz
                if 4 <= row < 4 + parents // 4:
                    second_z = 2 * (row - 4 + s - 1) + dz
                    if 0 <= second_z < parents // 2:
                        for dz_one in range(2):
                            two_rows[dz_one, sd, row] = rows == 2 * second_z + dz_one
    return (
        spread.reshape(128, 4 * slot),
        along_z.reshape(cells_z, 4 * slot),
        cell_rows.reshape(48, cells_z),
        pick_up.reshape(4 * slot, slot),
        one_rows.reshape(48, 8),
        second,
        two_rows.reshape(96, 8),
        (np.arange(cells_z)[None, :] // SUB == np.arange(cells_z // SUB)[:, None]).astype(float),
    )


def down_tables(cells_z):
    def stacked(spacing):
        down = np.asarray(downward_matrices(spacing), np.float64)
        out = np.zeros((2, 2, 2, 32, 2, 32))
        for bz in range(2):
            for child in range(2):
                out[:, :, bz, :count_m, child, :count_m] = down[:, :, child].transpose(0, 1, 3, 2)
        return out

    scale = np.zeros((16, 8, 32))
    scale[:8, :, :count_m] = 1.0
    scale[8:12, :, :count_m] = 0.5 ** (degrees + 1)
    scale[12:14, :, :count_m] = 0.25 ** (degrees + 1)
    near = stacked(1.0)
    near = near.transpose(2, 3, 0, 1, 4, 5).reshape(64, wide)
    rows = np.arange(8)
    take_one = (np.arange(16)[None, :] == 8 + rows[:, None]) & (rows[:, None] < 4)
    take_two = (np.arange(16)[None, :] == 12 + rows[:, None] // 2) & (rows[:, None] < 4)
    take_zero = np.arange(8)[None, :] == rows[:, None] // 2
    centres = (np.arange(SUB) + 0.5) / SUB - 0.5
    to_z = np.arange(cells_z)[None, :] // (2 * SUB) == rows[:, None]
    heights = np.tile(centres, cells_z // SUB)
    bz_of = np.arange(cells_z) // SUB % 2
    weights = np.zeros((2, 2, 2, 2, 32, cells_z))
    fields = np.zeros((3, 2, 3, 2, SUB, 2, 2, 2, 32))
    for index, power in enumerate(multi_index):
        for bz in range(2):
            weights[0, :, :, bz, index] = (bz_of == bz) * heights ** power[2]
            if power[2] > 0:
                weights[1, :, :, bz, index] = (bz_of == bz) * heights ** (power[2] - 1)
        for k in range(3):
            if power[k] > 0:
                lowered = list(power)
                lowered[k] -= 1
                for bx in range(2):
                    for by in range(2):
                        fields[k, bx, lowered[0], by, :, bx, by, :, index] = (
                            -power[k] / factorial_of(power) * centres ** lowered[1]
                        )[:, None]
    return (
        scale.reshape(16, wide),
        stacked(2.0).reshape(4, 64, 64),
        near,
        take_one.astype(float),
        take_two.astype(float),
        take_zero.astype(float),
        to_z.astype(float),
        weights.reshape(2, wide, cells_z),
        fields.reshape(3, 96, wide),
    )


def top_tables(nx, ny):
    lift = np.asarray(upward_matrices(4.0), np.float64)
    raise_up = np.zeros((4, slot, slot))
    lower_down = np.zeros((4, slot, 64))
    down = np.asarray(downward_matrices(4.0), np.float64)
    for bx in range(2):
        for by in range(2):
            for dz in range(2):
                raise_up[bx * 2 + by, (2 + dz) * count_m : (3 + dz) * count_m, :count_m] = (
                    lift[bx, by, dz] * 4.0 ** degrees[None, :]
                ).T
                lower_down[bx * 2 + by, :count_m, dz * 32 : dz * 32 + count_m] = down[bx, by, dz].T
    offsets = np.array(offset_grid(nx - 1, ny - 1, 1))
    kernels = np.asarray(translation_kernel(8.0, offsets), np.float64)
    counting = np.abs(offsets).max(axis=1) > 1
    far = np.zeros((len(offsets), slot, slot))
    far[:, :count_m, :count_m] = (kernels * counting[:, None, None]).transpose(0, 2, 1)
    return bool(counting.any()), raise_up, lower_down, far


def halves(value):
    high = value.astype(jnp.bfloat16)
    return high, (value - high.astype(jnp.float32)).astype(jnp.bfloat16)


def product(left, right):
    return jnp.dot(left, right, preferred_element_type=jnp.float32)


def times(value, table_hi, table_lo):
    high, low = halves(value)
    size = value.shape[0]
    both = product(jnp.concatenate([high, low], axis=0), table_hi)
    both = both[:size] + both[size:]
    return both if table_lo is None else both + product(high, table_lo)


def wholly(left, right):
    return jnp.dot(left, right, precision=highest, preferred_element_type=jnp.float32)


def picked(zero_one, value):
    high, low = halves(value)
    pick = zero_one.astype(jnp.bfloat16)
    return product(pick, high) + product(pick, low)


def sound(entropy, inverse):
    pressure = (gamma_gas - 1.0) * jnp.exp(gamma_gas * jnp.log(entropy))
    return pressure, jnp.sqrt(gamma_gas * pressure * inverse)


def states_of(stencil):
    a, b, c, d, e, f = stencil
    interface = (37.0 / 60.0) * (c + d) - (8.0 / 60.0) * (b + e) + (1.0 / 60.0) * (a + f)
    low, high = jnp.minimum(c, d), jnp.maximum(c, d)
    left = jnp.minimum(jnp.maximum(interface, jnp.minimum(b, low)), jnp.maximum(b, high))
    right = jnp.minimum(jnp.maximum(interface, jnp.minimum(e, low)), jnp.maximum(e, high))
    return left, right


def prepare(stencil_of, direction):
    mass = states_of(stencil_of(0))
    push = states_of(stencil_of(1 + direction))
    heat = states_of(stencil_of(5))
    inverse = [1.0 / value for value in mass]
    speed = [push[i] * inverse[i] for i in range(2)]
    gas = [sound(heat[i], inverse[i]) for i in range(2)]
    fastest = jnp.maximum(jnp.abs(speed[0]) + gas[0][1], jnp.abs(speed[1]) + gas[1][1])
    weights = 0.5 * (speed[0] + fastest), 0.5 * (speed[1] - fastest)
    flux = [left * weights[0] + right * weights[1] for left, right in (mass, push, heat)]
    flux[1] = flux[1] + 0.5 * (gas[0][0] + gas[1][0])
    work = 0.5 * (gas[0][0] * speed[0] + gas[1][0] * speed[1])
    return (*flux, *weights, work)


def apply(prepared, stencil_of, direction, count_fields, emit):
    known = dict(zip((0, 1 + direction, 5), prepared[:3]))
    for field in range(count_fields):
        if field in known:
            emit(field, known[field])
            continue
        left, right = states_of(stencil_of(field))
        flux = left * prepared[3] + right * prepared[4]
        emit(field, flux + prepared[5] if field == 4 else flux)


def section_kernel(
    sizes, top, names, density, momentum, energy, entropy, tracers, flags, *rest
):
    held_tables = dict(zip(names, rest[: len(names)]))
    section, accel = rest[len(names) : len(names) + 2]
    table = dict(zip(names, rest[len(names) + 2 : 2 * len(names) + 2]))
    (
        ext_x, ext_y, moved, previous, packed, packed_flux, tiles, near, window, rows_p, splits,
        load_sem, table_sem, halo_send, halo_recv, first_send, first_recv,
        second_send, second_recv, side_send, side_recv,
    ) = rest[2 * len(names) + 2 :]
    count_x, count_y, nf, cx, cy, cz = sizes
    mx, my = lax.axis_index("mx"), lax.axis_index("my")
    loads = [
        pltpu.make_async_copy(source, ext_x.at[pl.ds(begin, size), pl.ds(3, cx)], load_sem.at[i])
        for i, (source, begin, size) in enumerate(
            [(density, 0, 1), (momentum, 1, 3), (energy, 4, 1), (entropy, 5, 1), (tracers, 6, nf - 6)]
        )
    ]
    px, py = lax.rem(mx, 2), lax.rem(my, 2)
    tables = {}
    for i, name in enumerate(names):
        source = held_tables[name]
        if name.startswith("second"):
            source = source.at[px * 2 + py]
        tables[name] = pltpu.make_async_copy(source, table[name], table_sem.at[i])
    for copy in loads:
        copy.start()
    for copy in tables.values():
        copy.start()

    def at_x(step):
        return (lax.rem(mx + step + count_x, count_x), my)

    def at_y(step):
        return (mx, lax.rem(my + step + count_y, count_y))

    barrier = pltpu.get_barrier_semaphore()
    for step in range(1, count_x):
        pl.semaphore_signal(barrier, inc=1, device_id=at_x(step), device_id_type=MESH)
    for step in range(1, count_y):
        pl.semaphore_signal(barrier, inc=1, device_id=at_y(step), device_id_type=MESH)
    for copy in loads:
        copy.wait()

    def remote(source, target, send, recv, device):
        return pltpu.make_async_remote_copy(
            src_ref=source, dst_ref=target, send_sem=send, recv_sem=recv,
            device_id=device, device_id_type=MESH,
        )

    def halo_pair(buffer, length, base, place):
        lower = remote(
            buffer.at[:, pl.ds(3, 3)], buffer.at[:, pl.ds(length + 3, 3)],
            halo_send.at[base], halo_recv.at[base], place(-1),
        )
        upper = remote(
            buffer.at[:, pl.ds(length, 3)], buffer.at[:, pl.ds(0, 3)],
            halo_send.at[base + 1], halo_recv.at[base + 1], place(1),
        )
        return lower, upper

    def start_halo(pair, position, count):
        @pl.when(position > 0)
        def _():
            pair[0].start()

        @pl.when(position < count - 1)
        def _():
            pair[1].start()

    def finish_halo(pair, buffer, length, position, count):
        @pl.when(position > 0)
        def _():
            pair[0].wait_send()
            pair[1].wait_recv()

        @pl.when(position < count - 1)
        def _():
            pair[1].wait_send()
            pair[0].wait_recv()

        @pl.when(position == 0)
        def _():
            for row in range(3):
                buffer[:, row] = buffer[:, 3]

        @pl.when(position == count - 1)
        def _():
            for row in range(3):
                buffer[:, length + 3 + row] = buffer[:, length + 2]

    pair_x = halo_pair(ext_x, cx, 0, at_x)
    pair_y = halo_pair(ext_y, cy, 2, at_y)

    def turn(rows):
        def one(field, carry):
            for row in rows:
                ext_y[field, 3 + row] = ext_x[field, pl.ds(3, cx), row, :]
            return carry

        lax.fori_loop(0, nf, one, 0)

    turn([*range(3), *range(cy - 3, cy)])
    pl.semaphore_wait(barrier, count_x + count_y - 2)
    start_halo(pair_y, my, count_y)
    start_halo(pair_x, mx, count_x)
    turn(range(3, cy - 3))

    planes = 4

    def cell_speed(step, best):
        rows = pl.ds(3 + step * planes, planes)
        inverse = 1.0 / ext_x[0, rows]
        largest = jnp.maximum(
            jnp.maximum(jnp.abs(ext_x[1, rows]), jnp.abs(ext_x[2, rows])), jnp.abs(ext_x[3, rows])
        )
        _, speed = sound(ext_x[5, rows], inverse)
        return jnp.maximum(best, jnp.max(largest * inverse + speed, axis=0))

    best = lax.fori_loop(0, cx // planes, cell_speed, jnp.zeros((cy, cz), jnp.float32))
    best = jnp.max(best)

    for name in names:
        if name in early_names:
            tables[name].wait()

    def pair_of(name, *at):
        low = name + "_lo"
        return [table[name + "_hi"][(*at, ...)], table[low][(*at, ...)] if low in names else None]

    flagged = product(
        jnp.concatenate(
            [
                jnp.broadcast_to(
                    flags[bx, by : by + 1, :].astype(jnp.float32), (SUB, flags.shape[2])
                )
                for bx in range(2)
                for by in range(2)
            ],
            axis=0,
        ).astype(jnp.bfloat16),
        table["flag_z"][...].astype(jnp.bfloat16),
    )
    for bx in range(2):
        rows = [ext_x[0, 3 + bx * SUB + i] for i in range(SUB)]
        for power in range(4):
            total = rows[0] * ((0.5 / SUB - 0.5) ** power)
            for i in range(1, SUB):
                total = total + rows[i] * (((i + 0.5) / SUB - 0.5) ** power)
            rows_p[pl.ds((bx * 4 + power) * 2 * SUB, 2 * SUB), :] = (
                total * flagged[bx * 2 * SUB : (bx + 1) * 2 * SUB]
            )
    weighted = times(rows_p[...].T, *pair_of("spread"))
    shifted = picked(table["cell_rows"][...], weighted * table["along_z"][...])

    def choose(stack, lanes):
        lane = lax.rem(lax.broadcasted_iota(jnp.int32, (8, lanes), 1), slot)
        total = jnp.zeros((8, lanes), jnp.float32)
        for sd in range(6):
            inside = (lane >= sd * count_m) & (lane < (sd + 1) * count_m)
            total = total + jnp.where(inside, stack[sd * 8 : sd * 8 + 8], 0.0)
        return total

    block = choose(shifted, 4 * slot)
    near[1, 1] = block
    first = times(block, *pair_of("pick_up"))
    tile = choose(picked(table["one_rows"][...], first), slot)
    lifted = times(first, *pair_of("second"))
    for dz in range(2):
        part = picked(
            table["two_rows"][dz * 48 : dz * 48 + 48], lifted[:, dz * slot : (dz + 1) * slot]
        )
        tile = tile + choose(part, slot)
    row_index = lax.broadcasted_iota(jnp.int32, (8, slot), 0)
    tiles[mx, my] = jnp.where(row_index == 7, best, tile)

    for step in range(1, count_x):
        remote(
            tiles.at[mx, my], tiles.at[mx, my],
            first_send.at[step], first_recv.at[step], at_x(step),
        ).start()
    side_x = (
        remote(near.at[1, 1], near.at[2, 1], side_send.at[0], side_recv.at[0], at_x(-1)),
        remote(near.at[1, 1], near.at[0, 1], side_send.at[1], side_recv.at[1], at_x(1)),
    )
    start_halo(side_x, mx, count_x)

    lane_z = lax.broadcasted_iota(jnp.int32, (cy, cz), 1)

    def pack(row, carry):
        mine = (lane_z >= row * 8) & (lane_z < row * 8 + 8)
        for field in range(nf):
            turned = pltpu.roll(ext_x[field, 3 + row], row * 8 + 3, 1)
            packed[field] = jnp.where(mine, turned, packed[field])
        return carry

    packed[...] = jnp.ones(packed.shape, jnp.float32)
    lax.fori_loop(0, cx, pack, 0)

    def end_stencil(field):
        value = packed[field]
        one = pltpu.roll(value, cz - 1, 1)
        two = pltpu.roll(value, cz - 2, 1)
        return value, one, two, two, two, two

    def end_emit(field, flux):
        packed_flux[field] = flux

    apply(prepare(end_stencil, 2), end_stencil, 2, nf, end_emit)

    def stencil_z(row):
        def stencil(field):
            value = ext_x[field, 3 + row]
            out = [value]
            for step in range(3):
                out.insert(0, jnp.where(lane_z < 1, value, pltpu.roll(out[0], 1, 1)))
            for step in range(2):
                out.append(jnp.where(lane_z == cz - 1, value, pltpu.roll(out[-1], cz - 1, 1)))
            return out

        return stencil

    def sweep_z(row, prepared):
        following = prepare(stencil_z(jnp.minimum(row + 1, cx - 1)), 2)

        def emit(field, flux):
            ending = pltpu.roll(packed_flux[field], cz - 1 - row * 8, 1)
            above = jnp.where(lane_z == cz - 1, ending, pltpu.roll(flux, cz - 1, 1))
            section[field, row] = above - flux

        apply(prepared, stencil_z(row), 2, nf, emit)
        return following

    lax.fori_loop(0, cx, sweep_z, prepare(stencil_z(0), 2))

    def finish_side(pair, position, count, low, high):
        @pl.when(position > 0)
        def _():
            pair[0].wait_send()
            pair[1].wait_recv()

        @pl.when(position < count - 1)
        def _():
            pair[1].wait_send()
            pair[0].wait_recv()

        @pl.when(position == 0)
        def _():
            low[...] = jnp.zeros(low.shape, jnp.float32)

        @pl.when(position == count - 1)
        def _():
            high[...] = jnp.zeros(high.shape, jnp.float32)

    for step in range(1, count_x):
        arrived = tiles.at[lax.rem(mx - step + count_x, count_x), my]
        copy = remote(arrived, arrived, first_send.at[step], first_recv.at[step], at_x(step))
        copy.wait_send()
        copy.wait_recv()
    finish_side(side_x, mx, count_x, near.at[0, 1], near.at[2, 1])
    for step in range(1, count_y):
        remote(
            tiles.at[:, my], tiles.at[:, my], second_send.at[step], second_recv.at[step], at_y(step)
        ).start()
    side_y = (
        remote(near.at[:, 1], near.at[:, 2], side_send.at[2], side_recv.at[2], at_y(-1)),
        remote(near.at[:, 1], near.at[:, 0], side_send.at[3], side_recv.at[3], at_y(1)),
    )
    start_halo(side_y, my, count_y)


    def sweep(buffer, length, direction, store):
        def stencil_at(face):
            return lambda field: [buffer[field, face + i] for i in range(6)]

        def start_emit(field, flux):
            previous[field] = flux

        apply(prepare(stencil_at(0), direction), stencil_at(0), direction, nf, start_emit)

        def body(cell, prepared):
            following = prepare(stencil_at(jnp.minimum(cell + 2, length)), direction)

            def emit(field, flux):
                store(field, cell, flux - previous[field])
                previous[field] = flux

            apply(prepared, stencil_at(cell + 1), direction, nf, emit)
            return following

        lax.fori_loop(0, length, body, prepare(stencil_at(1), direction))

    finish_halo(pair_x, ext_x, cx, mx, count_x)

    def store_x(field, cell, value):
        section[field, cell] = section[field, cell] + value

    sweep(ext_x, cx, 0, store_x)

    finish_halo(pair_y, ext_y, cy, my, count_y)

    def store_y(field, cell, value):
        moved[field, cell] = value

    sweep(ext_y, cy, 1, store_y)

    for step in range(1, count_y):
        arrived = tiles.at[:, lax.rem(my - step + count_y, count_y)]
        copy = remote(arrived, arrived, second_send.at[step], second_recv.at[step], at_y(step))
        copy.wait_send()
        copy.wait_recv()
    finish_side(side_y, my, count_y, near.at[:, 0], near.at[:, 2])

    fastest = jnp.max(jnp.max(tiles[...], axis=(0, 1))[7:8, :])
    step_size = courant / (SUB * jnp.full((1, cz), fastest, jnp.float32))

    one_x, one_y = mx // 2, my // 2
    two_x, two_y = mx // 4, my // 4

    def united(ux, uy):
        return (
            tiles[2 * ux, 2 * uy] + tiles[2 * ux, 2 * uy + 1]
            + tiles[2 * ux + 1, 2 * uy] + tiles[2 * ux + 1, 2 * uy + 1]
        )

    def held(value, count):
        return jnp.clip(value, 0, count - 1), (value >= 0) & (value < count)

    for dx in range(3):
        for dy in range(3):
            base = (dx * 3 + dy) * 4 * slot
            window[0:8, base : base + 4 * slot] = near[dx, dy]
            for bx in range(2):
                for by in range(2):
                    at = base + (bx * 2 + by) * slot
                    gx, in_x = held(2 * (one_x + dx - 1) + bx, count_x)
                    gy, in_y = held(2 * (one_y + dy - 1) + by, count_y)
                    ux, in_ux = held(2 * (two_x + dx - 1) + bx, count_x // 2)
                    uy, in_uy = held(2 * (two_y + dy - 1) + by, count_y // 2)
                    own = jnp.where(in_x & in_y, tiles[gx, gy], 0.0)
                    joint = jnp.where(in_ux & in_uy, united(ux, uy), 0.0)
                    window[8:16, at : at + slot] = jnp.where(
                        row_index < 4, own, jnp.where(row_index < 6, joint, 0.0)
                    )

    for name in names:
        if name not in early_names:
            tables[name].wait()

    keep = (lax.broadcasted_iota(jnp.int32, (16, wide), 0) < 8).astype(jnp.float32)
    middle_chunks = 36 * slot // wide
    chunks = middle_chunks + len(inner_columns) * slot // wide
    for index in range(chunks):
        if index < middle_chunks:
            value = window[:, index * wide : (index + 1) * wide]
        else:
            pair = inner_columns[2 * (index - middle_chunks) :][:2]
            value = keep * jnp.concatenate(
                [window[:, column * slot : (column + 1) * slot] for column in pair], axis=1
            )
        high, low = halves(value)
        splits[index, 0:16] = high
        splits[index, 16:32] = low

    upper = jnp.zeros((32, wide), jnp.float32)
    lower = jnp.zeros((16, wide), jnp.float32)
    for index in range(chunks):
        both = splits[index]
        upper = upper + product(both, table["window_hi"][index])
        lower = lower + product(both[:16], table["window_lo"][index])
    sums = (upper[:16] + upper[16:] + lower) * table["scale"][...]


    def select(values, which):
        total = jnp.zeros((values.shape[0], 64), jnp.float32)
        for child in range(4):
            total = total + jnp.where(which == child, values[:, child * 64 : child * 64 + 64], 0.0)
        return total

    lane_64 = lax.broadcasted_iota(jnp.int32, (8, 64), 1)
    same_half = (lane_64 >= 32) == (lax.rem(lax.broadcasted_iota(jnp.int32, (8, 64), 0), 2) == 1)
    which_two = lax.rem(one_x, 2) * 2 + lax.rem(one_y, 2)
    second_sum = select(sums, which_two)
    if top:
        nx3, ny3 = count_x // 4, count_y // 4
        grown = jnp.zeros((8, slot), jnp.float32)
        for sx in range(nx3):
            for sy in range(ny3):
                source = jnp.zeros((8, slot), jnp.float32)
                for bx in range(2):
                    for by in range(2):
                        source = source + wholly(
                            united(2 * sx + bx, 2 * sy + by), table["raise_up"][bx * 2 + by]
                        )
                source = jnp.where((row_index == 4) | (row_index == 5), source, 0.0)
                place = ((sx - two_x + nx3 - 1) * (2 * ny3 - 1) + (sy - two_y + ny3 - 1)) * 3
                for dz in range(3):
                    moved_rows = source if dz == 1 else pltpu.roll(source, 1 if dz == 0 else 7, 0)
                    grown = grown + wholly(moved_rows, table["far"][place + dz])
        grown = jnp.where((row_index == 4) | (row_index == 5), grown, 0.0)
        carried = wholly(grown, table["lower_down"][which_two])
        second_sum = second_sum + jnp.concatenate([jnp.zeros((8, 64), jnp.float32), carried], axis=0)
    from_two = jnp.where(same_half, picked(table["take_two"][...], second_sum), 0.0)
    which_one = px * 2 + py
    first_sum = picked(table["take_one"][...], select(sums, which_one)) + times(
        from_two, *pair_of("down_two", which_one)
    )
    from_one = jnp.where(same_half, picked(table["take_zero"][...], first_sum), 0.0)
    expansion = sums[0:8] + times(from_one, *pair_of("down_one"))
    turned_hi, turned_lo = halves(expansion.T)
    to_z = table["to_z"][...].astype(jnp.bfloat16)
    on_z = product(turned_hi, to_z) + product(turned_lo, to_z)
    pieces = []
    for which, first_row, last_row in ((0, 0, 192), (1, 192, 288)):
        high, low = halves(on_z * table["weights"][which])
        field_hi = table["fields_hi"][first_row:last_row]
        piece = product(field_hi, high) + product(field_hi, low)
        if "fields_lo" in names:
            piece = piece + product(table["fields_lo"][first_row:last_row], high)
        pieces.append(piece)
    for k in range(3):
        parts = pieces[0][k * 96 : k * 96 + 96] if k < 2 else pieces[1]
        for row in range(cx):
            bx, height = row // SUB, (row % SUB + 0.5) / SUB - 0.5
            base = bx * 6 * SUB
            accel[k, row] = (
                parts[base : base + 2 * SUB]
                + height * parts[base + 2 * SUB : base + 4 * SUB]
                + (height * height) * parts[base + 4 * SUB : base + 6 * SUB]
            )

    def finish(cell, carry):
        own = [ext_x[field, 3 + cell] for field in range(4)]
        pull = [accel[k, cell] for k in range(3)]
        for field in range(nf):
            total = (section[field, cell] + moved[field, :, cell, :]) * (-float(SUB))
            if 1 <= field <= 3:
                total = total + own[0] * pull[field - 1]
            if field == 4:
                total = total + own[1] * pull[0] + own[2] * pull[1] + own[3] * pull[2]
            section[field, cell] = ext_x[field, 3 + cell] + step_size * total
        return carry

    lax.fori_loop(0, cx, finish, 0)


def shards(density, momentum, energy, entropy, tracers, leaf_flags):
    count_x, count_y = lax.axis_size("mx"), lax.axis_size("my")
    cx, cy, cz = density.shape
    nf = 6 + tracers.shape[0]
    middle, close = window_tables()
    top, raise_up, lower_down, far = top_tables(count_x // 4, count_y // 4)
    spread, along_z, cell_rows, pick_up, one_rows, second, two_rows, flag_z = moment_tables(cz)
    scale, down_two, down_one, take_one, take_two, take_zero, to_z, weights, fields = down_tables(cz)
    constants = {}
    for name, array in (("flag_z", flag_z), ("cell_rows", cell_rows), ("along_z", along_z)):
        constants[name] = jnp.asarray(array, jnp.float32)
    for name, array in (("spread", spread), ("pick_up", pick_up), ("second", second)):
        for ending, part in split_pair(array):
            constants[name + ending] = jnp.asarray(part)
    for name, array in (("one_rows", one_rows), ("two_rows", two_rows)):
        constants[name] = jnp.asarray(array, jnp.float32)
    joined = np.concatenate([middle, close]).reshape(-1, wide, wide)
    for name, array in (
        ("window", joined), ("down_two", down_two), ("down_one", down_one),
        ("fields", fields.reshape(-1, wide)),
    ):
        for ending, part in split_pair(array):
            constants[name + ending] = jnp.asarray(part)
    for name, array in (
        ("scale", scale), ("take_one", take_one), ("take_two", take_two),
        ("take_zero", take_zero), ("to_z", to_z), ("weights", weights),
    ):
        constants[name] = jnp.asarray(array, jnp.float32)
    if top:
        for name, array in (("raise_up", raise_up), ("lower_down", lower_down), ("far", far)):
            constants[name] = jnp.asarray(array, jnp.float32)
    names = tuple(constants)
    shapes = [
        pltpu.VMEM(
            array.shape[1:] if name.startswith("second") else array.shape, array.dtype
        )
        for name, array in constants.items()
    ]
    anywhere = pl.BlockSpec(memory_space=pl.ANY)
    local = pl.BlockSpec(memory_space=pltpu.VMEM)
    dma = pltpu.SemaphoreType.DMA
    f32 = jnp.float32
    return pl.pallas_call(
        functools.partial(section_kernel, (count_x, count_y, nf, cx, cy, cz), top, names),
        out_shape=(
            jax.ShapeDtypeStruct((nf, cx, cy, cz), f32),
            jax.ShapeDtypeStruct((3, cx, cy, cz), f32),
        ),
        in_specs=[anywhere] * 5 + [local] + [anywhere] * len(names),
        out_specs=(local, local),
        scratch_shapes=shapes
        + [
            pltpu.VMEM((nf, cx + 6, cy, cz), f32),
            pltpu.VMEM((nf, cy + 6, cx, cz), f32),
            pltpu.VMEM((nf, cy, cx, cz), f32),
            pltpu.VMEM((nf, cy, cz), f32),
            pltpu.VMEM((nf, cy, cz), f32),
            pltpu.VMEM((nf, cy, cz), f32),
            pltpu.VMEM((count_x, count_y, 8, slot), f32),
            pltpu.VMEM((3, 3, 8, 4 * slot), f32),
            pltpu.VMEM((16, 36 * slot), f32),
            pltpu.VMEM((128, cz), f32),
            pltpu.VMEM((joined.shape[0], 32, wide), jnp.bfloat16),
            dma((5,)), dma((len(names),)), dma((4,)), dma((4,)),
            dma((count_x,)), dma((count_x,)), dma((count_y,)), dma((count_y,)),
            dma((4,)), dma((4,)),
        ],
        compiler_params=pltpu.CompilerParams(
            collective_id=0, has_side_effects=True, vmem_limit_bytes=56 * 1024 * 1024
        ),
    )(density[None], momentum, energy[None], entropy[None], tracers, leaf_flags, *constants.values())


def solution(mesh):
    placed = (
        P("mx", "my", None),
        P(None, "mx", "my", None),
        P("mx", "my", None),
        P("mx", "my", None),
        P(None, "mx", "my", None),
        P("mx", "my", None),
    )
    return jax.shard_map(
        shards,
        mesh=mesh,
        in_specs=placed,
        out_specs=(P(None, "mx", "my", None), P(None, "mx", "my", None)),
        check_vma=False,
    )
```

```python
import functools
import math

import jax
import jax.numpy as jnp
import numpy as np
from jax import lax
from jax.experimental import pallas as pl
from jax.experimental.pallas import tpu as pltpu
from jax.sharding import PartitionSpec as P

MESH = pl.DeviceIdType.MESH
SUB = 8
LEVELS = 3


gamma_gas = 5.0 / 3.0
courant = 0.3
gravity = 0.02
highest = lax.Precision.HIGHEST
multi_index = [
    (power_x, power_y, degree_sum - power_x - power_y)
    for degree_sum in range(4)
    for power_x in range(degree_sum, -1, -1)
    for power_y in range(degree_sum - power_x, -1, -1)
]


def factorial_of(exponent):
    return math.factorial(exponent[0]) * math.factorial(exponent[1]) * math.factorial(exponent[2])


def inverse_derivative(exponent, vectors):
    axes_list = [0] * exponent[0] + [1] * exponent[1] + [2] * exponent[2]
    radius = np.sqrt(np.sum(vectors * vectors, axis=1))
    radius_safe = np.where(radius > 0.0, radius, 1.0)
    degree = len(axes_list)
    if degree == 0:
        result = 1.0 / radius_safe
    elif degree == 1:
        result = -vectors[:, axes_list[0]] / radius_safe**3
    elif degree == 2:
        index_one, index_two = axes_list
        result = (
            3.0 * vectors[:, index_one] * vectors[:, index_two] / radius_safe**5
            - float(index_one == index_two) / radius_safe**3
        )
    else:
        index_one, index_two, index_three = axes_list
        crossed = (
            float(index_one == index_two) * vectors[:, index_three]
            + float(index_one == index_three) * vectors[:, index_two]
            + float(index_two == index_three) * vectors[:, index_one]
        )
        result = (
            -15.0
            * vectors[:, index_one]
            * vectors[:, index_two]
            * vectors[:, index_three]
            / radius_safe**7
            + 3.0 * crossed / radius_safe**5
        )
    return np.where(radius > 0.0, result, 0.0)


def offset_grid(reach_x, reach_y, reach_z):
    return [
        (shift_x, shift_y, shift_z)
        for shift_x in range(-reach_x, reach_x + 1)
        for shift_y in range(-reach_y, reach_y + 1)
        for shift_z in range(-reach_z, reach_z + 1)
    ]


def translation_kernel(spacing, offsets):
    vectors = np.asarray(offsets) * (-1.0 * spacing)
    entries = np.zeros((len(offsets), len(multi_index), len(multi_index)))
    for row_index, target_power in enumerate(multi_index):
        for column_index, source_power in enumerate(multi_index):
            if sum(target_power) + sum(source_power) <= 3:
                joined = (
                    target_power[0] + source_power[0],
                    target_power[1] + source_power[1],
                    target_power[2] + source_power[2],
                )
                entries[:, row_index, column_index] = (
                    -gravity
                    * (-1.0) ** sum(source_power)
                    / factorial_of(source_power)
                    * inverse_derivative(joined, vectors)
                )
    return entries.astype(np.float32)


def upward_matrices(spacing):
    entries = np.zeros((2, 2, 2, len(multi_index), len(multi_index)))
    for octant in range(8):
        octant_bits = (octant >> 2 & 1, octant >> 1 & 1, octant & 1)
        displacement = [(octant_bits[dimension] - 0.5) * spacing for dimension in range(3)]
        for row_index, target_power in enumerate(multi_index):
            for column_index, source_power in enumerate(multi_index):
                if all(
                    (source_power[dimension] <= target_power[dimension] for dimension in range(3))
                ):
                    entry_value = 1.0
                    for dimension in range(3):
                        entry_value *= math.comb(
                            target_power[dimension], source_power[dimension]
                        ) * displacement[dimension] ** (
                            target_power[dimension] - source_power[dimension]
                        )
                    entries[
                        octant_bits[0], octant_bits[1], octant_bits[2], row_index, column_index
                    ] = entry_value
    return entries.astype(np.float32)


def downward_matrices(spacing):
    entries = np.zeros((2, 2, 2, len(multi_index), len(multi_index)))
    for octant in range(8):
        octant_bits = (octant >> 2 & 1, octant >> 1 & 1, octant & 1)
        displacement = [(octant_bits[dimension] - 0.5) * spacing for dimension in range(3)]
        for row_index, target_power in enumerate(multi_index):
            for column_index, source_power in enumerate(multi_index):
                if all(
                    (source_power[dimension] >= target_power[dimension] for dimension in range(3))
                ):
                    entry_value = 1.0
                    for dimension in range(3):
                        lifted = source_power[dimension] - target_power[dimension]
                        entry_value *= displacement[dimension] ** lifted / math.factorial(lifted)
                    entries[
                        octant_bits[0], octant_bits[1], octant_bits[2], row_index, column_index
                    ] = entry_value
    return entries.astype(np.float32)


slot = 128
wide = 256
count_m = len(multi_index)
degrees = np.array([sum(exponent) for exponent in multi_index])
inner_columns = [
    (dx * 3 + dy) * 4 + bx * 2 + by
    for dx in range(3)
    for dy in range(3)
    for bx in range(2)
    for by in range(2)
    if 1 <= 2 * dx + bx <= 4 and 1 <= 2 * dy + by <= 4
]


early_names = (
    "flag_z", "cell_rows", "along_z", "spread_hi", "spread_lo", "pick_up_hi", "pick_up_lo",
    "second_hi", "second_lo", "one_rows", "two_rows",
)


def split_pair(table):
    table = np.asarray(table, np.float32)
    high = table.astype(jnp.bfloat16)
    low = (table - high.astype(np.float32)).astype(jnp.bfloat16)
    return [("_hi", high)] + ([("_lo", low)] if np.any(low.astype(np.float32)) else [])


def window_tables():
    columns = [
        (2 * dx - 2 + bx, 2 * dy - 2 + by)
        for dx in range(3)
        for dy in range(3)
        for bx in range(2)
        for by in range(2)
    ]
    children = [(i >> 2 & 1, i >> 1 & 1, i & 1) for i in range(8)]
    sources = [(cx, cy, sz - 2) for cx, cy in columns for sz in range(6)]
    offsets = np.array([[[s[k] - t[k] for k in range(3)] for t in children] for s in sources])
    kernels = np.asarray(translation_kernel(1.0, offsets.reshape(-1, 3)), np.float64)
    kernels = kernels.reshape(36, 6, 8, count_m, count_m)
    touching = (np.abs(offsets).max(axis=2) <= 1).reshape(36, 6, 8, 1, 1)

    def laid(part):
        out = np.zeros((36, slot, 8, 32))
        out[:, : 6 * count_m, :, :count_m] = part.transpose(0, 1, 4, 2, 3).reshape(
            36, 6 * count_m, 8, count_m
        )
        return out.reshape(36, slot, wide)

    middle = laid(np.where(touching, 0.0, kernels))
    close = laid(np.where(touching, kernels, 0.0))[np.array(inner_columns)]
    return middle.reshape(-1, wide), close.reshape(-1, wide)


def moment_tables(cells_z):
    centres = (np.arange(SUB) + 0.5) / SUB - 0.5
    spread = np.zeros((2, 4, 2, SUB, 4, slot))
    along_z = np.zeros((cells_z, 4, slot))
    pick_up = np.zeros((4, slot, slot))
    lift = np.asarray(upward_matrices(1.0), np.float64)
    lift_two = np.asarray(upward_matrices(2.0), np.float64)
    second = np.zeros((4, slot, 2 * slot))
    for sd in range(6):
        for index, power in enumerate(multi_index):
            lane = sd * count_m + index
            for bx in range(2):
                for by in range(2):
                    spread[bx, power[0], by, :, bx * 2 + by, lane] = (
                        centres ** power[1] / SUB**3
                    )
            along_z[:, :, lane] = (np.tile(centres, cells_z // SUB) ** power[2])[:, None]
            for bx in range(2):
                for by in range(2):
                    for dz in range(2):
                        for lower in range(count_m):
                            pick_up[bx * 2 + by, (2 + dz) * count_m + lower, lane] = (
                                lift[bx, by, dz, index, lower] * 0.5 ** sum(power)
                            )
                            second[bx * 2 + by, lower, dz * slot + lane] = (
                                lift_two[bx, by, dz, index, lower]
                                * 2.0 ** degrees[lower]
                                * 0.25 ** sum(power)
                            )
    parents = cells_z // SUB // 2
    rows = np.arange(8)
    cell_rows = np.zeros((6, 8, cells_z))
    one_rows = np.zeros((6, 8, 8))
    two_rows = np.zeros((2, 6, 8, 8))
    for s in range(3):
        for dz in range(2):
            sd = s * 2 + dz
            for row in rows:
                cell_rows[sd, row] = np.arange(cells_z) // SUB == 2 * (row + s - 1) + dz
                if row < parents // 2:
                    one_rows[sd, row] = rows == 2 * (row + s - 1) + dz
                if 4 <= row < 4 + parents // 4:
                    second_z = 2 * (row - 4 + s - 1) + dz
                    if 0 <= second_z < parents // 2:
                        for dz_one in range(2):
                            two_rows[dz_one, sd, row] = rows == 2 * second_z + dz_one
    return (
        spread.reshape(128, 4 * slot),
        along_z.reshape(cells_z, 4 * slot),
        cell_rows.reshape(48, cells_z),
        pick_up.reshape(4 * slot, slot),
        one_rows.reshape(48, 8),
        second,
        two_rows.reshape(96, 8),
        (np.arange(cells_z)[None, :] // SUB == np.arange(cells_z // SUB)[:, None]).astype(float),
    )


def down_tables(cells_z):
    def stacked(spacing):
        down = np.asarray(downward_matrices(spacing), np.float64)
        out = np.zeros((2, 2, 2, 32, 2, 32))
        for bz in range(2):
            for child in range(2):
                out[:, :, bz, :count_m, child, :count_m] = down[:, :, child].transpose(0, 1, 3, 2)
        return out

    scale = np.zeros((16, 8, 32))
    scale[:8, :, :count_m] = 1.0
    scale[8:12, :, :count_m] = 0.5 ** (degrees + 1)
    scale[12:14, :, :count_m] = 0.25 ** (degrees + 1)
    near = stacked(1.0)
    near = near.transpose(2, 3, 0, 1, 4, 5).reshape(64, wide)
    rows = np.arange(8)
    take_one = (np.arange(16)[None, :] == 8 + rows[:, None]) & (rows[:, None] < 4)
    take_two = (np.arange(16)[None, :] == 12 + rows[:, None] // 2) & (rows[:, None] < 4)
    take_zero = np.arange(8)[None, :] == rows[:, None] // 2
    centres = (np.arange(SUB) + 0.5) / SUB - 0.5
    to_z = np.arange(cells_z)[None, :] // (2 * SUB) == rows[:, None]
    heights = np.tile(centres, cells_z // SUB)
    bz_of = np.arange(cells_z) // SUB % 2
    weights = np.zeros((2, 2, 2, 2, 32, cells_z))
    fields = np.zeros((3, 2, 3, 2, SUB, 2, 2, 2, 32))
    for index, power in enumerate(multi_index):
        for bz in range(2):
            weights[0, :, :, bz, index] = (bz_of == bz) * heights ** power[2]
            if power[2] > 0:
                weights[1, :, :, bz, index] = (bz_of == bz) * heights ** (power[2] - 1)
        for k in range(3):
            if power[k] > 0:
                lowered = list(power)
                lowered[k] -= 1
                for bx in range(2):
                    for by in range(2):
                        fields[k, bx, lowered[0], by, :, bx, by, :, index] = (
                            -power[k] / factorial_of(power) * centres ** lowered[1]
                        )[:, None]
    return (
        scale.reshape(16, wide),
        stacked(2.0).reshape(4, 64, 64),
        near,
        take_one.astype(float),
        take_two.astype(float),
        take_zero.astype(float),
        to_z.astype(float),
        weights.reshape(2, wide, cells_z),
        fields.reshape(3, 96, wide),
    )


def top_tables(nx, ny):
    lift = np.asarray(upward_matrices(4.0), np.float64)
    raise_up = np.zeros((4, slot, slot))
    lower_down = np.zeros((4, slot, 64))
    down = np.asarray(downward_matrices(4.0), np.float64)
    for bx in range(2):
        for by in range(2):
            for dz in range(2):
                raise_up[bx * 2 + by, (2 + dz) * count_m : (3 + dz) * count_m, :count_m] = (
                    lift[bx, by, dz] * 4.0 ** degrees[None, :]
                ).T
                lower_down[bx * 2 + by, :count_m, dz * 32 : dz * 32 + count_m] = down[bx, by, dz].T
    offsets = np.array(offset_grid(nx - 1, ny - 1, 1))
    kernels = np.asarray(translation_kernel(8.0, offsets), np.float64)
    counting = np.abs(offsets).max(axis=1) > 1
    far = np.zeros((len(offsets), slot, slot))
    far[:, :count_m, :count_m] = (kernels * counting[:, None, None]).transpose(0, 2, 1)
    return bool(counting.any()), raise_up, lower_down, far


def halves(value):
    high = value.astype(jnp.bfloat16)
    return high, (value - high.astype(jnp.float32)).astype(jnp.bfloat16)


def product(left, right):
    return jnp.dot(left, right, preferred_element_type=jnp.float32)


def times(value, table_hi, table_lo):
    high, low = halves(value)
    size = value.shape[0]
    both = product(jnp.concatenate([high, low], axis=0), table_hi)
    both = both[:size] + both[size:]
    return both if table_lo is None else both + product(high, table_lo)


def wholly(left, right):
    return jnp.dot(left, right, precision=highest, preferred_element_type=jnp.float32)


def picked(zero_one, value):
    high, low = halves(value)
    pick = zero_one.astype(jnp.bfloat16)
    return product(pick, high) + product(pick, low)


def sound(entropy, inverse):
    pressure = (gamma_gas - 1.0) * jnp.exp(gamma_gas * jnp.log(entropy))
    return pressure, jnp.sqrt(gamma_gas * pressure * inverse)


def states_of(stencil):
    a, b, c, d, e, f = stencil
    interface = (37.0 / 60.0) * (c + d) - (8.0 / 60.0) * (b + e) + (1.0 / 60.0) * (a + f)
    low, high = jnp.minimum(c, d), jnp.maximum(c, d)
    left = jnp.minimum(jnp.maximum(interface, jnp.minimum(b, low)), jnp.maximum(b, high))
    right = jnp.minimum(jnp.maximum(interface, jnp.minimum(e, low)), jnp.maximum(e, high))
    return left, right


def prepare(stencil_of, direction):
    mass = states_of(stencil_of(0))
    push = states_of(stencil_of(1 + direction))
    heat = states_of(stencil_of(5))
    inverse = [1.0 / value for value in mass]
    speed = [push[i] * inverse[i] for i in range(2)]
    gas = [sound(heat[i], inverse[i]) for i in range(2)]
    fastest = jnp.maximum(jnp.abs(speed[0]) + gas[0][1], jnp.abs(speed[1]) + gas[1][1])
    weights = 0.5 * (speed[0] + fastest), 0.5 * (speed[1] - fastest)
    flux = [left * weights[0] + right * weights[1] for left, right in (mass, push, heat)]
    flux[1] = flux[1] + 0.5 * (gas[0][0] + gas[1][0])
    work = 0.5 * (gas[0][0] * speed[0] + gas[1][0] * speed[1])
    return (*flux, *weights, work)


def apply(prepared, stencil_of, direction, count_fields, emit):
    known = dict(zip((0, 1 + direction, 5), prepared[:3]))
    for field in range(count_fields):
        if field in known:
            emit(field, known[field])
            continue
        left, right = states_of(stencil_of(field))
        flux = left * prepared[3] + right * prepared[4]
        emit(field, flux + prepared[5] if field == 4 else flux)


def section_kernel(
    sizes, top, names, density, momentum, energy, entropy, tracers, flags, *rest
):
    held_tables = dict(zip(names, rest[: len(names)]))
    section_out, accel_out = rest[len(names) : len(names) + 2]
    table = dict(zip(names, rest[len(names) + 2 : 2 * len(names) + 2]))
    (
        ext_x, ext_y, moved, previous, packed, packed_flux, tiles, near, window, rows_p, splits,
        section, accel, out_sem,
        load_sem, table_sem, halo_send, halo_recv, first_send, first_recv,
        second_send, second_recv, side_send, side_recv,
    ) = rest[2 * len(names) + 2 :]
    count_x, count_y, nf, cx, cy, cz = sizes
    mx, my = lax.axis_index("mx"), lax.axis_index("my")
    loads = [
        pltpu.make_async_copy(source, ext_x.at[pl.ds(begin, size), pl.ds(3, cx)], load_sem.at[i])
        for i, (source, begin, size) in enumerate(
            [(density, 0, 1), (momentum, 1, 3), (energy, 4, 1), (entropy, 5, 1), (tracers, 6, nf - 6)]
        )
    ]
    px, py = lax.rem(mx, 2), lax.rem(my, 2)
    tables = {}
    for i, name in enumerate(names):
        source = held_tables[name]
        if name.startswith("second"):
            source = source.at[px * 2 + py]
        tables[name] = pltpu.make_async_copy(source, table[name], table_sem.at[i])
    for copy in loads:
        copy.start()
    for copy in tables.values():
        copy.start()

    def at_x(step):
        return (lax.rem(mx + step + count_x, count_x), my)

    def at_y(step):
        return (mx, lax.rem(my + step + count_y, count_y))

    barrier = pltpu.get_barrier_semaphore()
    for step in range(1, count_x):
        pl.semaphore_signal(barrier, inc=1, device_id=at_x(step), device_id_type=MESH)
    for step in range(1, count_y):
        pl.semaphore_signal(barrier, inc=1, device_id=at_y(step), device_id_type=MESH)
    for copy in loads:
        copy.wait()

    def remote(source, target, send, recv, device):
        return pltpu.make_async_remote_copy(
            src_ref=source, dst_ref=target, send_sem=send, recv_sem=recv,
            device_id=device, device_id_type=MESH,
        )

    def halo_pair(buffer, length, base, place):
        lower = remote(
            buffer.at[:, pl.ds(3, 3)], buffer.at[:, pl.ds(length + 3, 3)],
            halo_send.at[base], halo_recv.at[base], place(-1),
        )
        upper = remote(
            buffer.at[:, pl.ds(length, 3)], buffer.at[:, pl.ds(0, 3)],
            halo_send.at[base + 1], halo_recv.at[base + 1], place(1),
        )
        return lower, upper

    def start_halo(pair, position, count):
        @pl.when(position > 0)
        def _():
            pair[0].start()

        @pl.when(position < count - 1)
        def _():
            pair[1].start()

    def finish_halo(pair, buffer, length, position, count):
        @pl.when(position > 0)
        def _():
            pair[0].wait_send()
            pair[1].wait_recv()

        @pl.when(position < count - 1)
        def _():
            pair[1].wait_send()
            pair[0].wait_recv()

        @pl.when(position == 0)
        def _():
            for row in range(3):
                buffer[:, row] = buffer[:, 3]

        @pl.when(position == count - 1)
        def _():
            for row in range(3):
                buffer[:, length + 3 + row] = buffer[:, length + 2]

    pair_x = halo_pair(ext_x, cx, 0, at_x)
    pair_y = halo_pair(ext_y, cy, 2, at_y)

    def turn(rows):
        def one(field, carry):
            for row in rows:
                ext_y[field, 3 + row] = ext_x[field, pl.ds(3, cx), row, :]
            return carry

        lax.fori_loop(0, nf, one, 0)

    turn([*range(3), *range(cy - 3, cy)])
    pl.semaphore_wait(barrier, count_x + count_y - 2)
    start_halo(pair_y, my, count_y)
    start_halo(pair_x, mx, count_x)
    turn(range(3, cy - 3))

    planes = 4

    def cell_speed(step, best):
        rows = pl.ds(3 + step * planes, planes)
        inverse = 1.0 / ext_x[0, rows]
        largest = jnp.maximum(
            jnp.maximum(jnp.abs(ext_x[1, rows]), jnp.abs(ext_x[2, rows])), jnp.abs(ext_x[3, rows])
        )
        _, speed = sound(ext_x[5, rows], inverse)
        return jnp.maximum(best, jnp.max(largest * inverse + speed, axis=0))

    best = lax.fori_loop(0, cx // planes, cell_speed, jnp.zeros((cy, cz), jnp.float32))
    best = jnp.max(best)

    for name in names:
        if name in early_names:
            tables[name].wait()

    def pair_of(name, *at):
        low = name + "_lo"
        return [table[name + "_hi"][(*at, ...)], table[low][(*at, ...)] if low in names else None]

    flagged = product(
        jnp.concatenate(
            [
                jnp.broadcast_to(
                    flags[bx, by : by + 1, :].astype(jnp.float32), (SUB, flags.shape[2])
                )
                for bx in range(2)
                for by in range(2)
            ],
            axis=0,
        ).astype(jnp.bfloat16),
        table["flag_z"][...].astype(jnp.bfloat16),
    )
    for bx in range(2):
        rows = [ext_x[0, 3 + bx * SUB + i] for i in range(SUB)]
        for power in range(4):
            total = rows[0] * ((0.5 / SUB - 0.5) ** power)
            for i in range(1, SUB):
                total = total + rows[i] * (((i + 0.5) / SUB - 0.5) ** power)
            rows_p[pl.ds((bx * 4 + power) * 2 * SUB, 2 * SUB), :] = (
                total * flagged[bx * 2 * SUB : (bx + 1) * 2 * SUB]
            )
    weighted = times(rows_p[...].T, *pair_of("spread"))
    shifted = picked(table["cell_rows"][...], weighted * table["along_z"][...])

    def choose(stack, lanes):
        lane = lax.rem(lax.broadcasted_iota(jnp.int32, (8, lanes), 1), slot)
        total = jnp.zeros((8, lanes), jnp.float32)
        for sd in range(6):
            inside = (lane >= sd * count_m) & (lane < (sd + 1) * count_m)
            total = total + jnp.where(inside, stack[sd * 8 : sd * 8 + 8], 0.0)
        return total

    block = choose(shifted, 4 * slot)
    near[1, 1] = block
    first = times(block, *pair_of("pick_up"))
    tile = choose(picked(table["one_rows"][...], first), slot)
    lifted = times(first, *pair_of("second"))
    for dz in range(2):
        part = picked(
            table["two_rows"][dz * 48 : dz * 48 + 48], lifted[:, dz * slot : (dz + 1) * slot]
        )
        tile = tile + choose(part, slot)
    row_index = lax.broadcasted_iota(jnp.int32, (8, slot), 0)
    tiles[mx, my] = jnp.where(row_index == 7, best, tile)

    for step in range(1, count_x):
        remote(
            tiles.at[mx, my], tiles.at[mx, my],
            first_send.at[step], first_recv.at[step], at_x(step),
        ).start()
    side_x = (
        remote(near.at[1, 1], near.at[2, 1], side_send.at[0], side_recv.at[0], at_x(-1)),
        remote(near.at[1, 1], near.at[0, 1], side_send.at[1], side_recv.at[1], at_x(1)),
    )
    start_halo(side_x, mx, count_x)

    lane_z = lax.broadcasted_iota(jnp.int32, (cy, cz), 1)

    def pack(row, carry):
        mine = (lane_z >= row * 8) & (lane_z < row * 8 + 8)
        for field in range(nf):
            turned = pltpu.roll(ext_x[field, 3 + row], row * 8 + 3, 1)
            packed[field] = jnp.where(mine, turned, packed[field])
        return carry

    packed[...] = jnp.ones(packed.shape, jnp.float32)
    lax.fori_loop(0, cx, pack, 0)

    def end_stencil(field):
        value = packed[field]
        one = pltpu.roll(value, cz - 1, 1)
        two = pltpu.roll(value, cz - 2, 1)
        return value, one, two, two, two, two

    def end_emit(field, flux):
        packed_flux[field] = flux

    apply(prepare(end_stencil, 2), end_stencil, 2, nf, end_emit)

    def stencil_z(row):
        def stencil(field):
            value = ext_x[field, 3 + row]
            out = [value]
            for step in range(3):
                out.insert(0, jnp.where(lane_z < 1, value, pltpu.roll(out[0], 1, 1)))
            for step in range(2):
                out.append(jnp.where(lane_z == cz - 1, value, pltpu.roll(out[-1], cz - 1, 1)))
            return out

        return stencil

    def sweep_z(row, prepared):
        following = prepare(stencil_z(jnp.minimum(row + 1, cx - 1)), 2)

        def emit(field, flux):
            ending = pltpu.roll(packed_flux[field], cz - 1 - row * 8, 1)
            above = jnp.where(lane_z == cz - 1, ending, pltpu.roll(flux, cz - 1, 1))
            section[field, row] = above - flux

        apply(prepared, stencil_z(row), 2, nf, emit)
        return following

    lax.fori_loop(0, cx, sweep_z, prepare(stencil_z(0), 2))

    def finish_side(pair, position, count, low, high):
        @pl.when(position > 0)
        def _():
            pair[0].wait_send()
            pair[1].wait_recv()

        @pl.when(position < count - 1)
        def _():
            pair[1].wait_send()
            pair[0].wait_recv()

        @pl.when(position == 0)
        def _():
            low[...] = jnp.zeros(low.shape, jnp.float32)

        @pl.when(position == count - 1)
        def _():
            high[...] = jnp.zeros(high.shape, jnp.float32)

    for step in range(1, count_x):
        arrived = tiles.at[lax.rem(mx - step + count_x, count_x), my]
        copy = remote(arrived, arrived, first_send.at[step], first_recv.at[step], at_x(step))
        copy.wait_send()
        copy.wait_recv()
    finish_side(side_x, mx, count_x, near.at[0, 1], near.at[2, 1])
    for step in range(1, count_y):
        remote(
            tiles.at[:, my], tiles.at[:, my], second_send.at[step], second_recv.at[step], at_y(step)
        ).start()
    side_y = (
        remote(near.at[:, 1], near.at[:, 2], side_send.at[2], side_recv.at[2], at_y(-1)),
        remote(near.at[:, 1], near.at[:, 0], side_send.at[3], side_recv.at[3], at_y(1)),
    )
    start_halo(side_y, my, count_y)


    def sweep(buffer, length, direction, store):
        def stencil_at(face):
            return lambda field: [buffer[field, face + i] for i in range(6)]

        def start_emit(field, flux):
            previous[field] = flux

        apply(prepare(stencil_at(0), direction), stencil_at(0), direction, nf, start_emit)

        def body(cell, prepared):
            following = prepare(stencil_at(jnp.minimum(cell + 2, length)), direction)

            def emit(field, flux):
                store(field, cell, flux - previous[field])
                previous[field] = flux

            apply(prepared, stencil_at(cell + 1), direction, nf, emit)
            return following

        lax.fori_loop(0, length, body, prepare(stencil_at(1), direction))

    finish_halo(pair_x, ext_x, cx, mx, count_x)

    def store_x(field, cell, value):
        section[field, cell] = section[field, cell] + value

    sweep(ext_x, cx, 0, store_x)

    finish_halo(pair_y, ext_y, cy, my, count_y)

    def store_y(field, cell, value):
        moved[field, cell] = value

    sweep(ext_y, cy, 1, store_y)

    for step in range(1, count_y):
        arrived = tiles.at[:, lax.rem(my - step + count_y, count_y)]
        copy = remote(arrived, arrived, second_send.at[step], second_recv.at[step], at_y(step))
        copy.wait_send()
        copy.wait_recv()
    finish_side(side_y, my, count_y, near.at[:, 0], near.at[:, 2])

    fastest = jnp.max(jnp.max(tiles[...], axis=(0, 1))[7:8, :])
    step_size = courant / (SUB * jnp.full((1, cz), fastest, jnp.float32))

    one_x, one_y = mx // 2, my // 2
    two_x, two_y = mx // 4, my // 4

    def united(ux, uy):
        return (
            tiles[2 * ux, 2 * uy] + tiles[2 * ux, 2 * uy + 1]
            + tiles[2 * ux + 1, 2 * uy] + tiles[2 * ux + 1, 2 * uy + 1]
        )

    def held(value, count):
        return jnp.clip(value, 0, count - 1), (value >= 0) & (value < count)

    for dx in range(3):
        for dy in range(3):
            base = (dx * 3 + dy) * 4 * slot
            window[0:8, base : base + 4 * slot] = near[dx, dy]
            for bx in range(2):
                for by in range(2):
                    at = base + (bx * 2 + by) * slot
                    gx, in_x = held(2 * (one_x + dx - 1) + bx, count_x)
                    gy, in_y = held(2 * (one_y + dy - 1) + by, count_y)
                    ux, in_ux = held(2 * (two_x + dx - 1) + bx, count_x // 2)
                    uy, in_uy = held(2 * (two_y + dy - 1) + by, count_y // 2)
                    own = jnp.where(in_x & in_y, tiles[gx, gy], 0.0)
                    joint = jnp.where(in_ux & in_uy, united(ux, uy), 0.0)
                    window[8:16, at : at + slot] = jnp.where(
                        row_index < 4, own, jnp.where(row_index < 6, joint, 0.0)
                    )

    for name in names:
        if name not in early_names:
            tables[name].wait()

    keep = (lax.broadcasted_iota(jnp.int32, (16, wide), 0) < 8).astype(jnp.float32)
    middle_chunks = 36 * slot // wide
    chunks = middle_chunks + len(inner_columns) * slot // wide
    for index in range(chunks):
        if index < middle_chunks:
            value = window[:, index * wide : (index + 1) * wide]
        else:
            pair = inner_columns[2 * (index - middle_chunks) :][:2]
            value = keep * jnp.concatenate(
                [window[:, column * slot : (column + 1) * slot] for column in pair], axis=1
            )
        high, low = halves(value)
        splits[index, 0:16] = high
        splits[index, 16:32] = low

    upper = jnp.zeros((32, wide), jnp.float32)
    lower = jnp.zeros((16, wide), jnp.float32)
    for index in range(chunks):
        both = splits[index]
        upper = upper + product(both, table["window_hi"][index])
        lower = lower + product(both[:16], table["window_lo"][index])
    sums = (upper[:16] + upper[16:] + lower) * table["scale"][...]


    def select(values, which):
        total = jnp.zeros((values.shape[0], 64), jnp.float32)
        for child in range(4):
            total = total + jnp.where(which == child, values[:, child * 64 : child * 64 + 64], 0.0)
        return total

    lane_64 = lax.broadcasted_iota(jnp.int32, (8, 64), 1)
    same_half = (lane_64 >= 32) == (lax.rem(lax.broadcasted_iota(jnp.int32, (8, 64), 0), 2) == 1)
    which_two = lax.rem(one_x, 2) * 2 + lax.rem(one_y, 2)
    second_sum = select(sums, which_two)
    if top:
        nx3, ny3 = count_x // 4, count_y // 4
        grown = jnp.zeros((8, slot), jnp.float32)
        for sx in range(nx3):
            for sy in range(ny3):
                source = jnp.zeros((8, slot), jnp.float32)
                for bx in range(2):
                    for by in range(2):
                        source = source + wholly(
                            united(2 * sx + bx, 2 * sy + by), table["raise_up"][bx * 2 + by]
                        )
                source = jnp.where((row_index == 4) | (row_index == 5), source, 0.0)
                place = ((sx - two_x + nx3 - 1) * (2 * ny3 - 1) + (sy - two_y + ny3 - 1)) * 3
                for dz in range(3):
                    moved_rows = source if dz == 1 else pltpu.roll(source, 1 if dz == 0 else 7, 0)
                    grown = grown + wholly(moved_rows, table["far"][place + dz])
        grown = jnp.where((row_index == 4) | (row_index == 5), grown, 0.0)
        carried = wholly(grown, table["lower_down"][which_two])
        second_sum = second_sum + jnp.concatenate([jnp.zeros((8, 64), jnp.float32), carried], axis=0)
    from_two = jnp.where(same_half, picked(table["take_two"][...], second_sum), 0.0)
    which_one = px * 2 + py
    first_sum = picked(table["take_one"][...], select(sums, which_one)) + times(
        from_two, *pair_of("down_two", which_one)
    )
    from_one = jnp.where(same_half, picked(table["take_zero"][...], first_sum), 0.0)
    expansion = sums[0:8] + times(from_one, *pair_of("down_one"))
    turned_hi, turned_lo = halves(expansion.T)
    to_z = table["to_z"][...].astype(jnp.bfloat16)
    on_z = product(turned_hi, to_z) + product(turned_lo, to_z)
    pieces = []
    for which, first_row, last_row in ((0, 0, 192), (1, 192, 288)):
        high, low = halves(on_z * table["weights"][which])
        field_hi = table["fields_hi"][first_row:last_row]
        piece = product(field_hi, high) + product(field_hi, low)
        if "fields_lo" in names:
            piece = piece + product(table["fields_lo"][first_row:last_row], high)
        pieces.append(piece)
    for k in range(3):
        parts = pieces[0][k * 96 : k * 96 + 96] if k < 2 else pieces[1]
        for row in range(cx):
            bx, height = row // SUB, (row % SUB + 0.5) / SUB - 0.5
            base = bx * 6 * SUB
            accel[k, row] = (
                parts[base : base + 2 * SUB]
                + height * parts[base + 2 * SUB : base + 4 * SUB]
                + (height * height) * parts[base + 4 * SUB : base + 6 * SUB]
            )

    def finish(cell, carry):
        own = [ext_x[field, 3 + cell] for field in range(4)]
        pull = [accel[k, cell] for k in range(3)]
        for field in range(nf):
            total = (section[field, cell] + moved[field, :, cell, :]) * (-float(SUB))
            if 1 <= field <= 3:
                total = total + own[0] * pull[field - 1]
            if field == 4:
                total = total + own[1] * pull[0] + own[2] * pull[1] + own[3] * pull[2]
            section[field, cell] = ext_x[field, 3 + cell] + step_size * total
        return carry

    leaving = [pltpu.make_async_copy(accel, accel_out, out_sem.at[4])]
    leaving[0].start()
    for quarter in range(4):
        begin = quarter * cx // 4
        lax.fori_loop(begin, begin + cx // 4, finish, 0)
        planes_out = pl.ds(begin, cx // 4)
        leaving.append(
            pltpu.make_async_copy(
                section.at[:, planes_out], section_out.at[:, planes_out], out_sem.at[quarter]
            )
        )
        leaving[-1].start()
    for copy in leaving:
        copy.wait()


def hand_over_kernel(section, accel, section_out, accel_out, sem):
    copies = [
        pltpu.make_async_copy(source.at[i], target.at[i], sem.at[base + i])
        for base, source, target in ((0, section, section_out), (section.shape[0], accel, accel_out))
        for i in range(source.shape[0])
    ]
    for copy in copies:
        copy.start()
    for copy in copies:
        copy.wait()


def shards(density, momentum, energy, entropy, tracers, leaf_flags):
    count_x, count_y = lax.axis_size("mx"), lax.axis_size("my")
    cx, cy, cz = density.shape
    nf = 6 + tracers.shape[0]
    middle, close = window_tables()
    top, raise_up, lower_down, far = top_tables(count_x // 4, count_y // 4)
    spread, along_z, cell_rows, pick_up, one_rows, second, two_rows, flag_z = moment_tables(cz)
    scale, down_two, down_one, take_one, take_two, take_zero, to_z, weights, fields = down_tables(cz)
    constants = {}
    for name, array in (("flag_z", flag_z), ("cell_rows", cell_rows), ("along_z", along_z)):
        constants[name] = jnp.asarray(array, jnp.float32)
    for name, array in (("spread", spread), ("pick_up", pick_up), ("second", second)):
        for ending, part in split_pair(array):
            constants[name + ending] = jnp.asarray(part)
    for name, array in (("one_rows", one_rows), ("two_rows", two_rows)):
        constants[name] = jnp.asarray(array, jnp.float32)
    joined = np.concatenate([middle, close]).reshape(-1, wide, wide)
    for name, array in (
        ("window", joined), ("down_two", down_two), ("down_one", down_one),
        ("fields", fields.reshape(-1, wide)),
    ):
        for ending, part in split_pair(array):
            constants[name + ending] = jnp.asarray(part)
    for name, array in (
        ("scale", scale), ("take_one", take_one), ("take_two", take_two),
        ("take_zero", take_zero), ("to_z", to_z), ("weights", weights),
    ):
        constants[name] = jnp.asarray(array, jnp.float32)
    if top:
        for name, array in (("raise_up", raise_up), ("lower_down", lower_down), ("far", far)):
            constants[name] = jnp.asarray(array, jnp.float32)
    names = tuple(constants)
    shapes = [
        pltpu.VMEM(
            array.shape[1:] if name.startswith("second") else array.shape, array.dtype
        )
        for name, array in constants.items()
    ]
    anywhere = pl.BlockSpec(memory_space=pl.ANY)
    local = pl.BlockSpec(memory_space=pltpu.VMEM)
    dma = pltpu.SemaphoreType.DMA
    f32 = jnp.float32
    out_shape = (
        jax.ShapeDtypeStruct((nf, cx, cy, cz), f32),
        jax.ShapeDtypeStruct((3, cx, cy, cz), f32),
    )
    results = pl.pallas_call(
        functools.partial(section_kernel, (count_x, count_y, nf, cx, cy, cz), top, names),
        out_shape=out_shape,
        in_specs=[anywhere] * 5 + [local] + [anywhere] * len(names),
        out_specs=(anywhere, anywhere),
        scratch_shapes=shapes
        + [
            pltpu.VMEM((nf, cx + 6, cy, cz), f32),
            pltpu.VMEM((nf, cy + 6, cx, cz), f32),
            pltpu.VMEM((nf, cy, cx, cz), f32),
            pltpu.VMEM((nf, cy, cz), f32),
            pltpu.VMEM((nf, cy, cz), f32),
            pltpu.VMEM((nf, cy, cz), f32),
            pltpu.VMEM((count_x, count_y, 8, slot), f32),
            pltpu.VMEM((3, 3, 8, 4 * slot), f32),
            pltpu.VMEM((16, 36 * slot), f32),
            pltpu.VMEM((128, cz), f32),
            pltpu.VMEM((joined.shape[0], 32, wide), jnp.bfloat16),
            pltpu.VMEM((nf, cx, cy, cz), f32),
            pltpu.VMEM((3, cx, cy, cz), f32),
            dma((5,)),
            dma((5,)), dma((len(names),)), dma((4,)), dma((4,)),
            dma((count_x,)), dma((count_x,)), dma((count_y,)), dma((count_y,)),
            dma((4,)), dma((4,)),
        ],
        compiler_params=pltpu.CompilerParams(
            collective_id=0, has_side_effects=True, vmem_limit_bytes=56 * 1024 * 1024
        ),
    )(density[None], momentum, energy[None], entropy[None], tracers, leaf_flags, *constants.values())
    return pl.pallas_call(
        hand_over_kernel,
        out_shape=out_shape,
        in_specs=[anywhere] * 2,
        out_specs=(anywhere, anywhere),
        scratch_shapes=[dma((nf + 3,))],
    )(*results)


def solution(mesh):
    placed = (
        P("mx", "my", None),
        P(None, "mx", "my", None),
        P("mx", "my", None),
        P("mx", "my", None),
        P(None, "mx", "my", None),
        P("mx", "my", None),
    )
    return jax.shard_map(
        shards,
        mesh=mesh,
        in_specs=placed,
        out_specs=(P(None, "mx", "my", None), P(None, "mx", "my", None)),
        check_vma=False,
    )
```

```python
import functools
import math

import jax
import jax.numpy as jnp
import numpy as np
from jax import lax
from jax.experimental import pallas as pl
from jax.experimental.pallas import tpu as pltpu
from jax.sharding import PartitionSpec as P

MESH = pl.DeviceIdType.MESH
SUB = 8
LEVELS = 3


gamma_gas = 5.0 / 3.0
courant = 0.3
gravity = 0.02
highest = lax.Precision.HIGHEST
multi_index = [
    (power_x, power_y, degree_sum - power_x - power_y)
    for degree_sum in range(4)
    for power_x in range(degree_sum, -1, -1)
    for power_y in range(degree_sum - power_x, -1, -1)
]


def factorial_of(exponent):
    return math.factorial(exponent[0]) * math.factorial(exponent[1]) * math.factorial(exponent[2])


def inverse_derivative(exponent, vectors):
    axes_list = [0] * exponent[0] + [1] * exponent[1] + [2] * exponent[2]
    radius = np.sqrt(np.sum(vectors * vectors, axis=1))
    radius_safe = np.where(radius > 0.0, radius, 1.0)
    degree = len(axes_list)
    if degree == 0:
        result = 1.0 / radius_safe
    elif degree == 1:
        result = -vectors[:, axes_list[0]] / radius_safe**3
    elif degree == 2:
        index_one, index_two = axes_list
        result = (
            3.0 * vectors[:, index_one] * vectors[:, index_two] / radius_safe**5
            - float(index_one == index_two) / radius_safe**3
        )
    else:
        index_one, index_two, index_three = axes_list
        crossed = (
            float(index_one == index_two) * vectors[:, index_three]
            + float(index_one == index_three) * vectors[:, index_two]
            + float(index_two == index_three) * vectors[:, index_one]
        )
        result = (
            -15.0
            * vectors[:, index_one]
            * vectors[:, index_two]
            * vectors[:, index_three]
            / radius_safe**7
            + 3.0 * crossed / radius_safe**5
        )
    return np.where(radius > 0.0, result, 0.0)


def offset_grid(reach_x, reach_y, reach_z):
    return [
        (shift_x, shift_y, shift_z)
        for shift_x in range(-reach_x, reach_x + 1)
        for shift_y in range(-reach_y, reach_y + 1)
        for shift_z in range(-reach_z, reach_z + 1)
    ]


def translation_kernel(spacing, offsets):
    vectors = np.asarray(offsets) * (-1.0 * spacing)
    entries = np.zeros((len(offsets), len(multi_index), len(multi_index)))
    for row_index, target_power in enumerate(multi_index):
        for column_index, source_power in enumerate(multi_index):
            if sum(target_power) + sum(source_power) <= 3:
                joined = (
                    target_power[0] + source_power[0],
                    target_power[1] + source_power[1],
                    target_power[2] + source_power[2],
                )
                entries[:, row_index, column_index] = (
                    -gravity
                    * (-1.0) ** sum(source_power)
                    / factorial_of(source_power)
                    * inverse_derivative(joined, vectors)
                )
    return entries.astype(np.float32)


def upward_matrices(spacing):
    entries = np.zeros((2, 2, 2, len(multi_index), len(multi_index)))
    for octant in range(8):
        octant_bits = (octant >> 2 & 1, octant >> 1 & 1, octant & 1)
        displacement = [(octant_bits[dimension] - 0.5) * spacing for dimension in range(3)]
        for row_index, target_power in enumerate(multi_index):
            for column_index, source_power in enumerate(multi_index):
                if all(
                    (source_power[dimension] <= target_power[dimension] for dimension in range(3))
                ):
                    entry_value = 1.0
                    for dimension in range(3):
                        entry_value *= math.comb(
                            target_power[dimension], source_power[dimension]
                        ) * displacement[dimension] ** (
                            target_power[dimension] - source_power[dimension]
                        )
                    entries[
                        octant_bits[0], octant_bits[1], octant_bits[2], row_index, column_index
                    ] = entry_value
    return entries.astype(np.float32)


def downward_matrices(spacing):
    entries = np.zeros((2, 2, 2, len(multi_index), len(multi_index)))
    for octant in range(8):
        octant_bits = (octant >> 2 & 1, octant >> 1 & 1, octant & 1)
        displacement = [(octant_bits[dimension] - 0.5) * spacing for dimension in range(3)]
        for row_index, target_power in enumerate(multi_index):
            for column_index, source_power in enumerate(multi_index):
                if all(
                    (source_power[dimension] >= target_power[dimension] for dimension in range(3))
                ):
                    entry_value = 1.0
                    for dimension in range(3):
                        lifted = source_power[dimension] - target_power[dimension]
                        entry_value *= displacement[dimension] ** lifted / math.factorial(lifted)
                    entries[
                        octant_bits[0], octant_bits[1], octant_bits[2], row_index, column_index
                    ] = entry_value
    return entries.astype(np.float32)


slot = 128
wide = 256
count_m = len(multi_index)
degrees = np.array([sum(exponent) for exponent in multi_index])
inner_columns = [
    (dx * 3 + dy) * 4 + bx * 2 + by
    for dx in range(3)
    for dy in range(3)
    for bx in range(2)
    for by in range(2)
    if 1 <= 2 * dx + bx <= 4 and 1 <= 2 * dy + by <= 4
]


early_names = (
    "flag_z", "cell_rows", "along_z", "spread_hi", "spread_lo", "pick_up_hi", "pick_up_lo",
    "second_hi", "second_lo", "one_rows", "two_rows",
)


def split_pair(table):
    table = np.asarray(table, np.float32)
    high = table.astype(jnp.bfloat16)
    low = (table - high.astype(np.float32)).astype(jnp.bfloat16)
    return [("_hi", high)] + ([("_lo", low)] if np.any(low.astype(np.float32)) else [])


def window_tables():
    columns = [
        (2 * dx - 2 + bx, 2 * dy - 2 + by)
        for dx in range(3)
        for dy in range(3)
        for bx in range(2)
        for by in range(2)
    ]
    children = [(i >> 2 & 1, i >> 1 & 1, i & 1) for i in range(8)]
    sources = [(cx, cy, sz - 2) for cx, cy in columns for sz in range(6)]
    offsets = np.array([[[s[k] - t[k] for k in range(3)] for t in children] for s in sources])
    kernels = np.asarray(translation_kernel(1.0, offsets.reshape(-1, 3)), np.float64)
    kernels = kernels.reshape(36, 6, 8, count_m, count_m)
    touching = (np.abs(offsets).max(axis=2) <= 1).reshape(36, 6, 8, 1, 1)

    def laid(part):
        out = np.zeros((36, slot, 8, 32))
        out[:, : 6 * count_m, :, :count_m] = part.transpose(0, 1, 4, 2, 3).reshape(
            36, 6 * count_m, 8, count_m
        )
        return out.reshape(36, slot, wide)

    middle = laid(np.where(touching, 0.0, kernels))
    close = laid(np.where(touching, kernels, 0.0))[np.array(inner_columns)]
    return middle.reshape(-1, wide), close.reshape(-1, wide)


def moment_tables(cells_z):
    centres = (np.arange(SUB) + 0.5) / SUB - 0.5
    spread = np.zeros((2, 4, 2, SUB, 4, slot))
    along_z = np.zeros((cells_z, 4, slot))
    pick_up = np.zeros((4, slot, slot))
    lift = np.asarray(upward_matrices(1.0), np.float64)
    lift_two = np.asarray(upward_matrices(2.0), np.float64)
    second = np.zeros((4, slot, 2 * slot))
    for sd in range(6):
        for index, power in enumerate(multi_index):
            lane = sd * count_m + index
            for bx in range(2):
                for by in range(2):
                    spread[bx, power[0], by, :, bx * 2 + by, lane] = (
                        centres ** power[1] / SUB**3
                    )
            along_z[:, :, lane] = (np.tile(centres, cells_z // SUB) ** power[2])[:, None]
            for bx in range(2):
                for by in range(2):
                    for dz in range(2):
                        for lower in range(count_m):
                            pick_up[bx * 2 + by, (2 + dz) * count_m + lower, lane] = (
                                lift[bx, by, dz, index, lower] * 0.5 ** sum(power)
                            )
                            second[bx * 2 + by, lower, dz * slot + lane] = (
                                lift_two[bx, by, dz, index, lower]
                                * 2.0 ** degrees[lower]
                                * 0.25 ** sum(power)
                            )
    parents = cells_z // SUB // 2
    rows = np.arange(8)
    cell_rows = np.zeros((6, 8, cells_z))
    one_rows = np.zeros((6, 8, 8))
    two_rows = np.zeros((2, 6, 8, 8))
    for s in range(3):
        for dz in range(2):
            sd = s * 2 + dz
            for row in rows:
                cell_rows[sd, row] = np.arange(cells_z) // SUB == 2 * (row + s - 1) + dz
                if row < parents // 2:
                    one_rows[sd, row] = rows == 2 * (row + s - 1) + dz
                if 4 <= row < 4 + parents // 4:
                    second_z = 2 * (row - 4 + s - 1) + dz
                    if 0 <= second_z < parents // 2:
                        for dz_one in range(2):
                            two_rows[dz_one, sd, row] = rows == 2 * second_z + dz_one
    return (
        spread.reshape(128, 4 * slot),
        along_z.reshape(cells_z, 4 * slot),
        cell_rows.reshape(48, cells_z),
        pick_up.reshape(4 * slot, slot),
        one_rows.reshape(48, 8),
        second,
        two_rows.reshape(96, 8),
        (np.arange(cells_z)[None, :] // SUB == np.arange(cells_z // SUB)[:, None]).astype(float),
    )


def down_tables(cells_z):
    def stacked(spacing):
        down = np.asarray(downward_matrices(spacing), np.float64)
        out = np.zeros((2, 2, 2, 32, 2, 32))
        for bz in range(2):
            for child in range(2):
                out[:, :, bz, :count_m, child, :count_m] = down[:, :, child].transpose(0, 1, 3, 2)
        return out

    scale = np.zeros((16, 8, 32))
    scale[:8, :, :count_m] = 1.0
    scale[8:12, :, :count_m] = 0.5 ** (degrees + 1)
    scale[12:14, :, :count_m] = 0.25 ** (degrees + 1)
    near = stacked(1.0)
    near = near.transpose(2, 3, 0, 1, 4, 5).reshape(64, wide)
    rows = np.arange(8)
    take_one = (np.arange(16)[None, :] == 8 + rows[:, None]) & (rows[:, None] < 4)
    take_two = (np.arange(16)[None, :] == 12 + rows[:, None] // 2) & (rows[:, None] < 4)
    take_zero = np.arange(8)[None, :] == rows[:, None] // 2
    centres = (np.arange(SUB) + 0.5) / SUB - 0.5
    to_z = np.arange(cells_z)[None, :] // (2 * SUB) == rows[:, None]
    heights = np.tile(centres, cells_z // SUB)
    bz_of = np.arange(cells_z) // SUB % 2
    weights = np.zeros((2, 2, 2, 2, 32, cells_z))
    fields = np.zeros((3, 2, 3, 2, SUB, 2, 2, 2, 32))
    for index, power in enumerate(multi_index):
        for bz in range(2):
            weights[0, :, :, bz, index] = (bz_of == bz) * heights ** power[2]
            if power[2] > 0:
                weights[1, :, :, bz, index] = (bz_of == bz) * heights ** (power[2] - 1)
        for k in range(3):
            if power[k] > 0:
                lowered = list(power)
                lowered[k] -= 1
                for bx in range(2):
                    for by in range(2):
                        fields[k, bx, lowered[0], by, :, bx, by, :, index] = (
                            -power[k] / factorial_of(power) * centres ** lowered[1]
                        )[:, None]
    return (
        scale.reshape(16, wide),
        stacked(2.0).reshape(4, 64, 64),
        near,
        take_one.astype(float),
        take_two.astype(float),
        take_zero.astype(float),
        to_z.astype(float),
        weights.reshape(2, wide, cells_z),
        fields.reshape(3, 96, wide),
    )


def top_tables(nx, ny):
    lift = np.asarray(upward_matrices(4.0), np.float64)
    raise_up = np.zeros((4, slot, slot))
    lower_down = np.zeros((4, slot, 64))
    down = np.asarray(downward_matrices(4.0), np.float64)
    for bx in range(2):
        for by in range(2):
            for dz in range(2):
                raise_up[bx * 2 + by, (2 + dz) * count_m : (3 + dz) * count_m, :count_m] = (
                    lift[bx, by, dz] * 4.0 ** degrees[None, :]
                ).T
                lower_down[bx * 2 + by, :count_m, dz * 32 : dz * 32 + count_m] = down[bx, by, dz].T
    offsets = np.array(offset_grid(nx - 1, ny - 1, 1))
    kernels = np.asarray(translation_kernel(8.0, offsets), np.float64)
    counting = np.abs(offsets).max(axis=1) > 1
    far = np.zeros((len(offsets), slot, slot))
    far[:, :count_m, :count_m] = (kernels * counting[:, None, None]).transpose(0, 2, 1)
    return bool(counting.any()), raise_up, lower_down, far


def halves(value):
    high = value.astype(jnp.bfloat16)
    return high, (value - high.astype(jnp.float32)).astype(jnp.bfloat16)


def product(left, right):
    return jnp.dot(left, right, preferred_element_type=jnp.float32)


def times(value, table_hi, table_lo):
    high, low = halves(value)
    size = value.shape[0]
    both = product(jnp.concatenate([high, low], axis=0), table_hi)
    both = both[:size] + both[size:]
    return both if table_lo is None else both + product(high, table_lo)


def wholly(left, right):
    return jnp.dot(left, right, precision=highest, preferred_element_type=jnp.float32)


def picked(zero_one, value):
    high, low = halves(value)
    pick = zero_one.astype(jnp.bfloat16)
    return product(pick, high) + product(pick, low)


def sound(entropy, inverse):
    pressure = (gamma_gas - 1.0) * jnp.exp(gamma_gas * jnp.log(entropy))
    return pressure, jnp.sqrt(gamma_gas * pressure * inverse)


def states_of(stencil):
    a, b, c, d, e, f = stencil
    interface = (37.0 / 60.0) * (c + d) - (8.0 / 60.0) * (b + e) + (1.0 / 60.0) * (a + f)
    low, high = jnp.minimum(c, d), jnp.maximum(c, d)
    left = jnp.minimum(jnp.maximum(interface, jnp.minimum(b, low)), jnp.maximum(b, high))
    right = jnp.minimum(jnp.maximum(interface, jnp.minimum(e, low)), jnp.maximum(e, high))
    return left, right


def prepare(stencil_of, direction):
    mass = states_of(stencil_of(0))
    push = states_of(stencil_of(1 + direction))
    heat = states_of(stencil_of(5))
    inverse = [1.0 / value for value in mass]
    speed = [push[i] * inverse[i] for i in range(2)]
    gas = [sound(heat[i], inverse[i]) for i in range(2)]
    fastest = jnp.maximum(jnp.abs(speed[0]) + gas[0][1], jnp.abs(speed[1]) + gas[1][1])
    weights = 0.5 * (speed[0] + fastest), 0.5 * (speed[1] - fastest)
    flux = [left * weights[0] + right * weights[1] for left, right in (mass, push, heat)]
    flux[1] = flux[1] + 0.5 * (gas[0][0] + gas[1][0])
    work = 0.5 * (gas[0][0] * speed[0] + gas[1][0] * speed[1])
    return (*flux, *weights, work)


def apply(prepared, stencil_of, direction, count_fields, emit):
    known = dict(zip((0, 1 + direction, 5), prepared[:3]))
    for field in range(count_fields):
        if field in known:
            emit(field, known[field])
            continue
        left, right = states_of(stencil_of(field))
        flux = left * prepared[3] + right * prepared[4]
        emit(field, flux + prepared[5] if field == 4 else flux)


def section_kernel(
    sizes, top, names, density, momentum, energy, entropy, tracers, flags, *rest
):
    held_tables = dict(zip(names, rest[: len(names)]))
    section_out, accel_out = rest[len(names) : len(names) + 2]
    table = dict(zip(names, rest[len(names) + 2 : 2 * len(names) + 2]))
    (
        ext_x, ext_y, moved, previous, packed, packed_flux, tiles, near, window, rows_p, splits,
        section, accel, out_sem,
        load_sem, table_sem, halo_send, halo_recv, first_send, first_recv,
        second_send, second_recv, side_send, side_recv,
    ) = rest[2 * len(names) + 2 :]
    count_x, count_y, nf, cx, cy, cz = sizes
    mx, my = lax.axis_index("mx"), lax.axis_index("my")
    loads = [
        pltpu.make_async_copy(source, ext_x.at[pl.ds(begin, size), pl.ds(3, cx)], load_sem.at[i])
        for i, (source, begin, size) in enumerate(
            [(density, 0, 1), (momentum, 1, 3), (energy, 4, 1), (entropy, 5, 1), (tracers, 6, nf - 6)]
        )
    ]
    px, py = lax.rem(mx, 2), lax.rem(my, 2)
    tables = {}
    for i, name in enumerate(names):
        source = held_tables[name]
        if name.startswith("second"):
            source = source.at[px * 2 + py]
        tables[name] = pltpu.make_async_copy(source, table[name], table_sem.at[i])
    for copy in loads:
        copy.start()
    for copy in tables.values():
        copy.start()

    def at_x(step):
        return (lax.rem(mx + step + count_x, count_x), my)

    def at_y(step):
        return (mx, lax.rem(my + step + count_y, count_y))

    barrier = pltpu.get_barrier_semaphore()
    for step in range(1, count_x):
        pl.semaphore_signal(barrier, inc=1, device_id=at_x(step), device_id_type=MESH)
    for step in range(1, count_y):
        pl.semaphore_signal(barrier, inc=1, device_id=at_y(step), device_id_type=MESH)
    for copy in loads:
        copy.wait()

    def remote(source, target, send, recv, device):
        return pltpu.make_async_remote_copy(
            src_ref=source, dst_ref=target, send_sem=send, recv_sem=recv,
            device_id=device, device_id_type=MESH,
        )

    def halo_pair(buffer, length, base, place):
        lower = remote(
            buffer.at[:, pl.ds(3, 3)], buffer.at[:, pl.ds(length + 3, 3)],
            halo_send.at[base], halo_recv.at[base], place(-1),
        )
        upper = remote(
            buffer.at[:, pl.ds(length, 3)], buffer.at[:, pl.ds(0, 3)],
            halo_send.at[base + 1], halo_recv.at[base + 1], place(1),
        )
        return lower, upper

    def start_halo(pair, position, count):
        @pl.when(position > 0)
        def _():
            pair[0].start()

        @pl.when(position < count - 1)
        def _():
            pair[1].start()

    def finish_halo(pair, buffer, length, position, count):
        @pl.when(position > 0)
        def _():
            pair[0].wait_send()
            pair[1].wait_recv()

        @pl.when(position < count - 1)
        def _():
            pair[1].wait_send()
            pair[0].wait_recv()

        @pl.when(position == 0)
        def _():
            for row in range(3):
                buffer[:, row] = buffer[:, 3]

        @pl.when(position == count - 1)
        def _():
            for row in range(3):
                buffer[:, length + 3 + row] = buffer[:, length + 2]

    pair_x = halo_pair(ext_x, cx, 0, at_x)
    pair_y = halo_pair(ext_y, cy, 2, at_y)

    def turn(rows):
        def one(field, carry):
            for row in rows:
                ext_y[field, 3 + row] = ext_x[field, pl.ds(3, cx), row, :]
            return carry

        lax.fori_loop(0, nf, one, 0)

    turn([*range(3), *range(cy - 3, cy)])
    pl.semaphore_wait(barrier, count_x + count_y - 2)
    start_halo(pair_y, my, count_y)
    start_halo(pair_x, mx, count_x)
    turn(range(3, cy - 3))

    planes = 4

    def cell_speed(step, best):
        rows = pl.ds(3 + step * planes, planes)
        inverse = 1.0 / ext_x[0, rows]
        largest = jnp.maximum(
            jnp.maximum(jnp.abs(ext_x[1, rows]), jnp.abs(ext_x[2, rows])), jnp.abs(ext_x[3, rows])
        )
        _, speed = sound(ext_x[5, rows], inverse)
        return jnp.maximum(best, jnp.max(largest * inverse + speed, axis=0))

    best = lax.fori_loop(0, cx // planes, cell_speed, jnp.zeros((cy, cz), jnp.float32))
    best = jnp.max(best)

    for name in names:
        if name in early_names:
            tables[name].wait()

    def pair_of(name, *at):
        low = name + "_lo"
        return [table[name + "_hi"][(*at, ...)], table[low][(*at, ...)] if low in names else None]

    flagged = product(
        jnp.concatenate(
            [
                jnp.broadcast_to(
                    flags[bx, by : by + 1, :].astype(jnp.float32), (SUB, flags.shape[2])
                )
                for bx in range(2)
                for by in range(2)
            ],
            axis=0,
        ).astype(jnp.bfloat16),
        table["flag_z"][...].astype(jnp.bfloat16),
    )
    for bx in range(2):
        rows = [ext_x[0, 3 + bx * SUB + i] for i in range(SUB)]
        for power in range(4):
            total = rows[0] * ((0.5 / SUB - 0.5) ** power)
            for i in range(1, SUB):
                total = total + rows[i] * (((i + 0.5) / SUB - 0.5) ** power)
            rows_p[pl.ds((bx * 4 + power) * 2 * SUB, 2 * SUB), :] = (
                total * flagged[bx * 2 * SUB : (bx + 1) * 2 * SUB]
            )
    weighted = times(rows_p[...].T, *pair_of("spread"))
    shifted = picked(table["cell_rows"][...], weighted * table["along_z"][...])

    def choose(stack, lanes):
        lane = lax.rem(lax.broadcasted_iota(jnp.int32, (8, lanes), 1), slot)
        total = jnp.zeros((8, lanes), jnp.float32)
        for sd in range(6):
            inside = (lane >= sd * count_m) & (lane < (sd + 1) * count_m)
            total = total + jnp.where(inside, stack[sd * 8 : sd * 8 + 8], 0.0)
        return total

    block = choose(shifted, 4 * slot)
    near[1, 1] = block
    first = times(block, *pair_of("pick_up"))
    tile = choose(picked(table["one_rows"][...], first), slot)
    lifted = times(first, *pair_of("second"))
    for dz in range(2):
        part = picked(
            table["two_rows"][dz * 48 : dz * 48 + 48], lifted[:, dz * slot : (dz + 1) * slot]
        )
        tile = tile + choose(part, slot)
    row_index = lax.broadcasted_iota(jnp.int32, (8, slot), 0)
    tiles[mx, my] = jnp.where(row_index == 7, best, tile)

    for step in range(1, count_x):
        remote(
            tiles.at[mx, my], tiles.at[mx, my],
            first_send.at[step], first_recv.at[step], at_x(step),
        ).start()
    side_x = (
        remote(near.at[1, 1], near.at[2, 1], side_send.at[0], side_recv.at[0], at_x(-1)),
        remote(near.at[1, 1], near.at[0, 1], side_send.at[1], side_recv.at[1], at_x(1)),
    )
    start_halo(side_x, mx, count_x)

    lane_z = lax.broadcasted_iota(jnp.int32, (cy, cz), 1)

    def pack(row, carry):
        mine = (lane_z >= row * 8) & (lane_z < row * 8 + 8)
        for field in range(nf):
            turned = pltpu.roll(ext_x[field, 3 + row], row * 8 + 3, 1)
            packed[field] = jnp.where(mine, turned, packed[field])
        return carry

    packed[...] = jnp.ones(packed.shape, jnp.float32)
    lax.fori_loop(0, cx, pack, 0)

    def end_stencil(field):
        value = packed[field]
        one = pltpu.roll(value, cz - 1, 1)
        two = pltpu.roll(value, cz - 2, 1)
        return value, one, two, two, two, two

    def end_emit(field, flux):
        packed_flux[field] = flux

    apply(prepare(end_stencil, 2), end_stencil, 2, nf, end_emit)

    def stencil_z(row):
        def stencil(field):
            value = ext_x[field, 3 + row]
            out = [value]
            for step in range(3):
                out.insert(0, jnp.where(lane_z < 1, value, pltpu.roll(out[0], 1, 1)))
            for step in range(2):
                out.append(jnp.where(lane_z == cz - 1, value, pltpu.roll(out[-1], cz - 1, 1)))
            return out

        return stencil

    def sweep_z(row, prepared):
        following = prepare(stencil_z(jnp.minimum(row + 1, cx - 1)), 2)

        def emit(field, flux):
            ending = pltpu.roll(packed_flux[field], cz - 1 - row * 8, 1)
            above = jnp.where(lane_z == cz - 1, ending, pltpu.roll(flux, cz - 1, 1))
            section[field, row] = above - flux

        apply(prepared, stencil_z(row), 2, nf, emit)
        return following

    lax.fori_loop(0, cx, sweep_z, prepare(stencil_z(0), 2))

    def finish_side(pair, position, count, low, high):
        @pl.when(position > 0)
        def _():
            pair[0].wait_send()
            pair[1].wait_recv()

        @pl.when(position < count - 1)
        def _():
            pair[1].wait_send()
            pair[0].wait_recv()

        @pl.when(position == 0)
        def _():
            low[...] = jnp.zeros(low.shape, jnp.float32)

        @pl.when(position == count - 1)
        def _():
            high[...] = jnp.zeros(high.shape, jnp.float32)

    for step in range(1, count_x):
        arrived = tiles.at[lax.rem(mx - step + count_x, count_x), my]
        copy = remote(arrived, arrived, first_send.at[step], first_recv.at[step], at_x(step))
        copy.wait_send()
        copy.wait_recv()
    finish_side(side_x, mx, count_x, near.at[0, 1], near.at[2, 1])
    for step in range(1, count_y):
        remote(
            tiles.at[:, my], tiles.at[:, my], second_send.at[step], second_recv.at[step], at_y(step)
        ).start()
    side_y = (
        remote(near.at[:, 1], near.at[:, 2], side_send.at[2], side_recv.at[2], at_y(-1)),
        remote(near.at[:, 1], near.at[:, 0], side_send.at[3], side_recv.at[3], at_y(1)),
    )
    start_halo(side_y, my, count_y)


    def sweep(buffer, length, direction, store):
        def stencil_at(face):
            return lambda field: [buffer[field, face + i] for i in range(6)]

        def start_emit(field, flux):
            previous[field] = flux

        apply(prepare(stencil_at(0), direction), stencil_at(0), direction, nf, start_emit)

        def body(cell, prepared):
            following = prepare(stencil_at(jnp.minimum(cell + 2, length)), direction)

            def emit(field, flux):
                store(field, cell, flux - previous[field])
                previous[field] = flux

            apply(prepared, stencil_at(cell + 1), direction, nf, emit)
            return following

        lax.fori_loop(0, length, body, prepare(stencil_at(1), direction))

    finish_halo(pair_x, ext_x, cx, mx, count_x)

    def store_x(field, cell, value):
        section[field, cell] = section[field, cell] + value

    sweep(ext_x, cx, 0, store_x)

    finish_halo(pair_y, ext_y, cy, my, count_y)

    def store_y(field, cell, value):
        moved[field, cell] = value

    sweep(ext_y, cy, 1, store_y)

    for step in range(1, count_y):
        arrived = tiles.at[:, lax.rem(my - step + count_y, count_y)]
        copy = remote(arrived, arrived, second_send.at[step], second_recv.at[step], at_y(step))
        copy.wait_send()
        copy.wait_recv()
    finish_side(side_y, my, count_y, near.at[:, 0], near.at[:, 2])

    fastest = jnp.max(jnp.max(tiles[...], axis=(0, 1))[7:8, :])
    step_size = courant / (SUB * jnp.full((1, cz), fastest, jnp.float32))

    one_x, one_y = mx // 2, my // 2
    two_x, two_y = mx // 4, my // 4

    def united(ux, uy):
        return (
            tiles[2 * ux, 2 * uy] + tiles[2 * ux, 2 * uy + 1]
            + tiles[2 * ux + 1, 2 * uy] + tiles[2 * ux + 1, 2 * uy + 1]
        )

    def held(value, count):
        return jnp.clip(value, 0, count - 1), (value >= 0) & (value < count)

    for dx in range(3):
        for dy in range(3):
            base = (dx * 3 + dy) * 4 * slot
            window[0:8, base : base + 4 * slot] = near[dx, dy]
            for bx in range(2):
                for by in range(2):
                    at = base + (bx * 2 + by) * slot
                    gx, in_x = held(2 * (one_x + dx - 1) + bx, count_x)
                    gy, in_y = held(2 * (one_y + dy - 1) + by, count_y)
                    ux, in_ux = held(2 * (two_x + dx - 1) + bx, count_x // 2)
                    uy, in_uy = held(2 * (two_y + dy - 1) + by, count_y // 2)
                    own = jnp.where(in_x & in_y, tiles[gx, gy], 0.0)
                    joint = jnp.where(in_ux & in_uy, united(ux, uy), 0.0)
                    window[8:16, at : at + slot] = jnp.where(
                        row_index < 4, own, jnp.where(row_index < 6, joint, 0.0)
                    )

    for name in names:
        if name not in early_names:
            tables[name].wait()

    keep = (lax.broadcasted_iota(jnp.int32, (16, wide), 0) < 8).astype(jnp.float32)
    middle_chunks = 36 * slot // wide
    chunks = middle_chunks + len(inner_columns) * slot // wide
    for index in range(chunks):
        if index < middle_chunks:
            value = window[:, index * wide : (index + 1) * wide]
        else:
            pair = inner_columns[2 * (index - middle_chunks) :][:2]
            value = keep * jnp.concatenate(
                [window[:, column * slot : (column + 1) * slot] for column in pair], axis=1
            )
        high, low = halves(value)
        splits[index, 0:16] = high
        splits[index, 16:32] = low

    upper = jnp.zeros((32, wide), jnp.float32)
    lower = jnp.zeros((16, wide), jnp.float32)
    for index in range(chunks):
        both = splits[index]
        upper = upper + product(both, table["window_hi"][index])
        lower = lower + product(both[:16], table["window_lo"][index])
    sums = (upper[:16] + upper[16:] + lower) * table["scale"][...]


    def select(values, which):
        total = jnp.zeros((values.shape[0], 64), jnp.float32)
        for child in range(4):
            total = total + jnp.where(which == child, values[:, child * 64 : child * 64 + 64], 0.0)
        return total

    lane_64 = lax.broadcasted_iota(jnp.int32, (8, 64), 1)
    same_half = (lane_64 >= 32) == (lax.rem(lax.broadcasted_iota(jnp.int32, (8, 64), 0), 2) == 1)
    which_two = lax.rem(one_x, 2) * 2 + lax.rem(one_y, 2)
    second_sum = select(sums, which_two)
    if top:
        nx3, ny3 = count_x // 4, count_y // 4
        grown = jnp.zeros((8, slot), jnp.float32)
        for sx in range(nx3):
            for sy in range(ny3):
                source = jnp.zeros((8, slot), jnp.float32)
                for bx in range(2):
                    for by in range(2):
                        source = source + wholly(
                            united(2 * sx + bx, 2 * sy + by), table["raise_up"][bx * 2 + by]
                        )
                source = jnp.where((row_index == 4) | (row_index == 5), source, 0.0)
                place = ((sx - two_x + nx3 - 1) * (2 * ny3 - 1) + (sy - two_y + ny3 - 1)) * 3
                for dz in range(3):
                    moved_rows = source if dz == 1 else pltpu.roll(source, 1 if dz == 0 else 7, 0)
                    grown = grown + wholly(moved_rows, table["far"][place + dz])
        grown = jnp.where((row_index == 4) | (row_index == 5), grown, 0.0)
        carried = wholly(grown, table["lower_down"][which_two])
        second_sum = second_sum + jnp.concatenate([jnp.zeros((8, 64), jnp.float32), carried], axis=0)
    from_two = jnp.where(same_half, picked(table["take_two"][...], second_sum), 0.0)
    which_one = px * 2 + py
    first_sum = picked(table["take_one"][...], select(sums, which_one)) + times(
        from_two, *pair_of("down_two", which_one)
    )
    from_one = jnp.where(same_half, picked(table["take_zero"][...], first_sum), 0.0)
    expansion = sums[0:8] + times(from_one, *pair_of("down_one"))
    turned_hi, turned_lo = halves(expansion.T)
    to_z = table["to_z"][...].astype(jnp.bfloat16)
    on_z = product(turned_hi, to_z) + product(turned_lo, to_z)
    pieces = []
    for which, first_row, last_row in ((0, 0, 192), (1, 192, 288)):
        high, low = halves(on_z * table["weights"][which])
        field_hi = table["fields_hi"][first_row:last_row]
        piece = product(field_hi, high) + product(field_hi, low)
        if "fields_lo" in names:
            piece = piece + product(table["fields_lo"][first_row:last_row], high)
        pieces.append(piece)
    for k in range(3):
        parts = pieces[0][k * 96 : k * 96 + 96] if k < 2 else pieces[1]
        for row in range(cx):
            bx, height = row // SUB, (row % SUB + 0.5) / SUB - 0.5
            base = bx * 6 * SUB
            accel[k, row] = (
                parts[base : base + 2 * SUB]
                + height * parts[base + 2 * SUB : base + 4 * SUB]
                + (height * height) * parts[base + 4 * SUB : base + 6 * SUB]
            )

    def finish(cell, carry):
        own = [ext_x[field, 3 + cell] for field in range(4)]
        pull = [accel[k, cell] for k in range(3)]
        for field in range(nf):
            total = (section[field, cell] + moved[field, :, cell, :]) * (-float(SUB))
            if 1 <= field <= 3:
                total = total + own[0] * pull[field - 1]
            if field == 4:
                total = total + own[1] * pull[0] + own[2] * pull[1] + own[3] * pull[2]
            section[field, cell] = ext_x[field, 3 + cell] + step_size * total
        return carry

    leaving = [pltpu.make_async_copy(accel, accel_out, out_sem.at[4])]
    leaving[0].start()
    for quarter in range(4):
        begin = quarter * cx // 4
        lax.fori_loop(begin, begin + cx // 4, finish, 0)
        planes_out = pl.ds(begin, cx // 4)
        leaving.append(
            pltpu.make_async_copy(
                section.at[:, planes_out], section_out.at[:, planes_out], out_sem.at[quarter]
            )
        )
        leaving[-1].start()
    for copy in leaving:
        copy.wait()


def hand_over_kernel(section, accel, section_out, accel_out, staged, in_sem, out_sem):
    count = section.shape[0]
    pieces = [(section.at[i], section_out.at[i]) for i in range(count)]
    pieces += [(accel.at[i], accel_out.at[i]) for i in range(accel.shape[0])]
    arriving = [
        pltpu.make_async_copy(source, staged.at[i], in_sem.at[i])
        for i, (source, _) in enumerate(pieces)
    ]
    leaving = [
        pltpu.make_async_copy(staged.at[i], target, out_sem.at[i])
        for i, (_, target) in enumerate(pieces)
    ]
    for copy in arriving:
        copy.start()
    for before, after in zip(arriving, leaving):
        before.wait()
        after.start()
    for copy in leaving:
        copy.wait()


def shards(density, momentum, energy, entropy, tracers, leaf_flags):
    count_x, count_y = lax.axis_size("mx"), lax.axis_size("my")
    cx, cy, cz = density.shape
    nf = 6 + tracers.shape[0]
    middle, close = window_tables()
    top, raise_up, lower_down, far = top_tables(count_x // 4, count_y // 4)
    spread, along_z, cell_rows, pick_up, one_rows, second, two_rows, flag_z = moment_tables(cz)
    scale, down_two, down_one, take_one, take_two, take_zero, to_z, weights, fields = down_tables(cz)
    constants = {}
    for name, array in (("flag_z", flag_z), ("cell_rows", cell_rows), ("along_z", along_z)):
        constants[name] = jnp.asarray(array, jnp.float32)
    for name, array in (("spread", spread), ("pick_up", pick_up), ("second", second)):
        for ending, part in split_pair(array):
            constants[name + ending] = jnp.asarray(part)
    for name, array in (("one_rows", one_rows), ("two_rows", two_rows)):
        constants[name] = jnp.asarray(array, jnp.float32)
    joined = np.concatenate([middle, close]).reshape(-1, wide, wide)
    for name, array in (
        ("window", joined), ("down_two", down_two), ("down_one", down_one),
        ("fields", fields.reshape(-1, wide)),
    ):
        for ending, part in split_pair(array):
            constants[name + ending] = jnp.asarray(part)
    for name, array in (
        ("scale", scale), ("take_one", take_one), ("take_two", take_two),
        ("take_zero", take_zero), ("to_z", to_z), ("weights", weights),
    ):
        constants[name] = jnp.asarray(array, jnp.float32)
    if top:
        for name, array in (("raise_up", raise_up), ("lower_down", lower_down), ("far", far)):
            constants[name] = jnp.asarray(array, jnp.float32)
    names = tuple(constants)
    shapes = [
        pltpu.VMEM(
            array.shape[1:] if name.startswith("second") else array.shape, array.dtype
        )
        for name, array in constants.items()
    ]
    anywhere = pl.BlockSpec(memory_space=pl.ANY)
    local = pl.BlockSpec(memory_space=pltpu.VMEM)
    dma = pltpu.SemaphoreType.DMA
    f32 = jnp.float32
    out_shape = (
        jax.ShapeDtypeStruct((nf, cx, cy, cz), f32),
        jax.ShapeDtypeStruct((3, cx, cy, cz), f32),
    )
    results = pl.pallas_call(
        functools.partial(section_kernel, (count_x, count_y, nf, cx, cy, cz), top, names),
        out_shape=out_shape,
        in_specs=[anywhere] * 5 + [local] + [anywhere] * len(names),
        out_specs=(anywhere, anywhere),
        scratch_shapes=shapes
        + [
            pltpu.VMEM((nf, cx + 6, cy, cz), f32),
            pltpu.VMEM((nf, cy + 6, cx, cz), f32),
            pltpu.VMEM((nf, cy, cx, cz), f32),
            pltpu.VMEM((nf, cy, cz), f32),
            pltpu.VMEM((nf, cy, cz), f32),
            pltpu.VMEM((nf, cy, cz), f32),
            pltpu.VMEM((count_x, count_y, 8, slot), f32),
            pltpu.VMEM((3, 3, 8, 4 * slot), f32),
            pltpu.VMEM((16, 36 * slot), f32),
            pltpu.VMEM((128, cz), f32),
            pltpu.VMEM((joined.shape[0], 32, wide), jnp.bfloat16),
            pltpu.VMEM((nf, cx, cy, cz), f32),
            pltpu.VMEM((3, cx, cy, cz), f32),
            dma((5,)),
            dma((5,)), dma((len(names),)), dma((4,)), dma((4,)),
            dma((count_x,)), dma((count_x,)), dma((count_y,)), dma((count_y,)),
            dma((4,)), dma((4,)),
        ],
        compiler_params=pltpu.CompilerParams(
            collective_id=0, has_side_effects=True, vmem_limit_bytes=56 * 1024 * 1024
        ),
    )(density[None], momentum, energy[None], entropy[None], tracers, leaf_flags, *constants.values())
    return pl.pallas_call(
        hand_over_kernel,
        out_shape=out_shape,
        in_specs=[anywhere] * 2,
        out_specs=(anywhere, anywhere),
        scratch_shapes=[pltpu.VMEM((nf + 3, cx, cy, cz), f32), dma((nf + 3,)), dma((nf + 3,))],
    )(*results)


def solution(mesh):
    placed = (
        P("mx", "my", None),
        P(None, "mx", "my", None),
        P("mx", "my", None),
        P("mx", "my", None),
        P(None, "mx", "my", None),
        P("mx", "my", None),
    )
    return jax.shard_map(
        shards,
        mesh=mesh,
        in_specs=placed,
        out_specs=(P(None, "mx", "my", None), P(None, "mx", "my", None)),
        check_vma=False,
    )
```

```python
import functools
import math

import jax
import jax.numpy as jnp
import numpy as np
from jax import lax
from jax.experimental import pallas as pl
from jax.experimental.pallas import tpu as pltpu
from jax.sharding import PartitionSpec as P

MESH = pl.DeviceIdType.MESH
SUB = 8
LEVELS = 3


gamma_gas = 5.0 / 3.0
courant = 0.3
gravity = 0.02
highest = lax.Precision.HIGHEST
multi_index = [
    (power_x, power_y, degree_sum - power_x - power_y)
    for degree_sum in range(4)
    for power_x in range(degree_sum, -1, -1)
    for power_y in range(degree_sum - power_x, -1, -1)
]


def factorial_of(exponent):
    return math.factorial(exponent[0]) * math.factorial(exponent[1]) * math.factorial(exponent[2])


def inverse_derivative(exponent, vectors):
    axes_list = [0] * exponent[0] + [1] * exponent[1] + [2] * exponent[2]
    radius = np.sqrt(np.sum(vectors * vectors, axis=1))
    radius_safe = np.where(radius > 0.0, radius, 1.0)
    degree = len(axes_list)
    if degree == 0:
        result = 1.0 / radius_safe
    elif degree == 1:
        result = -vectors[:, axes_list[0]] / radius_safe**3
    elif degree == 2:
        index_one, index_two = axes_list
        result = (
            3.0 * vectors[:, index_one] * vectors[:, index_two] / radius_safe**5
            - float(index_one == index_two) / radius_safe**3
        )
    else:
        index_one, index_two, index_three = axes_list
        crossed = (
            float(index_one == index_two) * vectors[:, index_three]
            + float(index_one == index_three) * vectors[:, index_two]
            + float(index_two == index_three) * vectors[:, index_one]
        )
        result = (
            -15.0
            * vectors[:, index_one]
            * vectors[:, index_two]
            * vectors[:, index_three]
            / radius_safe**7
            + 3.0 * crossed / radius_safe**5
        )
    return np.where(radius > 0.0, result, 0.0)


def offset_grid(reach_x, reach_y, reach_z):
    return [
        (shift_x, shift_y, shift_z)
        for shift_x in range(-reach_x, reach_x + 1)
        for shift_y in range(-reach_y, reach_y + 1)
        for shift_z in range(-reach_z, reach_z + 1)
    ]


def translation_kernel(spacing, offsets):
    vectors = np.asarray(offsets) * (-1.0 * spacing)
    entries = np.zeros((len(offsets), len(multi_index), len(multi_index)))
    for row_index, target_power in enumerate(multi_index):
        for column_index, source_power in enumerate(multi_index):
            if sum(target_power) + sum(source_power) <= 3:
                joined = (
                    target_power[0] + source_power[0],
                    target_power[1] + source_power[1],
                    target_power[2] + source_power[2],
                )
                entries[:, row_index, column_index] = (
                    -gravity
                    * (-1.0) ** sum(source_power)
                    / factorial_of(source_power)
                    * inverse_derivative(joined, vectors)
                )
    return entries.astype(np.float32)


def upward_matrices(spacing):
    entries = np.zeros((2, 2, 2, len(multi_index), len(multi_index)))
    for octant in range(8):
        octant_bits = (octant >> 2 & 1, octant >> 1 & 1, octant & 1)
        displacement = [(octant_bits[dimension] - 0.5) * spacing for dimension in range(3)]
        for row_index, target_power in enumerate(multi_index):
            for column_index, source_power in enumerate(multi_index):
                if all(
                    (source_power[dimension] <= target_power[dimension] for dimension in range(3))
                ):
                    entry_value = 1.0
                    for dimension in range(3):
                        entry_value *= math.comb(
                            target_power[dimension], source_power[dimension]
                        ) * displacement[dimension] ** (
                            target_power[dimension] - source_power[dimension]
                        )
                    entries[
                        octant_bits[0], octant_bits[1], octant_bits[2], row_index, column_index
                    ] = entry_value
    return entries.astype(np.float32)


def downward_matrices(spacing):
    entries = np.zeros((2, 2, 2, len(multi_index), len(multi_index)))
    for octant in range(8):
        octant_bits = (octant >> 2 & 1, octant >> 1 & 1, octant & 1)
        displacement = [(octant_bits[dimension] - 0.5) * spacing for dimension in range(3)]
        for row_index, target_power in enumerate(multi_index):
            for column_index, source_power in enumerate(multi_index):
                if all(
                    (source_power[dimension] >= target_power[dimension] for dimension in range(3))
                ):
                    entry_value = 1.0
                    for dimension in range(3):
                        lifted = source_power[dimension] - target_power[dimension]
                        entry_value *= displacement[dimension] ** lifted / math.factorial(lifted)
                    entries[
                        octant_bits[0], octant_bits[1], octant_bits[2], row_index, column_index
                    ] = entry_value
    return entries.astype(np.float32)


slot = 128
wide = 256
count_m = len(multi_index)
degrees = np.array([sum(exponent) for exponent in multi_index])
inner_columns = [
    (dx * 3 + dy) * 4 + bx * 2 + by
    for dx in range(3)
    for dy in range(3)
    for bx in range(2)
    for by in range(2)
    if 1 <= 2 * dx + bx <= 4 and 1 <= 2 * dy + by <= 4
]


early_names = (
    "flag_z", "cell_rows", "along_z", "spread_hi", "spread_lo", "pick_up_hi", "pick_up_lo",
    "second_hi", "second_lo", "one_rows", "two_rows",
)


def split_pair(table):
    table = np.asarray(table, np.float32)
    high = table.astype(jnp.bfloat16)
    low = (table - high.astype(np.float32)).astype(jnp.bfloat16)
    return [("_hi", high)] + ([("_lo", low)] if np.any(low.astype(np.float32)) else [])


def window_tables():
    columns = [
        (2 * dx - 2 + bx, 2 * dy - 2 + by)
        for dx in range(3)
        for dy in range(3)
        for bx in range(2)
        for by in range(2)
    ]
    children = [(i >> 2 & 1, i >> 1 & 1, i & 1) for i in range(8)]
    sources = [(cx, cy, sz - 2) for cx, cy in columns for sz in range(6)]
    offsets = np.array([[[s[k] - t[k] for k in range(3)] for t in children] for s in sources])
    kernels = np.asarray(translation_kernel(1.0, offsets.reshape(-1, 3)), np.float64)
    kernels = kernels.reshape(36, 6, 8, count_m, count_m)
    touching = (np.abs(offsets).max(axis=2) <= 1).reshape(36, 6, 8, 1, 1)

    def laid(part):
        out = np.zeros((36, slot, 8, 32))
        out[:, : 6 * count_m, :, :count_m] = part.transpose(0, 1, 4, 2, 3).reshape(
            36, 6 * count_m, 8, count_m
        )
        return out.reshape(36, slot, wide)

    middle = laid(np.where(touching, 0.0, kernels))
    close = laid(np.where(touching, kernels, 0.0))[np.array(inner_columns)]
    return middle.reshape(-1, wide), close.reshape(-1, wide)


def moment_tables(cells_z):
    centres = (np.arange(SUB) + 0.5) / SUB - 0.5
    spread = np.zeros((2, 4, 2, SUB, 4, slot))
    along_z = np.zeros((cells_z, 4, slot))
    pick_up = np.zeros((4, slot, slot))
    lift = np.asarray(upward_matrices(1.0), np.float64)
    lift_two = np.asarray(upward_matrices(2.0), np.float64)
    second = np.zeros((4, slot, 2 * slot))
    for sd in range(6):
        for index, power in enumerate(multi_index):
            lane = sd * count_m + index
            for bx in range(2):
                for by in range(2):
                    spread[bx, power[0], by, :, bx * 2 + by, lane] = (
                        centres ** power[1] / SUB**3
                    )
            along_z[:, :, lane] = (np.tile(centres, cells_z // SUB) ** power[2])[:, None]
            for bx in range(2):
                for by in range(2):
                    for dz in range(2):
                        for lower in range(count_m):
                            pick_up[bx * 2 + by, (2 + dz) * count_m + lower, lane] = (
                                lift[bx, by, dz, index, lower] * 0.5 ** sum(power)
                            )
                            second[bx * 2 + by, lower, dz * slot + lane] = (
                                lift_two[bx, by, dz, index, lower]
                                * 2.0 ** degrees[lower]
                                * 0.25 ** sum(power)
                            )
    parents = cells_z // SUB // 2
    rows = np.arange(8)
    cell_rows = np.zeros((6, 8, cells_z))
    one_rows = np.zeros((6, 8, 8))
    two_rows = np.zeros((2, 6, 8, 8))
    for s in range(3):
        for dz in range(2):
            sd = s * 2 + dz
            for row in rows:
                cell_rows[sd, row] = np.arange(cells_z) // SUB == 2 * (row + s - 1) + dz
                if row < parents // 2:
                    one_rows[sd, row] = rows == 2 * (row + s - 1) + dz
                if 4 <= row < 4 + parents // 4:
                    second_z = 2 * (row - 4 + s - 1) + dz
                    if 0 <= second_z < parents // 2:
                        for dz_one in range(2):
                            two_rows[dz_one, sd, row] = rows == 2 * second_z + dz_one
    return (
        spread.reshape(128, 4 * slot),
        along_z.reshape(cells_z, 4 * slot),
        cell_rows.reshape(48, cells_z),
        pick_up.reshape(4 * slot, slot),
        one_rows.reshape(48, 8),
        second,
        two_rows.reshape(96, 8),
        (np.arange(cells_z)[None, :] // SUB == np.arange(cells_z // SUB)[:, None]).astype(float),
    )


def down_tables(cells_z):
    def stacked(spacing):
        down = np.asarray(downward_matrices(spacing), np.float64)
        out = np.zeros((2, 2, 2, 32, 2, 32))
        for bz in range(2):
            for child in range(2):
                out[:, :, bz, :count_m, child, :count_m] = down[:, :, child].transpose(0, 1, 3, 2)
        return out

    scale = np.zeros((16, 8, 32))
    scale[:8, :, :count_m] = 1.0
    scale[8:12, :, :count_m] = 0.5 ** (degrees + 1)
    scale[12:14, :, :count_m] = 0.25 ** (degrees + 1)
    near = stacked(1.0)
    near = near.transpose(2, 3, 0, 1, 4, 5).reshape(64, wide)
    rows = np.arange(8)
    take_one = (np.arange(16)[None, :] == 8 + rows[:, None]) & (rows[:, None] < 4)
    take_two = (np.arange(16)[None, :] == 12 + rows[:, None] // 2) & (rows[:, None] < 4)
    take_zero = np.arange(8)[None, :] == rows[:, None] // 2
    centres = (np.arange(SUB) + 0.5) / SUB - 0.5
    to_z = np.arange(cells_z)[None, :] // (2 * SUB) == rows[:, None]
    heights = np.tile(centres, cells_z // SUB)
    bz_of = np.arange(cells_z) // SUB % 2
    weights = np.zeros((2, 2, 2, 2, 32, cells_z))
    fields = np.zeros((3, 2, 3, 2, SUB, 2, 2, 2, 32))
    for index, power in enumerate(multi_index):
        for bz in range(2):
            weights[0, :, :, bz, index] = (bz_of == bz) * heights ** power[2]
            if power[2] > 0:
                weights[1, :, :, bz, index] = (bz_of == bz) * heights ** (power[2] - 1)
        for k in range(3):
            if power[k] > 0:
                lowered = list(power)
                lowered[k] -= 1
                for bx in range(2):
                    for by in range(2):
                        fields[k, bx, lowered[0], by, :, bx, by, :, index] = (
                            -power[k] / factorial_of(power) * centres ** lowered[1]
                        )[:, None]
    return (
        scale.reshape(16, wide),
        stacked(2.0).reshape(4, 64, 64),
        near,
        take_one.astype(float),
        take_two.astype(float),
        take_zero.astype(float),
        to_z.astype(float),
        weights.reshape(2, wide, cells_z),
        fields.reshape(3, 96, wide),
    )


def top_tables(nx, ny):
    lift = np.asarray(upward_matrices(4.0), np.float64)
    raise_up = np.zeros((4, slot, slot))
    lower_down = np.zeros((4, slot, 64))
    down = np.asarray(downward_matrices(4.0), np.float64)
    for bx in range(2):
        for by in range(2):
            for dz in range(2):
                raise_up[bx * 2 + by, (2 + dz) * count_m : (3 + dz) * count_m, :count_m] = (
                    lift[bx, by, dz] * 4.0 ** degrees[None, :]
                ).T
                lower_down[bx * 2 + by, :count_m, dz * 32 : dz * 32 + count_m] = down[bx, by, dz].T
    offsets = np.array(offset_grid(nx - 1, ny - 1, 1))
    kernels = np.asarray(translation_kernel(8.0, offsets), np.float64)
    counting = np.abs(offsets).max(axis=1) > 1
    far = np.zeros((len(offsets), slot, slot))
    far[:, :count_m, :count_m] = (kernels * counting[:, None, None]).transpose(0, 2, 1)
    return bool(counting.any()), raise_up, lower_down, far


def halves(value):
    high = value.astype(jnp.bfloat16)
    return high, (value - high.astype(jnp.float32)).astype(jnp.bfloat16)


def product(left, right):
    return jnp.dot(left, right, preferred_element_type=jnp.float32)


def times(value, table_hi, table_lo):
    high, low = halves(value)
    size = value.shape[0]
    both = product(jnp.concatenate([high, low], axis=0), table_hi)
    both = both[:size] + both[size:]
    return both if table_lo is None else both + product(high, table_lo)


def wholly(left, right):
    return jnp.dot(left, right, precision=highest, preferred_element_type=jnp.float32)


def picked(zero_one, value):
    high, low = halves(value)
    pick = zero_one.astype(jnp.bfloat16)
    return product(pick, high) + product(pick, low)


def sound(entropy, inverse):
    pressure = (gamma_gas - 1.0) * jnp.exp(gamma_gas * jnp.log(entropy))
    return pressure, jnp.sqrt(gamma_gas * pressure * inverse)


def states_of(stencil):
    a, b, c, d, e, f = stencil
    interface = (37.0 / 60.0) * (c + d) - (8.0 / 60.0) * (b + e) + (1.0 / 60.0) * (a + f)
    low, high = jnp.minimum(c, d), jnp.maximum(c, d)
    left = jnp.minimum(jnp.maximum(interface, jnp.minimum(b, low)), jnp.maximum(b, high))
    right = jnp.minimum(jnp.maximum(interface, jnp.minimum(e, low)), jnp.maximum(e, high))
    return left, right


def prepare(stencil_of, direction):
    mass = states_of(stencil_of(0))
    push = states_of(stencil_of(1 + direction))
    heat = states_of(stencil_of(5))
    inverse = [1.0 / value for value in mass]
    speed = [push[i] * inverse[i] for i in range(2)]
    gas = [sound(heat[i], inverse[i]) for i in range(2)]
    fastest = jnp.maximum(jnp.abs(speed[0]) + gas[0][1], jnp.abs(speed[1]) + gas[1][1])
    weights = 0.5 * (speed[0] + fastest), 0.5 * (speed[1] - fastest)
    flux = [left * weights[0] + right * weights[1] for left, right in (mass, push, heat)]
    flux[1] = flux[1] + 0.5 * (gas[0][0] + gas[1][0])
    work = 0.5 * (gas[0][0] * speed[0] + gas[1][0] * speed[1])
    return (*flux, *weights, work)


def apply(prepared, stencil_of, direction, count_fields, emit):
    known = dict(zip((0, 1 + direction, 5), prepared[:3]))
    for field in range(count_fields):
        if field in known:
            emit(field, known[field])
            continue
        left, right = states_of(stencil_of(field))
        flux = left * prepared[3] + right * prepared[4]
        emit(field, flux + prepared[5] if field == 4 else flux)


def section_kernel(
    sizes, top, names, density, momentum, energy, entropy, tracers, flags, *rest
):
    held_tables = dict(zip(names, rest[: len(names)]))
    section_out, accel_out = rest[len(names) : len(names) + 2]
    table = dict(zip(names, rest[len(names) + 2 : 2 * len(names) + 2]))
    (
        ext_x, ext_y, moved, previous, packed, packed_flux, tiles, near, window, rows_p, splits,
        section, accel, out_sem,
        load_sem, table_sem, halo_send, halo_recv, first_send, first_recv,
        second_send, second_recv, side_send, side_recv,
    ) = rest[2 * len(names) + 2 :]
    count_x, count_y, nf, cx, cy, cz = sizes
    mx, my = lax.axis_index("mx"), lax.axis_index("my")
    loads = [
        pltpu.make_async_copy(source, ext_x.at[pl.ds(begin, size), pl.ds(3, cx)], load_sem.at[i])
        for i, (source, begin, size) in enumerate(
            [(density, 0, 1), (momentum, 1, 3), (energy, 4, 1), (entropy, 5, 1), (tracers, 6, nf - 6)]
        )
    ]
    px, py = lax.rem(mx, 2), lax.rem(my, 2)
    tables = {}
    for i, name in enumerate(names):
        source = held_tables[name]
        if name.startswith("second"):
            source = source.at[px * 2 + py]
        tables[name] = pltpu.make_async_copy(source, table[name], table_sem.at[i])
    for copy in loads:
        copy.start()
    for copy in tables.values():
        copy.start()

    def at_x(step):
        return (lax.rem(mx + step + count_x, count_x), my)

    def at_y(step):
        return (mx, lax.rem(my + step + count_y, count_y))

    barrier = pltpu.get_barrier_semaphore()
    for step in range(1, count_x):
        pl.semaphore_signal(barrier, inc=1, device_id=at_x(step), device_id_type=MESH)
    for step in range(1, count_y):
        pl.semaphore_signal(barrier, inc=1, device_id=at_y(step), device_id_type=MESH)
    for copy in loads:
        copy.wait()

    def remote(source, target, send, recv, device):
        return pltpu.make_async_remote_copy(
            src_ref=source, dst_ref=target, send_sem=send, recv_sem=recv,
            device_id=device, device_id_type=MESH,
        )

    def halo_pair(buffer, length, base, place):
        lower = remote(
            buffer.at[:, pl.ds(3, 3)], buffer.at[:, pl.ds(length + 3, 3)],
            halo_send.at[base], halo_recv.at[base], place(-1),
        )
        upper = remote(
            buffer.at[:, pl.ds(length, 3)], buffer.at[:, pl.ds(0, 3)],
            halo_send.at[base + 1], halo_recv.at[base + 1], place(1),
        )
        return lower, upper

    def start_halo(pair, position, count):
        @pl.when(position > 0)
        def _():
            pair[0].start()

        @pl.when(position < count - 1)
        def _():
            pair[1].start()

    def finish_halo(pair, buffer, length, position, count):
        @pl.when(position > 0)
        def _():
            pair[0].wait_send()
            pair[1].wait_recv()

        @pl.when(position < count - 1)
        def _():
            pair[1].wait_send()
            pair[0].wait_recv()

        @pl.when(position == 0)
        def _():
            for row in range(3):
                buffer[:, row] = buffer[:, 3]

        @pl.when(position == count - 1)
        def _():
            for row in range(3):
                buffer[:, length + 3 + row] = buffer[:, length + 2]

    pair_x = halo_pair(ext_x, cx, 0, at_x)
    pair_y = halo_pair(ext_y, cy, 2, at_y)

    def turn(rows):
        def one(field, carry):
            for row in rows:
                ext_y[field, 3 + row] = ext_x[field, pl.ds(3, cx), row, :]
            return carry

        lax.fori_loop(0, nf, one, 0)

    turn([*range(3), *range(cy - 3, cy)])
    pl.semaphore_wait(barrier, count_x + count_y - 2)
    start_halo(pair_y, my, count_y)
    start_halo(pair_x, mx, count_x)
    turn(range(3, cy - 3))

    planes = 4

    def cell_speed(step, best):
        rows = pl.ds(3 + step * planes, planes)
        inverse = 1.0 / ext_x[0, rows]
        largest = jnp.maximum(
            jnp.maximum(jnp.abs(ext_x[1, rows]), jnp.abs(ext_x[2, rows])), jnp.abs(ext_x[3, rows])
        )
        _, speed = sound(ext_x[5, rows], inverse)
        return jnp.maximum(best, jnp.max(largest * inverse + speed, axis=0))

    best = lax.fori_loop(0, cx // planes, cell_speed, jnp.zeros((cy, cz), jnp.float32))
    best = jnp.max(best)

    for name in names:
        if name in early_names:
            tables[name].wait()

    def pair_of(name, *at):
        low = name + "_lo"
        return [table[name + "_hi"][(*at, ...)], table[low][(*at, ...)] if low in names else None]

    flagged = product(
        jnp.concatenate(
            [
                jnp.broadcast_to(
                    flags[bx, by : by + 1, :].astype(jnp.float32), (SUB, flags.shape[2])
                )
                for bx in range(2)
                for by in range(2)
            ],
            axis=0,
        ).astype(jnp.bfloat16),
        table["flag_z"][...].astype(jnp.bfloat16),
    )
    for bx in range(2):
        rows = [ext_x[0, 3 + bx * SUB + i] for i in range(SUB)]
        for power in range(4):
            total = rows[0] * ((0.5 / SUB - 0.5) ** power)
            for i in range(1, SUB):
                total = total + rows[i] * (((i + 0.5) / SUB - 0.5) ** power)
            rows_p[pl.ds((bx * 4 + power) * 2 * SUB, 2 * SUB), :] = (
                total * flagged[bx * 2 * SUB : (bx + 1) * 2 * SUB]
            )
    weighted = times(rows_p[...].T, *pair_of("spread"))
    shifted = picked(table["cell_rows"][...], weighted * table["along_z"][...])

    def choose(stack, lanes):
        lane = lax.rem(lax.broadcasted_iota(jnp.int32, (8, lanes), 1), slot)
        total = jnp.zeros((8, lanes), jnp.float32)
        for sd in range(6):
            inside = (lane >= sd * count_m) & (lane < (sd + 1) * count_m)
            total = total + jnp.where(inside, stack[sd * 8 : sd * 8 + 8], 0.0)
        return total

    block = choose(shifted, 4 * slot)
    near[1, 1] = block
    first = times(block, *pair_of("pick_up"))
    tile = choose(picked(table["one_rows"][...], first), slot)
    lifted = times(first, *pair_of("second"))
    for dz in range(2):
        part = picked(
            table["two_rows"][dz * 48 : dz * 48 + 48], lifted[:, dz * slot : (dz + 1) * slot]
        )
        tile = tile + choose(part, slot)
    row_index = lax.broadcasted_iota(jnp.int32, (8, slot), 0)
    tiles[mx, my] = jnp.where(row_index == 7, best, tile)

    for step in range(1, count_x):
        remote(
            tiles.at[mx, my], tiles.at[mx, my],
            first_send.at[step], first_recv.at[step], at_x(step),
        ).start()
    side_x = (
        remote(near.at[1, 1], near.at[2, 1], side_send.at[0], side_recv.at[0], at_x(-1)),
        remote(near.at[1, 1], near.at[0, 1], side_send.at[1], side_recv.at[1], at_x(1)),
    )
    start_halo(side_x, mx, count_x)

    lane_z = lax.broadcasted_iota(jnp.int32, (cy, cz), 1)

    def pack(row, carry):
        mine = (lane_z >= row * 8) & (lane_z < row * 8 + 8)
        for field in range(nf):
            turned = pltpu.roll(ext_x[field, 3 + row], row * 8 + 3, 1)
            packed[field] = jnp.where(mine, turned, packed[field])
        return carry

    packed[...] = jnp.ones(packed.shape, jnp.float32)
    lax.fori_loop(0, cx, pack, 0)

    def end_stencil(field):
        value = packed[field]
        one = pltpu.roll(value, cz - 1, 1)
        two = pltpu.roll(value, cz - 2, 1)
        return value, one, two, two, two, two

    def end_emit(field, flux):
        packed_flux[field] = flux

    apply(prepare(end_stencil, 2), end_stencil, 2, nf, end_emit)

    def stencil_z(row):
        def stencil(field):
            value = ext_x[field, 3 + row]
            out = [value]
            for step in range(3):
                out.insert(0, jnp.where(lane_z < 1, value, pltpu.roll(out[0], 1, 1)))
            for step in range(2):
                out.append(jnp.where(lane_z == cz - 1, value, pltpu.roll(out[-1], cz - 1, 1)))
            return out

        return stencil

    def sweep_z(row, prepared):
        following = prepare(stencil_z(jnp.minimum(row + 1, cx - 1)), 2)

        def emit(field, flux):
            ending = pltpu.roll(packed_flux[field], cz - 1 - row * 8, 1)
            above = jnp.where(lane_z == cz - 1, ending, pltpu.roll(flux, cz - 1, 1))
            section[field, row] = above - flux

        apply(prepared, stencil_z(row), 2, nf, emit)
        return following

    lax.fori_loop(0, cx, sweep_z, prepare(stencil_z(0), 2), unroll=2)

    def finish_side(pair, position, count, low, high):
        @pl.when(position > 0)
        def _():
            pair[0].wait_send()
            pair[1].wait_recv()

        @pl.when(position < count - 1)
        def _():
            pair[1].wait_send()
            pair[0].wait_recv()

        @pl.when(position == 0)
        def _():
            low[...] = jnp.zeros(low.shape, jnp.float32)

        @pl.when(position == count - 1)
        def _():
            high[...] = jnp.zeros(high.shape, jnp.float32)

    for step in range(1, count_x):
        arrived = tiles.at[lax.rem(mx - step + count_x, count_x), my]
        copy = remote(arrived, arrived, first_send.at[step], first_recv.at[step], at_x(step))
        copy.wait_send()
        copy.wait_recv()
    finish_side(side_x, mx, count_x, near.at[0, 1], near.at[2, 1])
    for step in range(1, count_y):
        remote(
            tiles.at[:, my], tiles.at[:, my], second_send.at[step], second_recv.at[step], at_y(step)
        ).start()
    side_y = (
        remote(near.at[:, 1], near.at[:, 2], side_send.at[2], side_recv.at[2], at_y(-1)),
        remote(near.at[:, 1], near.at[:, 0], side_send.at[3], side_recv.at[3], at_y(1)),
    )
    start_halo(side_y, my, count_y)


    def sweep(buffer, length, direction, store):
        def stencil_at(face):
            return lambda field: [buffer[field, face + i] for i in range(6)]

        def start_emit(field, flux):
            previous[field] = flux

        apply(prepare(stencil_at(0), direction), stencil_at(0), direction, nf, start_emit)

        def body(cell, prepared):
            following = prepare(stencil_at(jnp.minimum(cell + 2, length)), direction)

            def emit(field, flux):
                store(field, cell, flux - previous[field])
                previous[field] = flux

            apply(prepared, stencil_at(cell + 1), direction, nf, emit)
            return following

        lax.fori_loop(0, length, body, prepare(stencil_at(1), direction), unroll=2)

    finish_halo(pair_x, ext_x, cx, mx, count_x)

    def store_x(field, cell, value):
        section[field, cell] = section[field, cell] + value

    sweep(ext_x, cx, 0, store_x)

    finish_halo(pair_y, ext_y, cy, my, count_y)

    def store_y(field, cell, value):
        moved[field, cell] = value

    sweep(ext_y, cy, 1, store_y)

    for step in range(1, count_y):
        arrived = tiles.at[:, lax.rem(my - step + count_y, count_y)]
        copy = remote(arrived, arrived, second_send.at[step], second_recv.at[step], at_y(step))
        copy.wait_send()
        copy.wait_recv()
    finish_side(side_y, my, count_y, near.at[:, 0], near.at[:, 2])

    fastest = jnp.max(jnp.max(tiles[...], axis=(0, 1))[7:8, :])
    step_size = courant / (SUB * jnp.full((1, cz), fastest, jnp.float32))

    one_x, one_y = mx // 2, my // 2
    two_x, two_y = mx // 4, my // 4

    def united(ux, uy):
        return (
            tiles[2 * ux, 2 * uy] + tiles[2 * ux, 2 * uy + 1]
            + tiles[2 * ux + 1, 2 * uy] + tiles[2 * ux + 1, 2 * uy + 1]
        )

    def held(value, count):
        return jnp.clip(value, 0, count - 1), (value >= 0) & (value < count)

    for dx in range(3):
        for dy in range(3):
            base = (dx * 3 + dy) * 4 * slot
            window[0:8, base : base + 4 * slot] = near[dx, dy]
            for bx in range(2):
                for by in range(2):
                    at = base + (bx * 2 + by) * slot
                    gx, in_x = held(2 * (one_x + dx - 1) + bx, count_x)
                    gy, in_y = held(2 * (one_y + dy - 1) + by, count_y)
                    ux, in_ux = held(2 * (two_x + dx - 1) + bx, count_x // 2)
                    uy, in_uy = held(2 * (two_y + dy - 1) + by, count_y // 2)
                    own = jnp.where(in_x & in_y, tiles[gx, gy], 0.0)
                    joint = jnp.where(in_ux & in_uy, united(ux, uy), 0.0)
                    window[8:16, at : at + slot] = jnp.where(
                        row_index < 4, own, jnp.where(row_index < 6, joint, 0.0)
                    )

    for name in names:
        if name not in early_names:
            tables[name].wait()

    keep = (lax.broadcasted_iota(jnp.int32, (16, wide), 0) < 8).astype(jnp.float32)
    middle_chunks = 36 * slot // wide
    chunks = middle_chunks + len(inner_columns) * slot // wide
    for index in range(chunks):
        if index < middle_chunks:
            value = window[:, index * wide : (index + 1) * wide]
        else:
            pair = inner_columns[2 * (index - middle_chunks) :][:2]
            value = keep * jnp.concatenate(
                [window[:, column * slot : (column + 1) * slot] for column in pair], axis=1
            )
        high, low = halves(value)
        splits[index, 0:16] = high
        splits[index, 16:32] = low

    upper = jnp.zeros((32, wide), jnp.float32)
    lower = jnp.zeros((16, wide), jnp.float32)
    for index in range(chunks):
        both = splits[index]
        upper = upper + product(both, table["window_hi"][index])
        lower = lower + product(both[:16], table["window_lo"][index])
    sums = (upper[:16] + upper[16:] + lower) * table["scale"][...]


    def select(values, which):
        total = jnp.zeros((values.shape[0], 64), jnp.float32)
        for child in range(4):
            total = total + jnp.where(which == child, values[:, child * 64 : child * 64 + 64], 0.0)
        return total

    lane_64 = lax.broadcasted_iota(jnp.int32, (8, 64), 1)
    same_half = (lane_64 >= 32) == (lax.rem(lax.broadcasted_iota(jnp.int32, (8, 64), 0), 2) == 1)
    which_two = lax.rem(one_x, 2) * 2 + lax.rem(one_y, 2)
    second_sum = select(sums, which_two)
    if top:
        nx3, ny3 = count_x // 4, count_y // 4
        grown = jnp.zeros((8, slot), jnp.float32)
        for sx in range(nx3):
            for sy in range(ny3):
                source = jnp.zeros((8, slot), jnp.float32)
                for bx in range(2):
                    for by in range(2):
                        source = source + wholly(
                            united(2 * sx + bx, 2 * sy + by), table["raise_up"][bx * 2 + by]
                        )
                source = jnp.where((row_index == 4) | (row_index == 5), source, 0.0)
                place = ((sx - two_x + nx3 - 1) * (2 * ny3 - 1) + (sy - two_y + ny3 - 1)) * 3
                for dz in range(3):
                    moved_rows = source if dz == 1 else pltpu.roll(source, 1 if dz == 0 else 7, 0)
                    grown = grown + wholly(moved_rows, table["far"][place + dz])
        grown = jnp.where((row_index == 4) | (row_index == 5), grown, 0.0)
        carried = wholly(grown, table["lower_down"][which_two])
        second_sum = second_sum + jnp.concatenate([jnp.zeros((8, 64), jnp.float32), carried], axis=0)
    from_two = jnp.where(same_half, picked(table["take_two"][...], second_sum), 0.0)
    which_one = px * 2 + py
    first_sum = picked(table["take_one"][...], select(sums, which_one)) + times(
        from_two, *pair_of("down_two", which_one)
    )
    from_one = jnp.where(same_half, picked(table["take_zero"][...], first_sum), 0.0)
    expansion = sums[0:8] + times(from_one, *pair_of("down_one"))
    turned_hi, turned_lo = halves(expansion.T)
    to_z = table["to_z"][...].astype(jnp.bfloat16)
    on_z = product(turned_hi, to_z) + product(turned_lo, to_z)
    pieces = []
    for which, first_row, last_row in ((0, 0, 192), (1, 192, 288)):
        high, low = halves(on_z * table["weights"][which])
        field_hi = table["fields_hi"][first_row:last_row]
        piece = product(field_hi, high) + product(field_hi, low)
        if "fields_lo" in names:
            piece = piece + product(table["fields_lo"][first_row:last_row], high)
        pieces.append(piece)
    for k in range(3):
        parts = pieces[0][k * 96 : k * 96 + 96] if k < 2 else pieces[1]
        for row in range(cx):
            bx, height = row // SUB, (row % SUB + 0.5) / SUB - 0.5
            base = bx * 6 * SUB
            accel[k, row] = (
                parts[base : base + 2 * SUB]
                + height * parts[base + 2 * SUB : base + 4 * SUB]
                + (height * height) * parts[base + 4 * SUB : base + 6 * SUB]
            )

    def finish(cell, carry):
        own = [ext_x[field, 3 + cell] for field in range(4)]
        pull = [accel[k, cell] for k in range(3)]
        for field in range(nf):
            total = (section[field, cell] + moved[field, :, cell, :]) * (-float(SUB))
            if 1 <= field <= 3:
                total = total + own[0] * pull[field - 1]
            if field == 4:
                total = total + own[1] * pull[0] + own[2] * pull[1] + own[3] * pull[2]
            section[field, cell] = ext_x[field, 3 + cell] + step_size * total
        return carry

    leaving = [pltpu.make_async_copy(accel, accel_out, out_sem.at[4])]
    leaving[0].start()
    for quarter in range(4):
        begin = quarter * cx // 4
        lax.fori_loop(begin, begin + cx // 4, finish, 0)
        planes_out = pl.ds(begin, cx // 4)
        leaving.append(
            pltpu.make_async_copy(
                section.at[:, planes_out], section_out.at[:, planes_out], out_sem.at[quarter]
            )
        )
        leaving[-1].start()
    for copy in leaving:
        copy.wait()


def hand_over_kernel(section, accel, section_out, accel_out, staged, in_sem, out_sem):
    count = section.shape[0]
    pieces = [(section.at[i], section_out.at[i]) for i in range(count)]
    pieces += [(accel.at[i], accel_out.at[i]) for i in range(accel.shape[0])]
    arriving = [
        pltpu.make_async_copy(source, staged.at[i], in_sem.at[i])
        for i, (source, _) in enumerate(pieces)
    ]
    leaving = [
        pltpu.make_async_copy(staged.at[i], target, out_sem.at[i])
        for i, (_, target) in enumerate(pieces)
    ]
    for copy in arriving:
        copy.start()
    for before, after in zip(arriving, leaving):
        before.wait()
        after.start()
    for copy in leaving:
        copy.wait()


def shards(density, momentum, energy, entropy, tracers, leaf_flags):
    count_x, count_y = lax.axis_size("mx"), lax.axis_size("my")
    cx, cy, cz = density.shape
    nf = 6 + tracers.shape[0]
    middle, close = window_tables()
    top, raise_up, lower_down, far = top_tables(count_x // 4, count_y // 4)
    spread, along_z, cell_rows, pick_up, one_rows, second, two_rows, flag_z = moment_tables(cz)
    scale, down_two, down_one, take_one, take_two, take_zero, to_z, weights, fields = down_tables(cz)
    constants = {}
    for name, array in (("flag_z", flag_z), ("cell_rows", cell_rows), ("along_z", along_z)):
        constants[name] = jnp.asarray(array, jnp.float32)
    for name, array in (("spread", spread), ("pick_up", pick_up), ("second", second)):
        for ending, part in split_pair(array):
            constants[name + ending] = jnp.asarray(part)
    for name, array in (("one_rows", one_rows), ("two_rows", two_rows)):
        constants[name] = jnp.asarray(array, jnp.float32)
    joined = np.concatenate([middle, close]).reshape(-1, wide, wide)
    for name, array in (
        ("window", joined), ("down_two", down_two), ("down_one", down_one),
        ("fields", fields.reshape(-1, wide)),
    ):
        for ending, part in split_pair(array):
            constants[name + ending] = jnp.asarray(part)
    for name, array in (
        ("scale", scale), ("take_one", take_one), ("take_two", take_two),
        ("take_zero", take_zero), ("to_z", to_z), ("weights", weights),
    ):
        constants[name] = jnp.asarray(array, jnp.float32)
    if top:
        for name, array in (("raise_up", raise_up), ("lower_down", lower_down), ("far", far)):
            constants[name] = jnp.asarray(array, jnp.float32)
    names = tuple(constants)
    shapes = [
        pltpu.VMEM(
            array.shape[1:] if name.startswith("second") else array.shape, array.dtype
        )
        for name, array in constants.items()
    ]
    anywhere = pl.BlockSpec(memory_space=pl.ANY)
    local = pl.BlockSpec(memory_space=pltpu.VMEM)
    dma = pltpu.SemaphoreType.DMA
    f32 = jnp.float32
    out_shape = (
        jax.ShapeDtypeStruct((nf, cx, cy, cz), f32),
        jax.ShapeDtypeStruct((3, cx, cy, cz), f32),
    )
    results = pl.pallas_call(
        functools.partial(section_kernel, (count_x, count_y, nf, cx, cy, cz), top, names),
        out_shape=out_shape,
        in_specs=[anywhere] * 5 + [local] + [anywhere] * len(names),
        out_specs=(anywhere, anywhere),
        scratch_shapes=shapes
        + [
            pltpu.VMEM((nf, cx + 6, cy, cz), f32),
            pltpu.VMEM((nf, cy + 6, cx, cz), f32),
            pltpu.VMEM((nf, cy, cx, cz), f32),
            pltpu.VMEM((nf, cy, cz), f32),
            pltpu.VMEM((nf, cy, cz), f32),
            pltpu.VMEM((nf, cy, cz), f32),
            pltpu.VMEM((count_x, count_y, 8, slot), f32),
            pltpu.VMEM((3, 3, 8, 4 * slot), f32),
            pltpu.VMEM((16, 36 * slot), f32),
            pltpu.VMEM((128, cz), f32),
            pltpu.VMEM((joined.shape[0], 32, wide), jnp.bfloat16),
            pltpu.VMEM((nf, cx, cy, cz), f32),
            pltpu.VMEM((3, cx, cy, cz), f32),
            dma((5,)),
            dma((5,)), dma((len(names),)), dma((4,)), dma((4,)),
            dma((count_x,)), dma((count_x,)), dma((count_y,)), dma((count_y,)),
            dma((4,)), dma((4,)),
        ],
        compiler_params=pltpu.CompilerParams(
            collective_id=0, has_side_effects=True, vmem_limit_bytes=56 * 1024 * 1024
        ),
    )(density[None], momentum, energy[None], entropy[None], tracers, leaf_flags, *constants.values())
    return pl.pallas_call(
        hand_over_kernel,
        out_shape=out_shape,
        in_specs=[anywhere] * 2,
        out_specs=(anywhere, anywhere),
        scratch_shapes=[pltpu.VMEM((nf + 3, cx, cy, cz), f32), dma((nf + 3,)), dma((nf + 3,))],
    )(*results)


def solution(mesh):
    placed = (
        P("mx", "my", None),
        P(None, "mx", "my", None),
        P("mx", "my", None),
        P("mx", "my", None),
        P(None, "mx", "my", None),
        P("mx", "my", None),
    )
    return jax.shard_map(
        shards,
        mesh=mesh,
        in_specs=placed,
        out_specs=(P(None, "mx", "my", None), P(None, "mx", "my", None)),
        check_vma=False,
    )
```
